32 devices in a mesh: dp: 16 (over z, x, core), blk: 2 (over y).
Axes of the slice: x: 2, y: 2, z: 4, core: 2. Of those that a mesh axis runs over, the one named last changes fastest.
Arguments:
- waveform: bfloat16 [512, 330], P(('dp', 'blk')), may hold values from -6 to 6
- length_bin: int32 [512], P(('dp', 'blk')), may hold values from 1 to 4
- packing: int32 [32, 16], P(('dp', 'blk')), may hold values from 0 to 15, each once within a row
- cotangent: bfloat16 [512, 32, 512], P(('dp', 'blk')), may hold values from -6 to 6
- conv_one: bfloat16 [10, 512], replicated, may hold values from -2 to 2
- bias_one: float32 [512], replicated, may hold values from -6 to 6
- gain_one: float32 [512], replicated, may hold values from 2 to 8
- shift_one: float32 [512], replicated, may hold values from -12 to 12
- conv_two: bfloat16 [1536, 512], replicated, may hold values from -0.15625 to 0.15625
- bias_two: float32 [512], replicated, may hold values from -6 to 6
- gain_two: float32 [512], replicated, may hold values from 0.5 to 1.5
- shift_two: float32 [512], replicated, may hold values from -3 to 3
Outputs:
- grad_conv_two: float32 [1536, 512], P('dp')
- grad_small: float32 [16, 512], replicated
The draws below stay inside these ranges and needn't reach their ends.
All inputs are finite; a program needn't handle non-finite values.
Results may differ from the reference program's by a relative error of at most 0.0046.
Values may be sent and summed in bfloat16 or wider, within the bound.
No kernel may reach another device: no remote copies, remote signals or barrier semaphores. Data moves between devices by JAX's collectives and lax.ppermute only.
A program may use at most 64 MiB of HBM per device.

```python
import math
import jax
import jax.numpy as jnp
from jax import lax

D = 512
F2 = 32
PAIR = 1
NB = 4
GROUP = 8
U_DEV = 16
BLOCKS = 32
UTT = 512
RECW = 330
N_BLK = 2


def plant(values, rng, smallest, high):
    dims = values.shape
    spot = [jax.random.randint(jax.random.fold_in(rng, axis), (), 0, dims[axis]) for axis in range(len(dims))]
    values = values.at[tuple(spot)].set(smallest)
    longest = dims.index(max(dims))
    spot[longest] = (spot[longest] + 1) % dims[longest]
    return values.at[tuple(spot)].set(high)


def block_levels(stream_key, extent, shards, least, high):
    def one(position, blocks):
        heights = jax.random.uniform(jax.random.fold_in(jax.random.fold_in(stream_key, 6), position), (blocks,), jnp.float32, least / len(shards), high / len(shards))
        return jnp.repeat(jnp.exp(heights), extent[position] // blocks).reshape((-1,) + (1,) * (len(extent) - position - 1))

    level = one(*shards[0])
    for cut in shards[1:]:
        level = level * one(*cut)
    return level


def bell_draw(stream_key, dims, scale, reach, cuts=(), held_as=jnp.bfloat16):
    loudness = block_levels(stream_key, dims, cuts, -0.22, 0.18) if cuts else 1.0
    entries = jax.random.normal(stream_key, dims, jnp.float32) * scale * loudness
    return jnp.minimum(jnp.maximum(entries, -reach), reach).astype(held_as)


def setup_inputs(seed: int = 0) -> dict:
    arg_keys = jax.random.split(jax.random.key(seed), 13)
    waveform = bell_draw(arg_keys[0], (UTT, RECW), 1.0, 6.0, ((0, 32),))
    length_bin = plant(jax.random.randint(arg_keys[1], (UTT,), 1, NB + 1), jax.random.fold_in(arg_keys[1], 1), 1, NB).astype(jnp.int32)
    packing = jax.vmap(lambda own: jax.random.permutation(own, U_DEV))(jax.random.split(arg_keys[2], BLOCKS)).reshape((BLOCKS, U_DEV)).astype(jnp.int32)
    cotangent = bell_draw(arg_keys[3], (UTT, F2, D), 1.0, 6.0, ((0, 32),))
    conv_one = bell_draw(arg_keys[4], (10, D), 10 ** -0.5, 2.0)
    bias_one = bell_draw(arg_keys[5], (D,), 1.0, 6.0, (), jnp.float32)
    gain_one = jnp.clip(jnp.exp(jax.random.uniform(arg_keys[6], (D,), jnp.float32, math.log(2.0), math.log(8.0))), 2.0, 8.0)
    shift_one = bell_draw(arg_keys[7], (D,), 2.0, 12.0, (), jnp.float32)
    conv_two = bell_draw(arg_keys[8], (3 * D, D), (3 * D) ** -0.5, 0.15625)
    bias_two = bell_draw(arg_keys[9], (D,), 1.0, 6.0, (), jnp.float32)
    gain_two = jnp.clip(1.0 + 0.1 * jax.random.normal(arg_keys[10], (D,), jnp.float32), 0.5, 1.5)
    shift_two = bell_draw(arg_keys[11], (D,), 0.5, 3.0, (), jnp.float32)
    return dict(waveform=waveform, length_bin=length_bin, packing=packing, cotangent=cotangent, conv_one=conv_one, bias_one=bias_one, gain_one=gain_one, shift_one=shift_one, conv_two=conv_two, bias_two=bias_two, gain_two=gain_two, shift_two=shift_two)


def norm_act(z, gain, shift):
    mean = lax.optimization_barrier(jnp.mean(z, axis=-1, keepdims=True))
    cent = z - mean
    var = lax.optimization_barrier(jnp.mean(cent * cent, axis=-1, keepdims=True))
    rstd = lax.rsqrt(var + 1e-05)
    normed = cent * rstd
    return (normed * gain + shift, normed, rstd)

def gelu_exact(act):
    return 0.5 * act * (1.0 + lax.erf(act * 0.7071067811865476))

def norm_back(grad_out, act, normed, rstd, gain):
    cdf = 0.5 * (1.0 + lax.erf(act * 0.7071067811865476))
    pdf = jnp.exp(-0.5 * act * act) * 0.3989422804014327
    grad_act = grad_out * (cdf + act * pdf)
    grad_gain = lax.optimization_barrier(jnp.sum(grad_act * normed, axis=0))
    grad_shift = lax.optimization_barrier(jnp.sum(grad_act, axis=0))
    grad_norm = grad_act * gain
    inner = grad_norm - lax.optimization_barrier(jnp.mean(grad_norm, axis=-1, keepdims=True))
    inner = inner - normed * lax.optimization_barrier(jnp.mean(grad_norm * normed, axis=-1, keepdims=True))
    return (rstd * inner, grad_gain, grad_shift)

def pass_group(wave, bins, cot, conv_one, bias_one, gain_one, shift_one, conv_two, bias_two, gain_two, shift_two):
    count = wave.shape[0]
    frames_two = cot.shape[1]
    width = cot.shape[2]
    frames_one = 2 * frames_two + 1
    split = wave.reshape(count, frames_one + 1, 5)
    cols_one = jnp.concatenate([split[:, :-1], split[:, 1:]], axis=-1).reshape(count * frames_one, 10)
    z_one = jnp.dot(cols_one, conv_one, preferred_element_type=jnp.float32) + bias_one
    act_one, normed_one, rstd_one = norm_act(z_one, gain_one, shift_one)
    hidden = gelu_exact(act_one).astype(jnp.bfloat16).reshape(count, frames_one, width)
    cols_two = jnp.concatenate([hidden[:, :2 * frames_two].reshape(count, frames_two, 2 * width), hidden[:, 2::2]], axis=-1)
    cols_two = cols_two.reshape(count * frames_two, 3 * width)
    z_two = jnp.dot(cols_two, conv_two, preferred_element_type=jnp.float32) + bias_two
    act_two, normed_two, rstd_two = norm_act(z_two, gain_two, shift_two)
    limit = bins * frames_two // NB
    valid = (jnp.arange(frames_two, dtype=jnp.int32)[None, :] < limit[:, None]).astype(jnp.float32)
    grad_out = (cot.astype(jnp.float32) * valid[:, :, None]).reshape(count * frames_two, width)
    dz_two, dgain_two, dshift_two = norm_back(grad_out, act_two, normed_two, rstd_two, gain_two)
    dbias_two = lax.optimization_barrier(jnp.sum(dz_two, axis=0))
    dz_two_b = dz_two.astype(jnp.bfloat16)
    dcols = jnp.dot(dz_two_b, conv_two.T, preferred_element_type=jnp.float32).reshape(count, frames_two, 3 * width)
    part_a = dcols[:, :, :2 * width].reshape(count, 2 * frames_two, width)
    part_b = dcols[:, :, 2 * width:]
    spread = jnp.stack([part_b, jnp.zeros_like(part_b)], axis=2).reshape(count, 2 * frames_two, width)
    zero_one = jnp.zeros((count, 1, width), jnp.float32)
    zero_two = jnp.zeros((count, 2, width), jnp.float32)
    dhidden = jnp.concatenate([part_a, zero_one], axis=1) + jnp.concatenate([zero_two, spread[:, :2 * frames_two - 1]], axis=1)
    dz_one, dgain_one, dshift_one = norm_back(dhidden.reshape(count * frames_one, width), act_one, normed_one, rstd_one, gain_one)
    dbias_one = lax.optimization_barrier(jnp.sum(dz_one, axis=0))
    dconv_one = jnp.dot(cols_one.T, dz_one.astype(jnp.bfloat16), preferred_element_type=jnp.float32)
    small = jnp.concatenate([dconv_one, jnp.stack([dbias_one, dgain_one, dshift_one, dbias_two, dgain_two, dshift_two])], axis=0)
    return (cols_two, dz_two_b, small)

def reference(waveform, length_bin, packing, cotangent, conv_one, bias_one, gain_one, shift_one, conv_two, bias_two, gain_two, shift_two):
    block = jnp.arange(BLOCKS, dtype=jnp.int32)[:, None]
    slot = jnp.arange(U_DEV, dtype=jnp.int32)[None, :]
    dev_dp = block // N_BLK
    dev_blk = block % N_BLK
    source = slot // PAIR * N_BLK + dev_blk
    column = dev_dp * PAIR + slot % PAIR
    local = packing[source, column]
    index = (source * U_DEV + local).reshape(-1).astype(jnp.int32)
    wave = waveform[index]
    bins = length_bin[index]
    width = conv_two.shape[1]
    groups = UTT // GROUP
    xs = (wave.reshape(groups, GROUP, RECW), bins.reshape(groups, GROUP), cotangent.reshape(groups, GROUP, F2, width))

    def step(carry, item):
        grad_two, small_sum = carry
        cols_two, dz_two_b, small = pass_group(item[0], item[1], item[2], conv_one, bias_one, gain_one, shift_one, conv_two, bias_two, gain_two, shift_two)
        term = lax.dot_general(cols_two, dz_two_b, (((0,), (0,)), ((), ())), preferred_element_type=jnp.float32)
        return ((grad_two + term, small_sum + small), None)
    start = (jnp.zeros((3 * width, width), jnp.float32), jnp.zeros((16, width), jnp.float32))
    (grad_two, small_sum), _ = lax.scan(step, start, xs)
    return (grad_two, small_sum)
```

```python
import functools
import math

import jax
import jax.numpy as jnp
from jax import lax
from jax.experimental import pallas as pl
from jax.experimental.pallas import tpu as pltpu
from jax.sharding import PartitionSpec as P

NB = 4
TAPS = 10
STRIDE = 5
ROWS = 16
SPARE = 8
F32 = jnp.float32
BF16 = jnp.bfloat16


def split_two(x):
    hi = x.astype(BF16)
    return hi, (x - hi.astype(F32)).astype(BF16)


def gelu_parts(act):
    bell = jnp.exp(-0.5 * (act * act))
    t = 1.0 / (1.0 + 0.2316418882 * jnp.abs(act))
    poly = 0.5307027145 * t - 0.7265760135
    poly = poly * t + 0.7107068705
    poly = poly * t - 0.142248368
    poly = poly * t + 0.127414796
    tail = poly * t * bell
    cdf = jnp.where(act < 0.0, tail, 1.0 - tail)
    return cdf, 0.3989422804014327 * bell


def pack_kernel(packing, bins, wave_ref, out_ref, wide):
    count, record = wave_ref.shape
    width = wide.shape[1]
    wide[...] = jnp.zeros_like(wide)
    wide[:, :record] = wave_ref[...].astype(F32)
    lane = lax.broadcasted_iota(jnp.int32, (SPARE, width), 1)

    def one(slot):
        own = packing[0, slot]
        row = jnp.broadcast_to(wide[pl.ds(own, 1), :], (SPARE, width))
        return jnp.where(lane == record, bins[own].astype(F32), row)

    for pair in range(count // 2):
        both = jnp.concatenate([one(2 * pair), one(2 * pair + 1)], axis=0)
        out_ref[2 * SPARE * pair : 2 * SPARE * (pair + 1), :] = both.astype(BF16)


def pack(packing, length_bin, waveform):
    count, record = waveform.shape
    width = -(-(record + 1) // 128) * 128
    return pl.pallas_call(
        pack_kernel,
        out_shape=jax.ShapeDtypeStruct((count * SPARE, width), BF16),
        in_specs=[
            pl.BlockSpec(memory_space=pltpu.SMEM),
            pl.BlockSpec(memory_space=pltpu.SMEM),
            pl.BlockSpec(memory_space=pltpu.VMEM),
        ],
        out_specs=pl.BlockSpec(memory_space=pltpu.VMEM),
        scratch_shapes=[pltpu.VMEM((count, width), F32)],
    )(packing, length_bin, waveform)


def local_kernel(
    record,
    shares,
    place_ref,
    got_ref,
    cot_ref,
    conv_one_ref,
    bias_one_ref,
    gain_one_ref,
    shift_one_ref,
    conv_two_ref,
    bias_two_ref,
    gain_two_ref,
    shift_two_ref,
    send_ref,
    keep_ref,
    small_ref,
    taps,
    weight,
    norm_one,
    slope_one,
    rstd_one,
    hidden,
    norm_two,
    dz_two,
    dz_one,
    grad,
):
    count = got_ref.shape[0] // SPARE
    rows_two, width = cot_ref.shape
    frames_two = rows_two // count
    frames_one = 2 * frames_two + 1
    rows_even = rows_two + count
    rows_one = frames_one * count
    inv = 1.0 / width

    pick = (
        lax.broadcasted_iota(jnp.int32, (count, count * SPARE), 1)
        == SPARE * lax.broadcasted_iota(jnp.int32, (count, count * SPARE), 0)
    ).astype(BF16)
    wave = jnp.dot(pick, got_ref[...], preferred_element_type=F32)
    lane_in = lax.broadcasted_iota(jnp.int32, wave.shape, 1)
    bins = jnp.sum(jnp.where(lane_in == record, wave, 0.0), axis=1, keepdims=True)
    wave = jnp.concatenate([wave, jnp.zeros((count, 128), F32)], axis=1)

    for place, frame in enumerate(
        list(range(0, frames_one, 2)) + list(range(1, frames_one, 2))
    ):
        taps[count * place : count * (place + 1), :] = wave[
            :, STRIDE * frame : STRIDE * frame + 128
        ].astype(BF16)
    src = lax.broadcasted_iota(jnp.int32, (128, 128), 0)
    dst = lax.broadcasted_iota(jnp.int32, (128, 128), 1)
    thrice = ((src < TAPS) & (dst < 3 * ROWS) & (dst % ROWS == src)).astype(BF16)
    lane = lax.broadcasted_iota(jnp.int32, (1, 128), 1)
    ones = ((lane >= 3 * ROWS) & (lane < 3 * ROWS + 3)).astype(F32)
    taps[...] = (jnp.dot(taps[...], thrice, preferred_element_type=F32) + ones).astype(BF16)

    kernel_one = conv_one_ref[...].astype(F32)
    kernel_one = kernel_one - jnp.sum(kernel_one, axis=1, keepdims=True) * inv
    bias = bias_one_ref[...]
    bias = bias - jnp.sum(bias, axis=1, keepdims=True) * inv
    weight[...] = jnp.zeros_like(weight)
    for part in range(3):
        piece = kernel_one.astype(BF16).astype(F32)
        weight[part * ROWS : part * ROWS + TAPS, :] = piece
        kernel_one = kernel_one - piece
        piece = bias.astype(BF16).astype(F32)
        weight[3 * ROWS + part : 3 * ROWS + part + 1, :] = piece
        bias = bias - piece
    norm_one[...] = jnp.dot(taps[...], weight[...].astype(BF16), preferred_element_type=F32)

    gain = gain_one_ref[...]
    shift = shift_one_ref[...]

    def forward(step, _):
        at = pl.ds(pl.multiple_of(step * ROWS, ROWS), ROWS)
        cent = norm_one[at, :]
        var = jnp.sum(cent * cent, axis=1, keepdims=True) * inv
        rstd = lax.rsqrt(var + 1e-05)
        normed = cent * rstd
        act = normed * gain + shift
        cdf, pdf = gelu_parts(act)
        norm_one[at, :] = normed
        rstd_one[at, :] = jnp.broadcast_to(rstd, (ROWS, 128))
        slope_one[at, :] = cdf + act * pdf
        hidden[at, :] = (act * cdf).astype(BF16)
        return 0

    lax.fori_loop(0, rows_one // ROWS, forward, 0)

    windows = (
        slice(0, rows_two),
        slice(rows_even, rows_even + rows_two),
        slice(count, rows_even),
    )
    total = None
    for tap, rows in enumerate(windows):
        term = jnp.dot(
            hidden[rows, :],
            conv_two_ref[tap * width : (tap + 1) * width, :],
            preferred_element_type=F32,
        )
        total = term if total is None else total + term
    norm_two[...] = total

    row = lax.broadcasted_iota(jnp.int32, (rows_two, 1), 0)
    frame = row // count
    bins_all = jnp.concatenate([bins] * frames_two, axis=0)
    limit = bins_all.astype(jnp.int32) * frames_two // NB
    origin = jnp.where(frame < limit, (row % count) * frames_two + frame, -1)
    mover = (lax.broadcasted_iota(jnp.int32, (rows_two, rows_two), 1) == origin).astype(BF16)
    dz_one[:rows_two, :] = jnp.dot(mover, cot_ref[...], preferred_element_type=F32)

    bias_two = bias_two_ref[...]
    gain_b = gain_two_ref[...]
    shift_b = shift_two_ref[...]
    dz_two[:count, :] = jnp.zeros((count, width), BF16)
    dz_two[count + rows_two :, :] = jnp.zeros((count, width), BF16)

    def eighth(x):
        return x[:8] + x[8:]

    def middle(step, sums):
        start = pl.multiple_of(step * ROWS, ROWS)
        at = pl.ds(start, ROWS)
        z = norm_two[at, :] + bias_two
        cent = z - jnp.sum(z, axis=1, keepdims=True) * inv
        var = jnp.sum(cent * cent, axis=1, keepdims=True) * inv
        rstd = lax.rsqrt(var + 1e-05)
        normed = cent * rstd
        act = normed * gain_b + shift_b
        cdf, pdf = gelu_parts(act)
        dact = dz_one[at, :] * (cdf + act * pdf)
        dnorm = dact * gain_b
        mean_a = jnp.sum(dnorm, axis=1, keepdims=True) * inv
        mean_b = jnp.sum(dnorm * normed, axis=1, keepdims=True) * inv
        dz = rstd * (dnorm - mean_a - normed * mean_b)
        dz_two[pl.ds(pl.multiple_of(start + count, ROWS), ROWS), :] = dz.astype(BF16)
        return (
            sums[0] + eighth(dz),
            sums[1] + eighth(dact * normed),
            sums[2] + eighth(dact),
        )

    zero = jnp.zeros((8, width), F32)
    sums_two = lax.fori_loop(0, rows_two // ROWS, middle, (zero, zero, zero))

    dz_own = dz_two[count : count + rows_two, :]
    for tap, rows in enumerate(windows):
        grad[tap * width : (tap + 1) * width, :] = lax.dot_general(
            hidden[rows, :], dz_own, (((0,), (0,)), ((), ())), preferred_element_type=F32
        )
    share = grad.shape[0] // shares
    me = place_ref[0]
    bits = shares.bit_length() - 1
    for spot in range(shares):
        back = int(format(spot, f"0{bits}b")[::-1], 2)
        block = grad[pl.ds(pl.multiple_of((me ^ back) * share, 8), share), :]
        if spot < shares // 2:
            keep_ref[spot * share : (spot + 1) * share, :] = block
        else:
            at = (spot - shares // 2) * share
            send_ref[at : at + share, :] = block.astype(BF16)

    turn = (((1,), (1,)), ((), ()))
    dz_one[rows_even:, :] = lax.dot_general(
        dz_own, conv_two_ref[width : 2 * width, :], turn, preferred_element_type=F32
    )
    dz_one[:rows_even, :] = lax.dot_general(
        dz_two[count:, :], conv_two_ref[:width, :], turn, preferred_element_type=F32
    ) + lax.dot_general(
        dz_two[:rows_even, :], conv_two_ref[2 * width :, :], turn, preferred_element_type=F32
    )

    def backward(step, sums):
        at = pl.ds(pl.multiple_of(step * ROWS, ROWS), ROWS)
        normed = norm_one[at, :]
        dact = dz_one[at, :] * slope_one[at, :]
        dnorm = dact * gain
        mean_a = jnp.sum(dnorm, axis=1, keepdims=True) * inv
        mean_b = jnp.sum(dnorm * normed, axis=1, keepdims=True) * inv
        dz = rstd_one[at, :1] * (dnorm - mean_a - normed * mean_b)
        hidden[at, :] = dz.astype(BF16)
        return (
            sums[0] + eighth(dz),
            sums[1] + eighth(dact * normed),
            sums[2] + eighth(dact),
        )

    sums_one = lax.fori_loop(0, rows_one // ROWS, backward, (zero, zero, zero))
    first = lax.dot_general(
        taps[...], hidden[...], (((0,), (0,)), ((), ())), preferred_element_type=F32
    )
    small_ref[:TAPS, :] = first[:TAPS, :]
    for spot, sums in enumerate(sums_one + sums_two):
        small_ref[TAPS + spot : TAPS + spot + 1, :] = jnp.sum(sums, axis=0, keepdims=True)
    hi, lo = split_two(small_ref[...])
    half = send_ref.shape[0] - 2 * ROWS
    send_ref[half : half + ROWS, :] = hi
    send_ref[half + ROWS :, :] = lo


def local_pass(record, shares, place, got, cot, *params):
    count = got.shape[0] // SPARE
    rows_two, width = cot.shape
    rows_one = 2 * rows_two + count
    half = 3 * width // 2
    vmem = pl.BlockSpec(memory_space=pltpu.VMEM)
    return pl.pallas_call(
        functools.partial(local_kernel, record, shares),
        out_shape=(
            jax.ShapeDtypeStruct((half + 2 * ROWS, width), BF16),
            jax.ShapeDtypeStruct((half, width), F32),
            jax.ShapeDtypeStruct((ROWS, width), F32),
        ),
        in_specs=[pl.BlockSpec(memory_space=pltpu.SMEM)] + [vmem] * 10,
        out_specs=(vmem, vmem, vmem),
        scratch_shapes=[
            pltpu.VMEM((rows_one, 128), BF16),
            pltpu.VMEM((128, width), F32),
            pltpu.VMEM((rows_one, width), F32),
            pltpu.VMEM((rows_one, width), F32),
            pltpu.VMEM((rows_one, 128), F32),
            pltpu.VMEM((rows_one, width), BF16),
            pltpu.VMEM((rows_two, width), F32),
            pltpu.VMEM((rows_two + 2 * count, width), BF16),
            pltpu.VMEM((rows_one, width), F32),
            pltpu.VMEM((3 * width, width), F32),
        ],
        compiler_params=pltpu.CompilerParams(vmem_limit_bytes=40 * 1024 * 1024),
    )(place, got, cot, *params)


def tree(terms):
    while len(terms) > 1:
        terms = [terms[i] + terms[i + 1] for i in range(0, len(terms), 2)]
    return terms[0]


def exchange(sizes, stage, message):
    far = {axis: 0 for axis in sizes}
    for axis, bit in stage:
        far[axis] ^= 1 << bit
    axes = tuple(axis for axis in sizes if far[axis])
    pairs = [(0, 0)]
    for axis in axes:
        n = sizes[axis]
        pairs = [(a * n + i, b * n + (i ^ far[axis])) for a, b in pairs for i in range(n)]
    return lax.ppermute(message, axes if len(axes) > 1 else axes[0], pairs)


def merge(sizes, stage, blocks, small):
    dp_bits = [item for item in stage if item[0] == "dp"]
    blk_bits = [item for item in stage if item[0] != "dp"]
    hi, lo = split_two(small)
    tail = [hi, lo]
    messages = [jnp.concatenate([block.astype(BF16)] + tail, axis=0) for block in blocks]
    rows = blocks[0].shape[0]
    own = messages[0][:rows].astype(F32) if blk_bits else blocks[0]
    terms = [own]
    smalls = [hi.astype(F32) + lo.astype(F32)]
    for code in range(1, 1 << len(stage)):
        block = code >> len(blk_bits)
        chosen = [b for i, b in enumerate(dp_bits) if block >> (len(dp_bits) - 1 - i) & 1]
        chosen += [b for i, b in enumerate(blk_bits) if code >> i & 1]
        got = exchange(sizes, chosen, messages[block])
        terms.append(got[:rows].astype(F32))
        smalls.append(got[rows : rows + ROWS].astype(F32) + got[rows + ROWS :].astype(F32))
    return tree(terms), tree(smalls)


def per_device(sizes, waveform, length_bin, packing, cotangent, conv_one, *rest):
    record = waveform.shape[1]
    count, frames_two, width = cotangent.shape
    shares = sizes["dp"]
    share = 3 * width // shares
    packed = pack(packing, length_bin, waveform)
    packed = packed.reshape(count, SPARE, packed.shape[1])
    got = lax.all_to_all(packed, "dp", split_axis=0, concat_axis=0, tiled=True)
    got = got.reshape(count * SPARE, got.shape[2])
    params = [p if p.ndim == 2 else p.reshape(1, width) for p in (conv_one, *rest)]
    place = lax.axis_index("dp").astype(jnp.int32).reshape(1)
    send, keep, small = local_pass(
        record, shares, place, got, cotangent.reshape(count * frames_two, width), *params
    )
    half = keep.shape[0]
    other = exchange(sizes, [("dp", 0)], send)
    total = keep + other[:half].astype(F32)
    mine = send[half : half + ROWS].astype(F32) + send[half + ROWS :].astype(F32)
    yours = other[half : half + ROWS].astype(F32) + other[half + ROWS :].astype(F32)
    small = mine + yours
    left = [("dp", bit) for bit in range(1, shares.bit_length() - 1)]
    left += [("blk", bit) for bit in range(sizes["blk"].bit_length() - 1)]
    while left:
        stage, left = left[:2], left[2:]
        parts = 1 << sum(axis == "dp" for axis, _ in stage)
        rows = total.shape[0] // parts
        blocks = [total[i * rows : (i + 1) * rows] for i in range(parts)]
        total, small = merge(sizes, stage, blocks, small)
    return total, small


def solution(mesh):
    sizes = {axis: mesh.shape[axis] for axis in ("dp", "blk")}
    both = ("dp", "blk")
    return jax.shard_map(
        functools.partial(per_device, sizes),
        mesh=mesh,
        in_specs=(P(both, None), P(both), P(both, None), P(both, None, None)) + (P(),) * 8,
        out_specs=(P("dp", None), P()),
        check_vma=False,
    )
```

```python
import functools
import math

import jax
import jax.numpy as jnp
from jax import lax
from jax.experimental import pallas as pl
from jax.experimental.pallas import tpu as pltpu
from jax.sharding import PartitionSpec as P

NB = 4
TAPS = 10
STRIDE = 5
ROWS = 16
SPARE = 8
F32 = jnp.float32
BF16 = jnp.bfloat16


def split_two(x):
    hi = x.astype(BF16)
    return hi, (x - hi.astype(F32)).astype(BF16)


def gelu_parts(act):
    bell = jnp.exp(-0.5 * (act * act))
    t = 1.0 / (1.0 + 0.2316418882 * jnp.abs(act))
    poly = 0.5307027145 * t - 0.7265760135
    poly = poly * t + 0.7107068705
    poly = poly * t - 0.142248368
    poly = poly * t + 0.127414796
    tail = poly * t * bell
    cdf = jnp.where(act < 0.0, tail, 1.0 - tail)
    return cdf, 0.3989422804014327 * bell


def pack_kernel(packing, bins, wave_ref, out_ref, wide):
    count, record = wave_ref.shape
    width = wide.shape[1]
    wide[...] = jnp.zeros_like(wide)
    wide[:, :record] = wave_ref[...].astype(F32)
    lane = lax.broadcasted_iota(jnp.int32, (SPARE, width), 1)

    def one(slot):
        own = packing[0, slot]
        row = jnp.broadcast_to(wide[pl.ds(own, 1), :], (SPARE, width))
        return jnp.where(lane == record, bins[own].astype(F32), row)

    for pair in range(count // 2):
        both = jnp.concatenate([one(2 * pair), one(2 * pair + 1)], axis=0)
        out_ref[2 * SPARE * pair : 2 * SPARE * (pair + 1), :] = both.astype(BF16)


def pack(packing, length_bin, waveform):
    count, record = waveform.shape
    width = -(-(record + 1) // 128) * 128
    return pl.pallas_call(
        pack_kernel,
        out_shape=jax.ShapeDtypeStruct((count * SPARE, width), BF16),
        in_specs=[
            pl.BlockSpec(memory_space=pltpu.SMEM),
            pl.BlockSpec(memory_space=pltpu.SMEM),
            pl.BlockSpec(memory_space=pltpu.VMEM),
        ],
        out_specs=pl.BlockSpec(memory_space=pltpu.VMEM),
        scratch_shapes=[pltpu.VMEM((count, width), F32)],
    )(packing, length_bin, waveform)


def ready_kernel(
    count,
    cot_hbm,
    conv_two_hbm,
    conv_one_ref,
    bias_one_ref,
    gain_one_ref,
    shift_one_ref,
    bias_two_ref,
    gain_two_ref,
    shift_two_ref,
    weight_ref,
    cot_ref,
    conv_two_ref,
    vector_ref,
    weight,
    held,
    kernel_one,
    vectors,
    arrived,
):
    rows_two, width = held.shape
    frames_two = rows_two // count
    inv = 1.0 / width
    moves = [
        pltpu.make_async_copy(conv_one_ref, kernel_one, arrived.at[0]),
        pltpu.make_async_copy(bias_one_ref, vectors.at[0:1], arrived.at[1]),
        pltpu.make_async_copy(gain_one_ref, vectors.at[1:2], arrived.at[2]),
        pltpu.make_async_copy(shift_one_ref, vectors.at[2:3], arrived.at[3]),
        pltpu.make_async_copy(bias_two_ref, vectors.at[3:4], arrived.at[4]),
        pltpu.make_async_copy(gain_two_ref, vectors.at[4:5], arrived.at[5]),
        pltpu.make_async_copy(shift_two_ref, vectors.at[5:6], arrived.at[6]),
        pltpu.make_async_copy(cot_hbm, held, arrived.at[7]),
        pltpu.make_async_copy(conv_two_hbm, conv_two_ref, arrived.at[8]),
    ]
    for move in moves:
        move.start()
    row = lax.broadcasted_iota(jnp.int32, (rows_two, 1), 0)
    origin = (row % count) * frames_two + row // count
    mover = (lax.broadcasted_iota(jnp.int32, (rows_two, rows_two), 1) == origin).astype(BF16)
    weight[...] = jnp.zeros_like(weight)
    for move in moves[:7]:
        move.wait()
    kernel = kernel_one[...].astype(F32)
    kernel = kernel - jnp.sum(kernel, axis=1, keepdims=True) * inv
    bias = vectors[0:1, :]
    bias = bias - jnp.sum(bias, axis=1, keepdims=True) * inv
    for part in range(3):
        piece = kernel.astype(BF16).astype(F32)
        weight[part * ROWS : part * ROWS + TAPS, :] = piece
        kernel = kernel - piece
        piece = bias.astype(BF16).astype(F32)
        weight[3 * ROWS + part : 3 * ROWS + part + 1, :] = piece
        bias = bias - piece
    weight_ref[...] = weight[...].astype(BF16)
    vector_ref[0:6, :] = vectors[0:6, :]
    moves[7].wait()
    cot_ref[...] = jnp.dot(mover, held[...], preferred_element_type=F32).astype(BF16)
    moves[8].wait()


def ready(count, cot, conv_two, conv_one, *vectors):
    rows_two, width = cot.shape
    vmem = pl.BlockSpec(memory_space=pltpu.VMEM)
    return pl.pallas_call(
        functools.partial(ready_kernel, count),
        out_shape=(
            jax.ShapeDtypeStruct((128, width), BF16),
            jax.ShapeDtypeStruct(cot.shape, BF16),
            jax.ShapeDtypeStruct(conv_two.shape, BF16),
            jax.ShapeDtypeStruct((8, width), F32),
        ),
        in_specs=[pl.BlockSpec(memory_space=pltpu.HBM)] * 9,
        out_specs=(vmem, vmem, vmem, vmem),
        scratch_shapes=[
            pltpu.VMEM((128, width), F32),
            pltpu.VMEM(cot.shape, BF16),
            pltpu.VMEM(conv_one.shape, BF16),
            pltpu.VMEM((8, width), F32),
            pltpu.SemaphoreType.DMA((9,)),
        ],
        cost_estimate=pl.CostEstimate(
            flops=2 * rows_two * rows_two * width,
            bytes_accessed=4 * conv_two.size + 4 * cot.size,
            transcendentals=0,
        ),
        compiler_params=pltpu.CompilerParams(vmem_limit_bytes=16 * 1024 * 1024),
    )(cot, conv_two, conv_one, *vectors)


def together(steps):
    return max(n for n in range(1, 17) if steps % n == 0)


def local_kernel(
    record,
    shares,
    place_ref,
    got_ref,
    cot_ref,
    weight_ref,
    conv_two_ref,
    vector_ref,
    send_ref,
    keep_ref,
    small_ref,
    taps,
    limits,
    cent_one,
    norm_one,
    slope_one,
    rstd_one,
    hidden,
    norm_two,
    dz_two,
    dz_one,
    grad,
):
    count = got_ref.shape[0] // SPARE
    rows_two, width = cot_ref.shape
    frames_two = rows_two // count
    frames_one = 2 * frames_two + 1
    rows_even = rows_two + count
    rows_one = frames_one * count
    inv = 1.0 / width

    pick = (
        lax.broadcasted_iota(jnp.int32, (count, count * SPARE), 1)
        == SPARE * lax.broadcasted_iota(jnp.int32, (count, count * SPARE), 0)
    ).astype(BF16)
    wave = jnp.dot(pick, got_ref[...], preferred_element_type=F32)
    lane_in = lax.broadcasted_iota(jnp.int32, wave.shape, 1)
    bins = jnp.sum(jnp.where(lane_in == record, wave, 0.0), axis=1, keepdims=True)
    limit = bins.astype(jnp.int32) * frames_two // NB
    limits[...] = jnp.broadcast_to(limit, (count, 128))
    wave = jnp.concatenate([wave, jnp.zeros((count, 128), F32)], axis=1)

    for place, frame in enumerate(
        list(range(0, frames_one, 2)) + list(range(1, frames_one, 2))
    ):
        taps[count * place : count * (place + 1), :] = wave[
            :, STRIDE * frame : STRIDE * frame + 128
        ].astype(BF16)
    src = lax.broadcasted_iota(jnp.int32, (128, 128), 0)
    dst = lax.broadcasted_iota(jnp.int32, (128, 128), 1)
    thrice = ((src < TAPS) & (dst < 3 * ROWS) & (dst % ROWS == src)).astype(BF16)
    lane = lax.broadcasted_iota(jnp.int32, (1, 128), 1)
    ones = ((lane >= 3 * ROWS) & (lane < 3 * ROWS + 3)).astype(F32)
    taps[...] = (jnp.dot(taps[...], thrice, preferred_element_type=F32) + ones).astype(BF16)

    cent_one[...] = jnp.dot(taps[...], weight_ref[...], preferred_element_type=F32)
    gain = vector_ref[1:2, :]
    shift = vector_ref[2:3, :]
    steps_one = rows_one // ROWS
    steps_two = rows_two // ROWS

    def forward(step, _):
        at = pl.ds(pl.multiple_of(step * ROWS, ROWS), ROWS)
        cent = cent_one[at, :]
        var = jnp.sum(cent * cent, axis=1, keepdims=True) * inv
        rstd = lax.rsqrt(var + 1e-05)
        normed = cent * rstd
        act = normed * gain + shift
        cdf, pdf = gelu_parts(act)
        norm_one[at, :] = normed
        rstd_one[at, :] = jnp.broadcast_to(rstd, (ROWS, 128))
        slope_one[at, :] = cdf + act * pdf
        hidden[at, :] = (act * cdf).astype(BF16)
        return 0

    lax.fori_loop(0, steps_one, forward, 0, unroll=together(steps_one))

    windows = (
        slice(0, rows_two),
        slice(rows_even, rows_even + rows_two),
        slice(count, rows_even),
    )
    total = None
    for tap, rows in enumerate(windows):
        term = jnp.dot(
            hidden[rows, :],
            conv_two_ref[tap * width : (tap + 1) * width, :],
            preferred_element_type=F32,
        )
        total = term if total is None else total + term
    norm_two[...] = total

    bias_two = vector_ref[3:4, :]
    gain_b = vector_ref[4:5, :]
    shift_b = vector_ref[5:6, :]
    dz_two[:count, :] = jnp.zeros((count, width), BF16)
    dz_two[count + rows_two :, :] = jnp.zeros((count, width), BF16)

    def eighth(x):
        return x[:8] + x[8:]

    def middle(step, sums):
        start = pl.multiple_of(step * ROWS, ROWS)
        at = pl.ds(start, ROWS)
        first = pl.multiple_of(lax.rem(start, count), ROWS)
        valid = limits[pl.ds(first, ROWS), :1] > lax.div(start, count)
        z = norm_two[at, :] + bias_two
        cent = z - jnp.sum(z, axis=1, keepdims=True) * inv
        var = jnp.sum(cent * cent, axis=1, keepdims=True) * inv
        rstd = lax.rsqrt(var + 1e-05)
        normed = cent * rstd
        act = normed * gain_b + shift_b
        cdf, pdf = gelu_parts(act)
        dact = jnp.where(valid, cot_ref[at, :].astype(F32) * (cdf + act * pdf), 0.0)
        dnorm = dact * gain_b
        mean_a = jnp.sum(dnorm, axis=1, keepdims=True) * inv
        mean_b = jnp.sum(dnorm * normed, axis=1, keepdims=True) * inv
        dz = rstd * (dnorm - mean_a - normed * mean_b)
        dz_two[pl.ds(pl.multiple_of(start + count, ROWS), ROWS), :] = dz.astype(BF16)
        return (
            sums[0] + eighth(dz),
            sums[1] + eighth(dact * normed),
            sums[2] + eighth(dact),
        )

    zero = jnp.zeros((8, width), F32)
    sums_two = lax.fori_loop(
        0, steps_two, middle, (zero, zero, zero), unroll=together(steps_two)
    )

    dz_own = dz_two[count : count + rows_two, :]
    for tap, rows in enumerate(windows):
        grad[tap * width : (tap + 1) * width, :] = lax.dot_general(
            hidden[rows, :], dz_own, (((0,), (0,)), ((), ())), preferred_element_type=F32
        )
    share = grad.shape[0] // shares
    me = place_ref[0]
    bits = shares.bit_length() - 1
    for spot in range(shares):
        back = int(format(spot, f"0{bits}b")[::-1], 2)
        block = grad[pl.ds(pl.multiple_of((me ^ back) * share, 8), share), :]
        if spot < shares // 2:
            keep_ref[spot * share : (spot + 1) * share, :] = block
        else:
            at = (spot - shares // 2) * share
            send_ref[at : at + share, :] = block.astype(BF16)

    turn = (((1,), (1,)), ((), ()))
    dz_one[rows_even:, :] = lax.dot_general(
        dz_own, conv_two_ref[width : 2 * width, :], turn, preferred_element_type=F32
    )
    dz_one[:rows_even, :] = lax.dot_general(
        dz_two[count:, :], conv_two_ref[:width, :], turn, preferred_element_type=F32
    ) + lax.dot_general(
        dz_two[:rows_even, :], conv_two_ref[2 * width :, :], turn, preferred_element_type=F32
    )

    def backward(step, sums):
        at = pl.ds(pl.multiple_of(step * ROWS, ROWS), ROWS)
        normed = norm_one[at, :]
        dact = dz_one[at, :] * slope_one[at, :]
        dnorm = dact * gain
        mean_a = jnp.sum(dnorm, axis=1, keepdims=True) * inv
        mean_b = jnp.sum(dnorm * normed, axis=1, keepdims=True) * inv
        dz = rstd_one[at, :1] * (dnorm - mean_a - normed * mean_b)
        hidden[at, :] = dz.astype(BF16)
        return (
            sums[0] + eighth(dz),
            sums[1] + eighth(dact * normed),
            sums[2] + eighth(dact),
        )

    sums_one = lax.fori_loop(
        0, steps_one, backward, (zero, zero, zero), unroll=together(steps_one)
    )
    first = lax.dot_general(
        taps[...], hidden[...], (((0,), (0,)), ((), ())), preferred_element_type=F32
    )
    small_ref[:TAPS, :] = first[:TAPS, :]
    for spot, sums in enumerate(sums_one + sums_two):
        small_ref[TAPS + spot : TAPS + spot + 1, :] = jnp.sum(sums, axis=0, keepdims=True)
    hi, lo = split_two(small_ref[...])
    half = send_ref.shape[0] - 2 * ROWS
    send_ref[half : half + ROWS, :] = hi
    send_ref[half + ROWS :, :] = lo


def local_pass(record, shares, place, got, cot, weight, conv_two, vectors):
    count = got.shape[0] // SPARE
    rows_two, width = cot.shape
    rows_one = 2 * rows_two + count
    half = 3 * width // 2
    vmem = pl.BlockSpec(memory_space=pltpu.VMEM)
    return pl.pallas_call(
        functools.partial(local_kernel, record, shares),
        out_shape=(
            jax.ShapeDtypeStruct((half + 2 * ROWS, width), BF16),
            jax.ShapeDtypeStruct((half, width), F32),
            jax.ShapeDtypeStruct((ROWS, width), F32),
        ),
        in_specs=[pl.BlockSpec(memory_space=pltpu.SMEM)] + [vmem] * 5,
        out_specs=(vmem, vmem, vmem),
        scratch_shapes=[
            pltpu.VMEM((rows_one, 128), BF16),
            pltpu.VMEM((count, 128), jnp.int32),
            pltpu.VMEM((rows_one, width), F32),
            pltpu.VMEM((rows_one, width), F32),
            pltpu.VMEM((rows_one, width), F32),
            pltpu.VMEM((rows_one, 128), F32),
            pltpu.VMEM((rows_one, width), BF16),
            pltpu.VMEM((rows_two, width), F32),
            pltpu.VMEM((rows_two + 2 * count, width), BF16),
            pltpu.VMEM((rows_one, width), F32),
            pltpu.VMEM((3 * width, width), F32),
        ],
        cost_estimate=pl.CostEstimate(
            flops=2 * 9 * rows_two * width * width,
            bytes_accessed=8 * rows_one * width,
            transcendentals=3 * rows_one * width,
        ),
        compiler_params=pltpu.CompilerParams(vmem_limit_bytes=36 * 1024 * 1024),
    )(place, got, cot, weight, conv_two, vectors)


def tree(terms):
    while len(terms) > 1:
        terms = [terms[i] + terms[i + 1] for i in range(0, len(terms), 2)]
    return terms[0]


def exchange(sizes, stage, message):
    far = {axis: 0 for axis in sizes}
    for axis, bit in stage:
        far[axis] ^= 1 << bit
    axes = tuple(axis for axis in sizes if far[axis])
    pairs = [(0, 0)]
    for axis in axes:
        n = sizes[axis]
        pairs = [(a * n + i, b * n + (i ^ far[axis])) for a, b in pairs for i in range(n)]
    return lax.ppermute(message, axes if len(axes) > 1 else axes[0], pairs)


def merge(sizes, stage, blocks, small):
    dp_bits = [item for item in stage if item[0] == "dp"]
    blk_bits = [item for item in stage if item[0] != "dp"]
    hi, lo = split_two(small)
    tail = [hi, lo]
    messages = [jnp.concatenate([block.astype(BF16)] + tail, axis=0) for block in blocks]
    rows = blocks[0].shape[0]
    own = messages[0][:rows].astype(F32) if blk_bits else blocks[0]
    terms = [own]
    smalls = [hi.astype(F32) + lo.astype(F32)]
    for code in range(1, 1 << len(stage)):
        block = code >> len(blk_bits)
        chosen = [b for i, b in enumerate(dp_bits) if block >> (len(dp_bits) - 1 - i) & 1]
        chosen += [b for i, b in enumerate(blk_bits) if code >> i & 1]
        got = exchange(sizes, chosen, messages[block])
        terms.append(got[:rows].astype(F32))
        smalls.append(got[rows : rows + ROWS].astype(F32) + got[rows + ROWS :].astype(F32))
    return tree(terms), tree(smalls)


def per_device(
    sizes,
    waveform,
    length_bin,
    packing,
    cotangent,
    conv_one,
    bias_one,
    gain_one,
    shift_one,
    conv_two,
    bias_two,
    gain_two,
    shift_two,
):
    record = waveform.shape[1]
    count, frames_two, width = cotangent.shape
    shares = sizes["dp"]
    packed = pack(packing, length_bin, waveform)
    packed = packed.reshape(count, SPARE, packed.shape[1])
    got = lax.all_to_all(packed, "dp", split_axis=0, concat_axis=0, tiled=True)
    got = got.reshape(count * SPARE, got.shape[2])
    vectors = (bias_one, gain_one, shift_one, bias_two, gain_two, shift_two)
    weight, cot, conv_two, vectors = ready(
        count,
        cotangent.reshape(count * frames_two, width),
        conv_two,
        conv_one,
        *(v.reshape(1, width) for v in vectors),
    )
    place = lax.axis_index("dp").astype(jnp.int32).reshape(1)
    send, keep, small = local_pass(record, shares, place, got, cot, weight, conv_two, vectors)
    half = keep.shape[0]
    other = exchange(sizes, [("dp", 0)], send)
    total = keep + other[:half].astype(F32)
    mine = send[half : half + ROWS].astype(F32) + send[half + ROWS :].astype(F32)
    yours = other[half : half + ROWS].astype(F32) + other[half + ROWS :].astype(F32)
    small = mine + yours
    left = [("dp", bit) for bit in range(1, shares.bit_length() - 1)]
    left += [("blk", bit) for bit in range(sizes["blk"].bit_length() - 1)]
    while left:
        stage, left = left[:2], left[2:]
        parts = 1 << sum(axis == "dp" for axis, _ in stage)
        rows = total.shape[0] // parts
        blocks = [total[i * rows : (i + 1) * rows] for i in range(parts)]
        total, small = merge(sizes, stage, blocks, small)
    return total, small


def solution(mesh):
    sizes = {axis: mesh.shape[axis] for axis in ("dp", "blk")}
    both = ("dp", "blk")
    return jax.shard_map(
        functools.partial(per_device, sizes),
        mesh=mesh,
        in_specs=(P(both, None), P(both), P(both, None), P(both, None, None)) + (P(),) * 8,
        out_specs=(P("dp", None), P()),
        check_vma=False,
    )
```

```python
import functools
import math

import jax
import jax.numpy as jnp
from jax import lax
from jax.experimental import pallas as pl
from jax.experimental.pallas import tpu as pltpu
from jax.sharding import PartitionSpec as P

NB = 4
TAPS = 10
STRIDE = 5
ROWS = 16
SPARE = 8
F32 = jnp.float32
BF16 = jnp.bfloat16


def split_two(x):
    hi = x.astype(BF16)
    return hi, (x - hi.astype(F32)).astype(BF16)


def gelu_parts(act):
    bell = jnp.exp(-0.5 * (act * act))
    t = 1.0 / (1.0 + 0.2316418882 * jnp.abs(act))
    poly = 0.5307027145 * t - 0.7265760135
    poly = poly * t + 0.7107068705
    poly = poly * t - 0.142248368
    poly = poly * t + 0.127414796
    tail = poly * t * bell
    cdf = jnp.where(act < 0.0, tail, 1.0 - tail)
    return cdf, 0.3989422804014327 * bell


def pack_kernel(packing, bins, wave_ref, out_ref, wide):
    count, record = wave_ref.shape
    width = wide.shape[1]
    wide[...] = jnp.zeros_like(wide)
    wide[:, :record] = wave_ref[...].astype(F32)
    lane = lax.broadcasted_iota(jnp.int32, (SPARE, width), 1)

    def one(slot):
        own = packing[0, slot]
        row = jnp.broadcast_to(wide[pl.ds(own, 1), :], (SPARE, width))
        return jnp.where(lane == record, bins[own].astype(F32), row)

    for pair in range(count // 2):
        both = jnp.concatenate([one(2 * pair), one(2 * pair + 1)], axis=0)
        out_ref[2 * SPARE * pair : 2 * SPARE * (pair + 1), :] = both.astype(BF16)


def pack(packing, length_bin, waveform):
    count, record = waveform.shape
    width = -(-(record + 1) // 128) * 128
    return pl.pallas_call(
        pack_kernel,
        out_shape=jax.ShapeDtypeStruct((count * SPARE, width), BF16),
        in_specs=[
            pl.BlockSpec(memory_space=pltpu.SMEM),
            pl.BlockSpec(memory_space=pltpu.SMEM),
            pl.BlockSpec(memory_space=pltpu.VMEM),
        ],
        out_specs=pl.BlockSpec(memory_space=pltpu.VMEM),
        scratch_shapes=[pltpu.VMEM((count, width), F32)],
    )(packing, length_bin, waveform)


def ready_kernel(count, cot_ref, table_ref, conv_two_ref, moved_ref, weight_ref, weight):
    rows_two, width = cot_ref.shape
    frames_two = rows_two // count
    inv = 1.0 / width
    row = lax.broadcasted_iota(jnp.int32, (rows_two, 1), 0)
    origin = (row % count) * frames_two + row // count
    mover = (lax.broadcasted_iota(jnp.int32, (rows_two, rows_two), 1) == origin).astype(BF16)
    moved_ref[...] = jnp.dot(mover, cot_ref[...], preferred_element_type=F32).astype(BF16)
    weight[...] = jnp.zeros_like(weight)
    kernel = table_ref[:TAPS, :]
    kernel = kernel - jnp.sum(kernel, axis=1, keepdims=True) * inv
    bias = table_ref[TAPS : TAPS + 1, :]
    bias = bias - jnp.sum(bias, axis=1, keepdims=True) * inv
    for part in range(3):
        piece = kernel.astype(BF16).astype(F32)
        weight[part * ROWS : part * ROWS + TAPS, :] = piece
        kernel = kernel - piece
        piece = bias.astype(BF16).astype(F32)
        weight[3 * ROWS + part : 3 * ROWS + part + 1, :] = piece
        bias = bias - piece
    weight_ref[...] = weight[...].astype(BF16)


def ready(count, cot, table, conv_two):
    rows_two, width = cot.shape
    vmem = pl.BlockSpec(memory_space=pltpu.VMEM)
    return pl.pallas_call(
        functools.partial(ready_kernel, count),
        out_shape=(
            jax.ShapeDtypeStruct(cot.shape, BF16),
            jax.ShapeDtypeStruct((128, width), BF16),
        ),
        in_specs=[vmem, vmem, vmem],
        out_specs=(vmem, vmem),
        scratch_shapes=[pltpu.VMEM((128, width), F32)],
        cost_estimate=pl.CostEstimate(
            flops=2 * rows_two * rows_two * width,
            bytes_accessed=4 * cot.size,
            transcendentals=0,
        ),
        compiler_params=pltpu.CompilerParams(vmem_limit_bytes=16 * 1024 * 1024),
    )(cot, table, conv_two)


def together(steps):
    return max(n for n in range(1, 17) if steps % n == 0)


def local_kernel(
    record,
    shares,
    place_ref,
    got_ref,
    cot_ref,
    weight_ref,
    conv_two_ref,
    table_ref,
    send_ref,
    keep_ref,
    small_ref,
    taps,
    limits,
    cent_one,
    norm_one,
    slope_one,
    rstd_one,
    hidden,
    norm_two,
    dz_two,
    dz_one,
    grad,
):
    count = got_ref.shape[0] // SPARE
    rows_two, width = cot_ref.shape
    frames_two = rows_two // count
    frames_one = 2 * frames_two + 1
    rows_even = rows_two + count
    rows_one = frames_one * count
    inv = 1.0 / width

    pick = (
        lax.broadcasted_iota(jnp.int32, (count, count * SPARE), 1)
        == SPARE * lax.broadcasted_iota(jnp.int32, (count, count * SPARE), 0)
    ).astype(BF16)
    wave = jnp.dot(pick, got_ref[...], preferred_element_type=F32)
    lane_in = lax.broadcasted_iota(jnp.int32, wave.shape, 1)
    bins = jnp.sum(jnp.where(lane_in == record, wave, 0.0), axis=1, keepdims=True)
    limit = bins.astype(jnp.int32) * frames_two // NB
    limits[...] = jnp.broadcast_to(limit, (count, 128))
    wave = jnp.concatenate([wave, jnp.zeros((count, 128), F32)], axis=1)

    for place, frame in enumerate(
        list(range(0, frames_one, 2)) + list(range(1, frames_one, 2))
    ):
        taps[count * place : count * (place + 1), :] = wave[
            :, STRIDE * frame : STRIDE * frame + 128
        ].astype(BF16)
    src = lax.broadcasted_iota(jnp.int32, (128, 128), 0)
    dst = lax.broadcasted_iota(jnp.int32, (128, 128), 1)
    thrice = ((src < TAPS) & (dst < 3 * ROWS) & (dst % ROWS == src)).astype(BF16)
    lane = lax.broadcasted_iota(jnp.int32, (1, 128), 1)
    ones = ((lane >= 3 * ROWS) & (lane < 3 * ROWS + 3)).astype(F32)
    taps[...] = (jnp.dot(taps[...], thrice, preferred_element_type=F32) + ones).astype(BF16)

    cent_one[...] = jnp.dot(taps[...], weight_ref[...], preferred_element_type=F32)
    gain = table_ref[TAPS + 1 : TAPS + 2, :]
    shift = table_ref[TAPS + 2 : TAPS + 3, :]
    steps_one = rows_one // ROWS
    steps_two = rows_two // ROWS

    def forward(step, _):
        at = pl.ds(pl.multiple_of(step * ROWS, ROWS), ROWS)
        cent = cent_one[at, :]
        var = jnp.sum(cent * cent, axis=1, keepdims=True) * inv
        rstd = lax.rsqrt(var + 1e-05)
        normed = cent * rstd
        act = normed * gain + shift
        cdf, pdf = gelu_parts(act)
        norm_one[at, :] = normed
        rstd_one[at, :] = jnp.broadcast_to(rstd, (ROWS, 128))
        slope_one[at, :] = cdf + act * pdf
        hidden[at, :] = (act * cdf).astype(BF16)
        return 0

    lax.fori_loop(0, steps_one, forward, 0, unroll=together(steps_one))

    windows = (
        slice(0, rows_two),
        slice(rows_even, rows_even + rows_two),
        slice(count, rows_even),
    )
    total = None
    for tap, rows in enumerate(windows):
        term = jnp.dot(
            hidden[rows, :],
            conv_two_ref[tap * width : (tap + 1) * width, :],
            preferred_element_type=F32,
        )
        total = term if total is None else total + term
    norm_two[...] = total

    bias_two = table_ref[TAPS + 3 : TAPS + 4, :]
    gain_b = table_ref[TAPS + 4 : TAPS + 5, :]
    shift_b = table_ref[TAPS + 5 : TAPS + 6, :]
    dz_two[:count, :] = jnp.zeros((count, width), BF16)
    dz_two[count + rows_two :, :] = jnp.zeros((count, width), BF16)

    def eighth(x):
        return x[:8] + x[8:]

    def middle(step, sums):
        start = pl.multiple_of(step * ROWS, ROWS)
        at = pl.ds(start, ROWS)
        first = pl.multiple_of(lax.rem(start, count), ROWS)
        valid = limits[pl.ds(first, ROWS), :1] > lax.div(start, count)
        z = norm_two[at, :] + bias_two
        cent = z - jnp.sum(z, axis=1, keepdims=True) * inv
        var = jnp.sum(cent * cent, axis=1, keepdims=True) * inv
        rstd = lax.rsqrt(var + 1e-05)
        normed = cent * rstd
        act = normed * gain_b + shift_b
        cdf, pdf = gelu_parts(act)
        dact = jnp.where(valid, cot_ref[at, :].astype(F32) * (cdf + act * pdf), 0.0)
        dnorm = dact * gain_b
        mean_a = jnp.sum(dnorm, axis=1, keepdims=True) * inv
        mean_b = jnp.sum(dnorm * normed, axis=1, keepdims=True) * inv
        dz = rstd * (dnorm - mean_a - normed * mean_b)
        dz_two[pl.ds(pl.multiple_of(start + count, ROWS), ROWS), :] = dz.astype(BF16)
        return (
            sums[0] + eighth(dz),
            sums[1] + eighth(dact * normed),
            sums[2] + eighth(dact),
        )

    zero = jnp.zeros((8, width), F32)
    sums_two = lax.fori_loop(
        0, steps_two, middle, (zero, zero, zero), unroll=together(steps_two)
    )

    dz_own = dz_two[count : count + rows_two, :]
    for tap, rows in enumerate(windows):
        grad[tap * width : (tap + 1) * width, :] = lax.dot_general(
            hidden[rows, :], dz_own, (((0,), (0,)), ((), ())), preferred_element_type=F32
        )
    share = grad.shape[0] // shares
    me = place_ref[0]
    bits = shares.bit_length() - 1
    for spot in range(shares):
        back = int(format(spot, f"0{bits}b")[::-1], 2)
        block = grad[pl.ds(pl.multiple_of((me ^ back) * share, 8), share), :]
        if spot < shares // 2:
            keep_ref[spot * share : (spot + 1) * share, :] = block
        else:
            at = (spot - shares // 2) * share
            send_ref[at : at + share, :] = block.astype(BF16)

    turn = (((1,), (1,)), ((), ()))
    dz_one[rows_even:, :] = lax.dot_general(
        dz_own, conv_two_ref[width : 2 * width, :], turn, preferred_element_type=F32
    )
    dz_one[:rows_even, :] = lax.dot_general(
        dz_two[count:, :], conv_two_ref[:width, :], turn, preferred_element_type=F32
    ) + lax.dot_general(
        dz_two[:rows_even, :], conv_two_ref[2 * width :, :], turn, preferred_element_type=F32
    )

    def backward(step, sums):
        at = pl.ds(pl.multiple_of(step * ROWS, ROWS), ROWS)
        normed = norm_one[at, :]
        dact = dz_one[at, :] * slope_one[at, :]
        dnorm = dact * gain
        mean_a = jnp.sum(dnorm, axis=1, keepdims=True) * inv
        mean_b = jnp.sum(dnorm * normed, axis=1, keepdims=True) * inv
        dz = rstd_one[at, :1] * (dnorm - mean_a - normed * mean_b)
        hidden[at, :] = dz.astype(BF16)
        return (
            sums[0] + eighth(dz),
            sums[1] + eighth(dact * normed),
            sums[2] + eighth(dact),
        )

    sums_one = lax.fori_loop(
        0, steps_one, backward, (zero, zero, zero), unroll=together(steps_one)
    )
    first = lax.dot_general(
        taps[...], hidden[...], (((0,), (0,)), ((), ())), preferred_element_type=F32
    )
    small_ref[:TAPS, :] = first[:TAPS, :]
    for spot, sums in enumerate(sums_one + sums_two):
        small_ref[TAPS + spot : TAPS + spot + 1, :] = jnp.sum(sums, axis=0, keepdims=True)
    hi, lo = split_two(small_ref[...])
    half = send_ref.shape[0] - 2 * ROWS
    send_ref[half : half + ROWS, :] = hi
    send_ref[half + ROWS :, :] = lo


def local_pass(record, shares, place, got, cot, weight, conv_two, table):
    count = got.shape[0] // SPARE
    rows_two, width = cot.shape
    rows_one = 2 * rows_two + count
    half = 3 * width // 2
    vmem = pl.BlockSpec(memory_space=pltpu.VMEM)
    return pl.pallas_call(
        functools.partial(local_kernel, record, shares),
        out_shape=(
            jax.ShapeDtypeStruct((half + 2 * ROWS, width), BF16),
            jax.ShapeDtypeStruct((half, width), F32),
            jax.ShapeDtypeStruct((ROWS, width), F32),
        ),
        in_specs=[pl.BlockSpec(memory_space=pltpu.SMEM)] + [vmem] * 5,
        out_specs=(vmem, vmem, vmem),
        scratch_shapes=[
            pltpu.VMEM((rows_one, 128), BF16),
            pltpu.VMEM((count, 128), jnp.int32),
            pltpu.VMEM((rows_one, width), F32),
            pltpu.VMEM((rows_one, width), F32),
            pltpu.VMEM((rows_one, width), F32),
            pltpu.VMEM((rows_one, 128), F32),
            pltpu.VMEM((rows_one, width), BF16),
            pltpu.VMEM((rows_two, width), F32),
            pltpu.VMEM((rows_two + 2 * count, width), BF16),
            pltpu.VMEM((rows_one, width), F32),
            pltpu.VMEM((3 * width, width), F32),
        ],
        cost_estimate=pl.CostEstimate(
            flops=2 * 9 * rows_two * width * width,
            bytes_accessed=8 * rows_one * width,
            transcendentals=3 * rows_one * width,
        ),
        compiler_params=pltpu.CompilerParams(vmem_limit_bytes=36 * 1024 * 1024),
    )(place, got, cot, weight, conv_two, table)


def tree(terms):
    while len(terms) > 1:
        terms = [terms[i] + terms[i + 1] for i in range(0, len(terms), 2)]
    return terms[0]


def exchange(sizes, stage, message):
    far = {axis: 0 for axis in sizes}
    for axis, bit in stage:
        far[axis] ^= 1 << bit
    axes = tuple(axis for axis in sizes if far[axis])
    pairs = [(0, 0)]
    for axis in axes:
        n = sizes[axis]
        pairs = [(a * n + i, b * n + (i ^ far[axis])) for a, b in pairs for i in range(n)]
    return lax.ppermute(message, axes if len(axes) > 1 else axes[0], pairs)


def merge(sizes, stage, blocks, small):
    dp_bits = [item for item in stage if item[0] == "dp"]
    blk_bits = [item for item in stage if item[0] != "dp"]
    hi, lo = split_two(small)
    tail = [hi, lo]
    messages = [jnp.concatenate([block.astype(BF16)] + tail, axis=0) for block in blocks]
    rows = blocks[0].shape[0]
    own = messages[0][:rows].astype(F32) if blk_bits else blocks[0]
    terms = [own]
    smalls = [hi.astype(F32) + lo.astype(F32)]
    for code in range(1, 1 << len(stage)):
        block = code >> len(blk_bits)
        chosen = [b for i, b in enumerate(dp_bits) if block >> (len(dp_bits) - 1 - i) & 1]
        chosen += [b for i, b in enumerate(blk_bits) if code >> i & 1]
        got = exchange(sizes, chosen, messages[block])
        terms.append(got[:rows].astype(F32))
        smalls.append(got[rows : rows + ROWS].astype(F32) + got[rows + ROWS :].astype(F32))
    return tree(terms), tree(smalls)


def per_device(
    sizes,
    waveform,
    length_bin,
    packing,
    cotangent,
    conv_one,
    bias_one,
    gain_one,
    shift_one,
    conv_two,
    bias_two,
    gain_two,
    shift_two,
):
    record = waveform.shape[1]
    count, frames_two, width = cotangent.shape
    shares = sizes["dp"]
    packed = pack(packing, length_bin, waveform)
    packed = packed.reshape(count, SPARE, packed.shape[1])
    got = lax.all_to_all(packed, "dp", split_axis=0, concat_axis=0, tiled=True)
    got = got.reshape(count * SPARE, got.shape[2])
    vectors = (bias_one, gain_one, shift_one, bias_two, gain_two, shift_two)
    table = jnp.concatenate([conv_one.astype(F32), jnp.stack(vectors)], axis=0)
    cot = cotangent.reshape(count * frames_two, width)
    cot, weight = ready(count, cot, table, conv_two)
    place = lax.axis_index("dp").astype(jnp.int32).reshape(1)
    send, keep, small = local_pass(record, shares, place, got, cot, weight, conv_two, table)
    half = keep.shape[0]
    other = exchange(sizes, [("dp", 0)], send)
    total = keep + other[:half].astype(F32)
    mine = send[half : half + ROWS].astype(F32) + send[half + ROWS :].astype(F32)
    yours = other[half : half + ROWS].astype(F32) + other[half + ROWS :].astype(F32)
    small = mine + yours
    left = [("dp", bit) for bit in range(1, shares.bit_length() - 1)]
    left += [("blk", bit) for bit in range(sizes["blk"].bit_length() - 1)]
    while left:
        near = left[0][0] == "dp" and left[0][1] < 3 and len(left) > 2
        stage, left = (left[:2], left[2:]) if near else (left[:1], left[1:])
        parts = 1 << sum(axis == "dp" for axis, _ in stage)
        rows = total.shape[0] // parts
        blocks = [total[i * rows : (i + 1) * rows] for i in range(parts)]
        total, small = merge(sizes, stage, blocks, small)
    return total, small


def solution(mesh):
    sizes = {axis: mesh.shape[axis] for axis in ("dp", "blk")}
    both = ("dp", "blk")
    return jax.shard_map(
        functools.partial(per_device, sizes),
        mesh=mesh,
        in_specs=(P(both, None), P(both), P(both, None), P(both, None, None)) + (P(),) * 8,
        out_specs=(P("dp", None), P()),
        check_vma=False,
    )
```

```python
import functools
import math

import jax
import jax.numpy as jnp
from jax import lax
from jax.experimental import pallas as pl
from jax.experimental.pallas import tpu as pltpu
from jax.sharding import PartitionSpec as P

NB = 4
TAPS = 10
STRIDE = 5
ROWS = 16
SPARE = 8
F32 = jnp.float32
BF16 = jnp.bfloat16


def split_two(x):
    hi = x.astype(BF16)
    return hi, (x - hi.astype(F32)).astype(BF16)


def gelu_parts(act):
    cdf = 0.5 + 0.5 * lax.erf(act * 0.7071067811865476)
    return cdf, 0.3989422804014327 * jnp.exp(-0.5 * (act * act))


def pack_kernel(packing, bins, wave_ref, out_ref, wide):
    count, record = wave_ref.shape
    width = wide.shape[1]
    wide[...] = jnp.zeros_like(wide)
    wide[:, :record] = wave_ref[...].astype(F32)
    lane = lax.broadcasted_iota(jnp.int32, (SPARE, width), 1)

    def one(slot):
        own = packing[0, slot]
        row = jnp.broadcast_to(wide[pl.ds(own, 1), :], (SPARE, width))
        return jnp.where(lane == record, bins[own].astype(F32), row)

    for pair in range(count // 2):
        both = jnp.concatenate([one(2 * pair), one(2 * pair + 1)], axis=0)
        out_ref[2 * SPARE * pair : 2 * SPARE * (pair + 1), :] = both.astype(BF16)


def pack(packing, length_bin, waveform):
    count, record = waveform.shape
    width = -(-(record + 1) // 128) * 128
    return pl.pallas_call(
        pack_kernel,
        out_shape=jax.ShapeDtypeStruct((count * SPARE, width), BF16),
        in_specs=[
            pl.BlockSpec(memory_space=pltpu.SMEM),
            pl.BlockSpec(memory_space=pltpu.SMEM),
            pl.BlockSpec(memory_space=pltpu.VMEM),
        ],
        out_specs=pl.BlockSpec(memory_space=pltpu.VMEM),
        scratch_shapes=[pltpu.VMEM((count, width), F32)],
    )(packing, length_bin, waveform)


def ready_kernel(count, cot_ref, table_ref, conv_two_ref, moved_ref, weight_ref, weight):
    rows_two, width = cot_ref.shape
    frames_two = rows_two // count
    inv = 1.0 / width
    row = lax.broadcasted_iota(jnp.int32, (rows_two, 1), 0)
    origin = (row % count) * frames_two + row // count
    mover = (lax.broadcasted_iota(jnp.int32, (rows_two, rows_two), 1) == origin).astype(BF16)
    moved_ref[...] = jnp.dot(mover, cot_ref[...], preferred_element_type=F32).astype(BF16)
    weight[...] = jnp.zeros_like(weight)
    kernel = table_ref[:TAPS, :]
    kernel = kernel - jnp.sum(kernel, axis=1, keepdims=True) * inv
    bias = table_ref[TAPS : TAPS + 1, :]
    bias = bias - jnp.sum(bias, axis=1, keepdims=True) * inv
    for part in range(3):
        piece = kernel.astype(BF16).astype(F32)
        weight[part * ROWS : part * ROWS + TAPS, :] = piece
        kernel = kernel - piece
        piece = bias.astype(BF16).astype(F32)
        weight[3 * ROWS + part : 3 * ROWS + part + 1, :] = piece
        bias = bias - piece
    weight_ref[...] = weight[...].astype(BF16)


def ready(count, cot, table, conv_two):
    rows_two, width = cot.shape
    vmem = pl.BlockSpec(memory_space=pltpu.VMEM)
    return pl.pallas_call(
        functools.partial(ready_kernel, count),
        out_shape=(
            jax.ShapeDtypeStruct(cot.shape, BF16),
            jax.ShapeDtypeStruct((128, width), BF16),
        ),
        in_specs=[vmem, vmem, vmem],
        out_specs=(vmem, vmem),
        scratch_shapes=[pltpu.VMEM((128, width), F32)],
        cost_estimate=pl.CostEstimate(
            flops=2 * rows_two * rows_two * width,
            bytes_accessed=4 * cot.size,
            transcendentals=0,
        ),
        compiler_params=pltpu.CompilerParams(vmem_limit_bytes=16 * 1024 * 1024),
    )(cot, table, conv_two)


def together(steps):
    return max(n for n in range(1, 66) if steps % n == 0)


def local_kernel(
    record,
    shares,
    place_ref,
    got_ref,
    cot_ref,
    weight_ref,
    conv_two_ref,
    table_ref,
    send_ref,
    keep_ref,
    small_ref,
    taps,
    limits,
    cent_one,
    norm_one,
    slope_one,
    rstd_one,
    hidden,
    norm_two,
    dz_two,
    dz_one,
    grad,
):
    count = got_ref.shape[0] // SPARE
    rows_two, width = cot_ref.shape
    frames_two = rows_two // count
    frames_one = 2 * frames_two + 1
    rows_even = rows_two + count
    rows_one = frames_one * count
    inv = 1.0 / width

    pick = (
        lax.broadcasted_iota(jnp.int32, (count, count * SPARE), 1)
        == SPARE * lax.broadcasted_iota(jnp.int32, (count, count * SPARE), 0)
    ).astype(BF16)
    wave = jnp.dot(pick, got_ref[...], preferred_element_type=F32)
    lane_in = lax.broadcasted_iota(jnp.int32, wave.shape, 1)
    bins = jnp.sum(jnp.where(lane_in == record, wave, 0.0), axis=1, keepdims=True)
    limit = bins.astype(jnp.int32) * frames_two // NB
    limits[...] = jnp.broadcast_to(limit, (count, 128))
    wave = jnp.concatenate([wave, jnp.zeros((count, 128), F32)], axis=1)

    for place, frame in enumerate(
        list(range(0, frames_one, 2)) + list(range(1, frames_one, 2))
    ):
        taps[count * place : count * (place + 1), :] = wave[
            :, STRIDE * frame : STRIDE * frame + 128
        ].astype(BF16)
    src = lax.broadcasted_iota(jnp.int32, (128, 128), 0)
    dst = lax.broadcasted_iota(jnp.int32, (128, 128), 1)
    thrice = ((src < TAPS) & (dst < 3 * ROWS) & (dst % ROWS == src)).astype(BF16)
    lane = lax.broadcasted_iota(jnp.int32, (1, 128), 1)
    ones = ((lane >= 3 * ROWS) & (lane < 3 * ROWS + 3)).astype(F32)
    taps[...] = (jnp.dot(taps[...], thrice, preferred_element_type=F32) + ones).astype(BF16)

    cent_one[...] = jnp.dot(taps[...], weight_ref[...], preferred_element_type=F32)
    gain = table_ref[TAPS + 1 : TAPS + 2, :]
    shift = table_ref[TAPS + 2 : TAPS + 3, :]
    steps_one = rows_one // ROWS
    steps_two = rows_two // ROWS

    def forward(step, _):
        at = pl.ds(pl.multiple_of(step * ROWS, ROWS), ROWS)
        cent = cent_one[at, :]
        var = jnp.sum(cent * cent, axis=1, keepdims=True) * inv
        rstd = lax.rsqrt(var + 1e-05)
        normed = cent * rstd
        act = normed * gain + shift
        cdf, pdf = gelu_parts(act)
        norm_one[at, :] = normed
        rstd_one[at, :] = jnp.broadcast_to(rstd, (ROWS, 128))
        slope_one[at, :] = cdf + act * pdf
        hidden[at, :] = (act * cdf).astype(BF16)
        return 0

    lax.fori_loop(0, steps_one, forward, 0, unroll=together(steps_one))

    windows = (
        slice(0, rows_two),
        slice(rows_even, rows_even + rows_two),
        slice(count, rows_even),
    )
    total = None
    for tap, rows in enumerate(windows):
        term = jnp.dot(
            hidden[rows, :],
            conv_two_ref[tap * width : (tap + 1) * width, :],
            preferred_element_type=F32,
        )
        total = term if total is None else total + term
    norm_two[...] = total

    bias_two = table_ref[TAPS + 3 : TAPS + 4, :]
    gain_b = table_ref[TAPS + 4 : TAPS + 5, :]
    shift_b = table_ref[TAPS + 5 : TAPS + 6, :]
    dz_two[:count, :] = jnp.zeros((count, width), BF16)
    dz_two[count + rows_two :, :] = jnp.zeros((count, width), BF16)

    def eighth(x):
        return x[:8] + x[8:]

    def middle(step, sums):
        start = pl.multiple_of(step * ROWS, ROWS)
        at = pl.ds(start, ROWS)
        first = pl.multiple_of(lax.rem(start, count), ROWS)
        valid = limits[pl.ds(first, ROWS), :1] > lax.div(start, count)
        z = norm_two[at, :] + bias_two
        cent = z - jnp.sum(z, axis=1, keepdims=True) * inv
        var = jnp.sum(cent * cent, axis=1, keepdims=True) * inv
        rstd = lax.rsqrt(var + 1e-05)
        normed = cent * rstd
        act = normed * gain_b + shift_b
        cdf, pdf = gelu_parts(act)
        dact = jnp.where(valid, cot_ref[at, :].astype(F32) * (cdf + act * pdf), 0.0)
        dnorm = dact * gain_b
        mean_a = jnp.sum(dnorm, axis=1, keepdims=True) * inv
        mean_b = jnp.sum(dnorm * normed, axis=1, keepdims=True) * inv
        dz = rstd * (dnorm - mean_a - normed * mean_b)
        dz_two[pl.ds(pl.multiple_of(start + count, ROWS), ROWS), :] = dz.astype(BF16)
        return (
            sums[0] + eighth(dz),
            sums[1] + eighth(dact * normed),
            sums[2] + eighth(dact),
        )

    zero = jnp.zeros((8, width), F32)
    sums_two = lax.fori_loop(
        0, steps_two, middle, (zero, zero, zero), unroll=together(steps_two)
    )

    dz_own = dz_two[count : count + rows_two, :]
    for tap, rows in enumerate(windows):
        grad[tap * width : (tap + 1) * width, :] = lax.dot_general(
            hidden[rows, :], dz_own, (((0,), (0,)), ((), ())), preferred_element_type=F32
        )
    share = grad.shape[0] // shares
    me = place_ref[0]
    bits = shares.bit_length() - 1
    for spot in range(shares):
        back = int(format(spot, f"0{bits}b")[::-1], 2)
        block = grad[pl.ds(pl.multiple_of((me ^ back) * share, 8), share), :]
        if spot < shares // 2:
            keep_ref[spot * share : (spot + 1) * share, :] = block
        else:
            at = (spot - shares // 2) * share
            send_ref[at : at + share, :] = block.astype(BF16)

    turn = (((1,), (1,)), ((), ()))
    dz_one[rows_even:, :] = lax.dot_general(
        dz_own, conv_two_ref[width : 2 * width, :], turn, preferred_element_type=F32
    )
    dz_one[:rows_even, :] = lax.dot_general(
        dz_two[count:, :], conv_two_ref[:width, :], turn, preferred_element_type=F32
    ) + lax.dot_general(
        dz_two[:rows_even, :], conv_two_ref[2 * width :, :], turn, preferred_element_type=F32
    )

    def backward(step, sums):
        at = pl.ds(pl.multiple_of(step * ROWS, ROWS), ROWS)
        normed = norm_one[at, :]
        dact = dz_one[at, :] * slope_one[at, :]
        dnorm = dact * gain
        mean_a = jnp.sum(dnorm, axis=1, keepdims=True) * inv
        mean_b = jnp.sum(dnorm * normed, axis=1, keepdims=True) * inv
        dz = rstd_one[at, :1] * (dnorm - mean_a - normed * mean_b)
        hidden[at, :] = dz.astype(BF16)
        return (
            sums[0] + eighth(dz),
            sums[1] + eighth(dact * normed),
            sums[2] + eighth(dact),
        )

    sums_one = lax.fori_loop(
        0, steps_one, backward, (zero, zero, zero), unroll=together(steps_one)
    )
    first = lax.dot_general(
        taps[...], hidden[...], (((0,), (0,)), ((), ())), preferred_element_type=F32
    )
    small_ref[:TAPS, :] = first[:TAPS, :]
    for spot, sums in enumerate(sums_one + sums_two):
        small_ref[TAPS + spot : TAPS + spot + 1, :] = jnp.sum(sums, axis=0, keepdims=True)
    hi, lo = split_two(small_ref[...])
    half = send_ref.shape[0] - 2 * ROWS
    send_ref[half : half + ROWS, :] = hi
    send_ref[half + ROWS :, :] = lo


def local_pass(record, shares, place, got, cot, weight, conv_two, table):
    count = got.shape[0] // SPARE
    rows_two, width = cot.shape
    rows_one = 2 * rows_two + count
    half = 3 * width // 2
    vmem = pl.BlockSpec(memory_space=pltpu.VMEM)
    return pl.pallas_call(
        functools.partial(local_kernel, record, shares),
        out_shape=(
            jax.ShapeDtypeStruct((half + 2 * ROWS, width), BF16),
            jax.ShapeDtypeStruct((half, width), F32),
            jax.ShapeDtypeStruct((ROWS, width), F32),
        ),
        in_specs=[pl.BlockSpec(memory_space=pltpu.SMEM)] + [vmem] * 5,
        out_specs=(vmem, vmem, vmem),
        scratch_shapes=[
            pltpu.VMEM((rows_one, 128), BF16),
            pltpu.VMEM((count, 128), jnp.int32),
            pltpu.VMEM((rows_one, width), F32),
            pltpu.VMEM((rows_one, width), F32),
            pltpu.VMEM((rows_one, width), F32),
            pltpu.VMEM((rows_one, 128), F32),
            pltpu.VMEM((rows_one, width), BF16),
            pltpu.VMEM((rows_two, width), F32),
            pltpu.VMEM((rows_two + 2 * count, width), BF16),
            pltpu.VMEM((rows_one, width), F32),
            pltpu.VMEM((3 * width, width), F32),
        ],
        cost_estimate=pl.CostEstimate(
            flops=2 * 9 * rows_two * width * width,
            bytes_accessed=8 * rows_one * width,
            transcendentals=3 * rows_one * width,
        ),
        compiler_params=pltpu.CompilerParams(vmem_limit_bytes=36 * 1024 * 1024),
    )(place, got, cot, weight, conv_two, table)


def tree(terms):
    while len(terms) > 1:
        terms = [terms[i] + terms[i + 1] for i in range(0, len(terms), 2)]
    return terms[0]


def exchange(sizes, stage, message):
    far = {axis: 0 for axis in sizes}
    for axis, bit in stage:
        far[axis] ^= 1 << bit
    axes = tuple(axis for axis in sizes if far[axis])
    pairs = [(0, 0)]
    for axis in axes:
        n = sizes[axis]
        pairs = [(a * n + i, b * n + (i ^ far[axis])) for a, b in pairs for i in range(n)]
    return lax.ppermute(message, axes if len(axes) > 1 else axes[0], pairs)


def merge(sizes, stage, blocks, small):
    dp_bits = [item for item in stage if item[0] == "dp"]
    blk_bits = [item for item in stage if item[0] != "dp"]
    hi, lo = split_two(small)
    tail = [hi, lo]
    messages = [jnp.concatenate([block.astype(BF16)] + tail, axis=0) for block in blocks]
    rows = blocks[0].shape[0]
    own = messages[0][:rows].astype(F32) if blk_bits else blocks[0]
    terms = [own]
    smalls = [hi.astype(F32) + lo.astype(F32)]
    for code in range(1, 1 << len(stage)):
        block = code >> len(blk_bits)
        chosen = [b for i, b in enumerate(dp_bits) if block >> (len(dp_bits) - 1 - i) & 1]
        chosen += [b for i, b in enumerate(blk_bits) if code >> i & 1]
        got = exchange(sizes, chosen, messages[block])
        terms.append(got[:rows].astype(F32))
        smalls.append(got[rows : rows + ROWS].astype(F32) + got[rows + ROWS :].astype(F32))
    return tree(terms), tree(smalls)


def per_device(
    sizes,
    waveform,
    length_bin,
    packing,
    cotangent,
    conv_one,
    bias_one,
    gain_one,
    shift_one,
    conv_two,
    bias_two,
    gain_two,
    shift_two,
):
    record = waveform.shape[1]
    count, frames_two, width = cotangent.shape
    shares = sizes["dp"]
    packed = pack(packing, length_bin, waveform)
    packed = packed.reshape(count, SPARE, packed.shape[1])
    got = lax.all_to_all(packed, "dp", split_axis=0, concat_axis=0, tiled=True)
    got = got.reshape(count * SPARE, got.shape[2])
    vectors = (bias_one, gain_one, shift_one, bias_two, gain_two, shift_two)
    table = jnp.concatenate([conv_one.astype(F32), jnp.stack(vectors)], axis=0)
    cot = cotangent.reshape(count * frames_two, width)
    cot, weight = ready(count, cot, table, conv_two)
    place = lax.axis_index("dp").astype(jnp.int32).reshape(1)
    send, keep, small = local_pass(record, shares, place, got, cot, weight, conv_two, table)
    half = keep.shape[0]
    other = exchange(sizes, [("dp", 0)], send)
    total = keep + other[:half].astype(F32)
    mine = send[half : half + ROWS].astype(F32) + send[half + ROWS :].astype(F32)
    yours = other[half : half + ROWS].astype(F32) + other[half + ROWS :].astype(F32)
    small = mine + yours
    left = [("dp", bit) for bit in range(1, shares.bit_length() - 1)]
    left += [("blk", bit) for bit in range(sizes["blk"].bit_length() - 1)]
    while left:
        near = left[0][0] == "dp" and left[0][1] < 3 and len(left) > 2
        stage, left = (left[:2], left[2:]) if near else (left[:1], left[1:])
        parts = 1 << sum(axis == "dp" for axis, _ in stage)
        rows = total.shape[0] // parts
        blocks = [total[i * rows : (i + 1) * rows] for i in range(parts)]
        total, small = merge(sizes, stage, blocks, small)
    return total, small


def solution(mesh):
    sizes = {axis: mesh.shape[axis] for axis in ("dp", "blk")}
    both = ("dp", "blk")
    return jax.shard_map(
        functools.partial(per_device, sizes),
        mesh=mesh,
        in_specs=(P(both, None), P(both), P(both, None), P(both, None, None)) + (P(),) * 8,
        out_specs=(P("dp", None), P()),
        check_vma=False,
    )
```

```python
import functools
import math

import jax
import jax.numpy as jnp
from jax import lax
from jax.experimental import pallas as pl
from jax.experimental.pallas import tpu as pltpu
from jax.sharding import PartitionSpec as P

NB = 4
TAPS = 10
STRIDE = 5
ROWS = 16
SPARE = 8
F32 = jnp.float32
BF16 = jnp.bfloat16


def gelu_parts(act):
    cdf = 0.5 + 0.5 * lax.erf(act * 0.7071067811865476)
    return cdf, 0.3989422804014327 * jnp.exp(-0.5 * (act * act))


def pack_kernel(packing, bins, wave_ref, out_ref, wide):
    count, record = wave_ref.shape
    width = wide.shape[1]
    wide[...] = jnp.zeros_like(wide)
    wide[:, :record] = wave_ref[...].astype(F32)
    lane = lax.broadcasted_iota(jnp.int32, (SPARE, width), 1)

    def one(slot):
        own = packing[0, slot]
        row = jnp.broadcast_to(wide[pl.ds(own, 1), :], (SPARE, width))
        return jnp.where(lane == record, bins[own].astype(F32), row)

    for pair in range(count // 2):
        both = jnp.concatenate([one(2 * pair), one(2 * pair + 1)], axis=0)
        out_ref[2 * SPARE * pair : 2 * SPARE * (pair + 1), :] = both.astype(BF16)


def pack(packing, length_bin, waveform):
    count, record = waveform.shape
    width = -(-(record + 1) // 128) * 128
    return pl.pallas_call(
        pack_kernel,
        out_shape=jax.ShapeDtypeStruct((count * SPARE, width), BF16),
        in_specs=[
            pl.BlockSpec(memory_space=pltpu.SMEM),
            pl.BlockSpec(memory_space=pltpu.SMEM),
            pl.BlockSpec(memory_space=pltpu.VMEM),
        ],
        out_specs=pl.BlockSpec(memory_space=pltpu.VMEM),
        scratch_shapes=[pltpu.VMEM((count, width), F32)],
    )(packing, length_bin, waveform)


def ready_kernel(count, cot_ref, table_ref, conv_two_ref, moved_ref, weight_ref, weight):
    rows_two, width = cot_ref.shape
    frames_two = rows_two // count
    inv = 1.0 / width
    row = lax.broadcasted_iota(jnp.int32, (rows_two, 1), 0)
    origin = (row % count) * frames_two + row // count
    mover = (lax.broadcasted_iota(jnp.int32, (rows_two, rows_two), 1) == origin).astype(BF16)
    moved_ref[...] = jnp.dot(mover, cot_ref[...], preferred_element_type=F32).astype(BF16)
    weight[...] = jnp.zeros_like(weight)
    kernel = table_ref[:TAPS, :]
    kernel = kernel - jnp.sum(kernel, axis=1, keepdims=True) * inv
    bias = table_ref[TAPS : TAPS + 1, :]
    bias = bias - jnp.sum(bias, axis=1, keepdims=True) * inv
    for part in range(3):
        piece = kernel.astype(BF16).astype(F32)
        weight[part * ROWS : part * ROWS + TAPS, :] = piece
        kernel = kernel - piece
        piece = bias.astype(BF16).astype(F32)
        weight[3 * ROWS + part : 3 * ROWS + part + 1, :] = piece
        bias = bias - piece
    weight_ref[...] = weight[...].astype(BF16)


def ready(count, cot, table, conv_two):
    rows_two, width = cot.shape
    vmem = pl.BlockSpec(memory_space=pltpu.VMEM)
    return pl.pallas_call(
        functools.partial(ready_kernel, count),
        out_shape=(
            jax.ShapeDtypeStruct(cot.shape, BF16),
            jax.ShapeDtypeStruct((128, width), BF16),
        ),
        in_specs=[vmem, vmem, vmem],
        out_specs=(vmem, vmem),
        scratch_shapes=[pltpu.VMEM((128, width), F32)],
        cost_estimate=pl.CostEstimate(
            flops=2 * rows_two * rows_two * width,
            bytes_accessed=4 * cot.size,
            transcendentals=0,
        ),
        compiler_params=pltpu.CompilerParams(vmem_limit_bytes=16 * 1024 * 1024),
    )(cot, table, conv_two)


def together(steps):
    return max(n for n in range(1, 66) if steps % n == 0)


def local_kernel(
    record,
    shares,
    place_ref,
    got_ref,
    cot_ref,
    weight_ref,
    conv_two_ref,
    table_ref,
    send_ref,
    keep_ref,
    small_ref,
    taps,
    limits,
    cent_one,
    norm_one,
    slope_one,
    rstd_one,
    hidden,
    norm_two,
    dz_two,
    dz_one,
    grad,
):
    count = got_ref.shape[0] // SPARE
    rows_two, width = cot_ref.shape
    frames_two = rows_two // count
    frames_one = 2 * frames_two + 1
    rows_even = rows_two + count
    rows_one = frames_one * count
    inv = 1.0 / width

    pick = (
        lax.broadcasted_iota(jnp.int32, (count, count * SPARE), 1)
        == SPARE * lax.broadcasted_iota(jnp.int32, (count, count * SPARE), 0)
    ).astype(BF16)
    wave = jnp.dot(pick, got_ref[...], preferred_element_type=F32)
    lane_in = lax.broadcasted_iota(jnp.int32, wave.shape, 1)
    bins = jnp.sum(jnp.where(lane_in == record, wave, 0.0), axis=1, keepdims=True)
    limit = bins.astype(jnp.int32) * frames_two // NB
    limits[...] = jnp.broadcast_to(limit, (count, 128))
    wave = jnp.concatenate([wave, jnp.zeros((count, 128), F32)], axis=1)

    for place, frame in enumerate(
        list(range(0, frames_one, 2)) + list(range(1, frames_one, 2))
    ):
        taps[count * place : count * (place + 1), :] = wave[
            :, STRIDE * frame : STRIDE * frame + 128
        ].astype(BF16)
    src = lax.broadcasted_iota(jnp.int32, (128, 128), 0)
    dst = lax.broadcasted_iota(jnp.int32, (128, 128), 1)
    thrice = ((src < TAPS) & (dst < 3 * ROWS) & (dst % ROWS == src)).astype(BF16)
    lane = lax.broadcasted_iota(jnp.int32, (1, 128), 1)
    ones = ((lane >= 3 * ROWS) & (lane < 3 * ROWS + 3)).astype(F32)
    taps[...] = (jnp.dot(taps[...], thrice, preferred_element_type=F32) + ones).astype(BF16)

    cent_one[...] = jnp.dot(taps[...], weight_ref[...], preferred_element_type=F32)
    gain = table_ref[TAPS + 1 : TAPS + 2, :]
    shift = table_ref[TAPS + 2 : TAPS + 3, :]
    steps_one = rows_one // ROWS
    steps_two = rows_two // ROWS

    def forward(step, _):
        at = pl.ds(pl.multiple_of(step * ROWS, ROWS), ROWS)
        cent = cent_one[at, :]
        var = jnp.sum(cent * cent, axis=1, keepdims=True) * inv
        rstd = lax.rsqrt(var + 1e-05)
        normed = cent * rstd
        act = normed * gain + shift
        cdf, pdf = gelu_parts(act)
        norm_one[at, :] = normed
        rstd_one[at, :] = jnp.broadcast_to(rstd, (ROWS, 128))
        slope_one[at, :] = cdf + act * pdf
        hidden[at, :] = (act * cdf).astype(BF16)
        return 0

    lax.fori_loop(0, steps_one, forward, 0, unroll=together(steps_one))

    windows = (
        slice(0, rows_two),
        slice(rows_even, rows_even + rows_two),
        slice(count, rows_even),
    )
    total = None
    for tap, rows in enumerate(windows):
        term = jnp.dot(
            hidden[rows, :],
            conv_two_ref[tap * width : (tap + 1) * width, :],
            preferred_element_type=F32,
        )
        total = term if total is None else total + term
    norm_two[...] = total

    bias_two = table_ref[TAPS + 3 : TAPS + 4, :]
    gain_b = table_ref[TAPS + 4 : TAPS + 5, :]
    shift_b = table_ref[TAPS + 5 : TAPS + 6, :]
    dz_two[:count, :] = jnp.zeros((count, width), BF16)
    dz_two[count + rows_two :, :] = jnp.zeros((count, width), BF16)

    def eighth(x):
        return x[:8] + x[8:]

    def middle(step, sums):
        start = pl.multiple_of(step * ROWS, ROWS)
        at = pl.ds(start, ROWS)
        first = pl.multiple_of(lax.rem(start, count), ROWS)
        valid = limits[pl.ds(first, ROWS), :1] > lax.div(start, count)
        z = norm_two[at, :] + bias_two
        cent = z - jnp.sum(z, axis=1, keepdims=True) * inv
        var = jnp.sum(cent * cent, axis=1, keepdims=True) * inv
        rstd = lax.rsqrt(var + 1e-05)
        normed = cent * rstd
        act = normed * gain_b + shift_b
        cdf, pdf = gelu_parts(act)
        dact = jnp.where(valid, cot_ref[at, :].astype(F32) * (cdf + act * pdf), 0.0)
        dnorm = dact * gain_b
        mean_a = jnp.sum(dnorm, axis=1, keepdims=True) * inv
        mean_b = jnp.sum(dnorm * normed, axis=1, keepdims=True) * inv
        dz = rstd * (dnorm - mean_a - normed * mean_b)
        dz_two[pl.ds(pl.multiple_of(start + count, ROWS), ROWS), :] = dz.astype(BF16)
        return (
            sums[0] + eighth(dz),
            sums[1] + eighth(dact * normed),
            sums[2] + eighth(dact),
        )

    zero = jnp.zeros((8, width), F32)
    sums_two = lax.fori_loop(
        0, steps_two, middle, (zero, zero, zero), unroll=together(steps_two)
    )

    dz_own = dz_two[count : count + rows_two, :]
    for tap, rows in enumerate(windows):
        grad[tap * width : (tap + 1) * width, :] = lax.dot_general(
            hidden[rows, :], dz_own, (((0,), (0,)), ((), ())), preferred_element_type=F32
        )
    share = grad.shape[0] // shares
    me = place_ref[0]
    bits = shares.bit_length() - 1
    for spot in range(shares):
        back = int(format(spot, f"0{bits}b")[::-1], 2)
        block = grad[pl.ds(pl.multiple_of((me ^ back) * share, 8), share), :]
        if spot < shares // 2:
            keep_ref[spot * share : (spot + 1) * share, :] = block
        else:
            at = (spot - shares // 2) * share
            send_ref[at : at + share, :] = block.astype(BF16)

    turn = (((1,), (1,)), ((), ()))
    dz_one[rows_even:, :] = lax.dot_general(
        dz_own, conv_two_ref[width : 2 * width, :], turn, preferred_element_type=F32
    )
    dz_one[:rows_even, :] = lax.dot_general(
        dz_two[count:, :], conv_two_ref[:width, :], turn, preferred_element_type=F32
    ) + lax.dot_general(
        dz_two[:rows_even, :], conv_two_ref[2 * width :, :], turn, preferred_element_type=F32
    )

    def backward(step, sums):
        at = pl.ds(pl.multiple_of(step * ROWS, ROWS), ROWS)
        normed = norm_one[at, :]
        dact = dz_one[at, :] * slope_one[at, :]
        dnorm = dact * gain
        mean_a = jnp.sum(dnorm, axis=1, keepdims=True) * inv
        mean_b = jnp.sum(dnorm * normed, axis=1, keepdims=True) * inv
        dz = rstd_one[at, :1] * (dnorm - mean_a - normed * mean_b)
        hidden[at, :] = dz.astype(BF16)
        return (
            sums[0] + eighth(dz),
            sums[1] + eighth(dact * normed),
            sums[2] + eighth(dact),
        )

    sums_one = lax.fori_loop(
        0, steps_one, backward, (zero, zero, zero), unroll=together(steps_one)
    )
    first = lax.dot_general(
        taps[...], hidden[...], (((0,), (0,)), ((), ())), preferred_element_type=F32
    )
    small_ref[:TAPS, :] = first[:TAPS, :]
    for spot, sums in enumerate(sums_one + sums_two):
        small_ref[TAPS + spot : TAPS + spot + 1, :] = jnp.sum(sums, axis=0, keepdims=True)


def local_pass(record, shares, place, got, cot, weight, conv_two, table):
    count = got.shape[0] // SPARE
    rows_two, width = cot.shape
    rows_one = 2 * rows_two + count
    half = 3 * width // 2
    vmem = pl.BlockSpec(memory_space=pltpu.VMEM)
    return pl.pallas_call(
        functools.partial(local_kernel, record, shares),
        out_shape=(
            jax.ShapeDtypeStruct((half, width), BF16),
            jax.ShapeDtypeStruct((half, width), F32),
            jax.ShapeDtypeStruct((ROWS, width), F32),
        ),
        in_specs=[pl.BlockSpec(memory_space=pltpu.SMEM)] + [vmem] * 5,
        out_specs=(vmem, vmem, vmem),
        scratch_shapes=[
            pltpu.VMEM((rows_one, 128), BF16),
            pltpu.VMEM((count, 128), jnp.int32),
            pltpu.VMEM((rows_one, width), F32),
            pltpu.VMEM((rows_one, width), F32),
            pltpu.VMEM((rows_one, width), F32),
            pltpu.VMEM((rows_one, 128), F32),
            pltpu.VMEM((rows_one, width), BF16),
            pltpu.VMEM((rows_two, width), F32),
            pltpu.VMEM((rows_two + 2 * count, width), BF16),
            pltpu.VMEM((rows_one, width), F32),
            pltpu.VMEM((3 * width, width), F32),
        ],
        cost_estimate=pl.CostEstimate(
            flops=2 * 9 * rows_two * width * width,
            bytes_accessed=8 * rows_one * width,
            transcendentals=3 * rows_one * width,
        ),
        compiler_params=pltpu.CompilerParams(vmem_limit_bytes=36 * 1024 * 1024),
    )(place, got, cot, weight, conv_two, table)


def tree(terms):
    while len(terms) > 1:
        terms = [terms[i] + terms[i + 1] for i in range(0, len(terms), 2)]
    return terms[0]


def exchange(sizes, stage, message):
    far = {axis: 0 for axis in sizes}
    for axis, bit in stage:
        far[axis] ^= 1 << bit
    axes = tuple(axis for axis in sizes if far[axis])
    pairs = [(0, 0)]
    for axis in axes:
        n = sizes[axis]
        pairs = [(a * n + i, b * n + (i ^ far[axis])) for a, b in pairs for i in range(n)]
    return lax.ppermute(message, axes if len(axes) > 1 else axes[0], pairs)


def sum_all(sizes, send, keep, small):
    near = exchange(sizes, [("dp", 0)], small)
    total = keep + exchange(sizes, [("dp", 0)], send).astype(F32)
    total, small = lax.optimization_barrier((total, small + near))
    left = [("dp", bit) for bit in range(1, sizes["dp"].bit_length() - 1)]
    for bit in left:
        small = small + exchange(sizes, [bit], small)
    if len(left) >= 3:
        pair, onward = left[:2], left[2]
        rows = total.shape[0] // 8
        sums = {}
        for part in (1, 0):
            blocks = [total[(2 * i + part) * rows : (2 * i + part + 1) * rows] for i in range(4)]
            terms = [blocks[0]]
            for code in (1, 2, 3):
                chosen = [bit for i, bit in enumerate(pair) if code >> (1 - i) & 1]
                terms.append(exchange(sizes, chosen, blocks[code].astype(BF16)).astype(F32))
            sums[part] = tree(terms)
        total = sums[0] + exchange(sizes, [onward], sums[1].astype(BF16)).astype(F32)
        left = left[3:]
    for bit in left:
        half = total.shape[0] // 2
        total = total[:half] + exchange(sizes, [bit], total[half:].astype(BF16)).astype(F32)
    rows = total.shape[0]
    for bit in range(sizes["blk"].bit_length() - 1):
        hi = small.astype(BF16)
        lo = (small - hi.astype(F32)).astype(BF16)
        own = jnp.concatenate([total.astype(BF16), hi, lo], axis=0)
        both = own.astype(F32), exchange(sizes, [("blk", bit)], own).astype(F32)
        total = both[0][:rows] + both[1][:rows]
        parts = [b[rows : rows + ROWS] + b[rows + ROWS :] for b in both]
        small = parts[0] + parts[1]
    return total, small


def per_device(
    sizes,
    waveform,
    length_bin,
    packing,
    cotangent,
    conv_one,
    bias_one,
    gain_one,
    shift_one,
    conv_two,
    bias_two,
    gain_two,
    shift_two,
):
    record = waveform.shape[1]
    count, frames_two, width = cotangent.shape
    shares = sizes["dp"]
    packed = pack(packing, length_bin, waveform)
    packed = packed.reshape(count, SPARE, packed.shape[1])
    got = lax.all_to_all(packed, "dp", split_axis=0, concat_axis=0, tiled=True)
    got = got.reshape(count * SPARE, got.shape[2])
    vectors = (bias_one, gain_one, shift_one, bias_two, gain_two, shift_two)
    table = jnp.concatenate([conv_one.astype(F32), jnp.stack(vectors)], axis=0)
    cot = cotangent.reshape(count * frames_two, width)
    cot, weight = ready(count, cot, table, conv_two)
    place = lax.axis_index("dp").astype(jnp.int32).reshape(1)
    send, keep, small = local_pass(record, shares, place, got, cot, weight, conv_two, table)
    return sum_all(sizes, send, keep, small)


def solution(mesh):
    sizes = {axis: mesh.shape[axis] for axis in ("dp", "blk")}
    both = ("dp", "blk")
    return jax.shard_map(
        functools.partial(per_device, sizes),
        mesh=mesh,
        in_specs=(P(both, None), P(both), P(both, None), P(both, None, None)) + (P(),) * 8,
        out_specs=(P("dp", None), P()),
        check_vma=False,
    )
```

```python
import functools
import math

import jax
import jax.numpy as jnp
from jax import lax
from jax.experimental import pallas as pl
from jax.experimental.pallas import tpu as pltpu
from jax.sharding import PartitionSpec as P

NB = 4
TAPS = 10
STRIDE = 5
ROWS = 16
F32 = jnp.float32
BF16 = jnp.bfloat16


def gelu_parts(act):
    cdf = 0.5 + 0.5 * lax.erf(act * 0.7071067811865476)
    return cdf, 0.3989422804014327 * jnp.exp(-0.5 * (act * act))


def split_two(x):
    hi = x.astype(BF16)
    return hi, (x - hi.astype(F32)).astype(BF16)


def pack_kernel(packing, bins, wave_ref, out_ref, wide):
    count, record = wave_ref.shape
    width = wide.shape[1]
    wide[...] = jnp.zeros_like(wide)
    wide[:, :record] = wave_ref[...].astype(F32)
    lane = lax.broadcasted_iota(jnp.int32, (1, width), 1)
    for slot in range(count):
        own = packing[0, slot]
        row = wide[pl.ds(own, 1), :]
        out_ref[slot] = jnp.where(lane == record, bins[own].astype(F32), row)


def pack(packing, length_bin, waveform):
    count, record = waveform.shape
    width = -(-(record + 1) // 128) * 128
    return pl.pallas_call(
        pack_kernel,
        out_shape=jax.ShapeDtypeStruct((count, 1, width), F32),
        in_specs=[
            pl.BlockSpec(memory_space=pltpu.SMEM),
            pl.BlockSpec(memory_space=pltpu.SMEM),
            pl.BlockSpec(memory_space=pltpu.VMEM),
        ],
        out_specs=pl.BlockSpec(memory_space=pltpu.VMEM),
        scratch_shapes=[pltpu.VMEM((count, width), F32)],
    )(packing, length_bin, waveform)


def ready_kernel(count, cot_ref, table_ref, conv_two_ref, moved_ref, weight_ref, weight):
    rows_two, width = cot_ref.shape
    frames_two = rows_two // count
    inv = 1.0 / width
    row = lax.broadcasted_iota(jnp.int32, (rows_two, 1), 0)
    origin = (row % count) * frames_two + row // count
    mover = (lax.broadcasted_iota(jnp.int32, (rows_two, rows_two), 1) == origin).astype(BF16)
    moved_ref[...] = jnp.dot(mover, cot_ref[...], preferred_element_type=F32).astype(BF16)
    weight[...] = jnp.zeros_like(weight)
    kernel = table_ref[:TAPS, :]
    kernel = kernel - jnp.sum(kernel, axis=1, keepdims=True) * inv
    bias = table_ref[TAPS : TAPS + 1, :]
    bias = bias - jnp.sum(bias, axis=1, keepdims=True) * inv
    for part in range(3):
        piece = kernel.astype(BF16).astype(F32)
        weight[part * ROWS : part * ROWS + TAPS, :] = piece
        kernel = kernel - piece
        piece = bias.astype(BF16).astype(F32)
        weight[3 * ROWS + part : 3 * ROWS + part + 1, :] = piece
        bias = bias - piece
    weight_ref[...] = weight[...].astype(BF16)


def ready(count, cot, table, conv_two):
    rows_two, width = cot.shape
    vmem = pl.BlockSpec(memory_space=pltpu.VMEM)
    return pl.pallas_call(
        functools.partial(ready_kernel, count),
        out_shape=(
            jax.ShapeDtypeStruct(cot.shape, BF16),
            jax.ShapeDtypeStruct((128, width), BF16),
        ),
        in_specs=[vmem, vmem, vmem],
        out_specs=(vmem, vmem),
        scratch_shapes=[pltpu.VMEM((128, width), F32)],
        cost_estimate=pl.CostEstimate(
            flops=2 * rows_two * rows_two * width,
            bytes_accessed=4 * cot.size,
            transcendentals=0,
        ),
        compiler_params=pltpu.CompilerParams(vmem_limit_bytes=16 * 1024 * 1024),
    )(cot, table, conv_two)


def together(steps):
    return max(n for n in range(1, 66) if steps % n == 0)


def bit_order(shares):
    bits = shares.bit_length() - 1
    return [0, 3, 1, 2, *range(4, bits)]


def local_kernel(
    record,
    shares,
    place_ref,
    got_ref,
    cot_ref,
    weight_ref,
    conv_two_ref,
    table_ref,
    send_ref,
    keep_ref,
    small_ref,
    taps,
    limits,
    cent_one,
    norm_one,
    slope_one,
    rstd_one,
    hidden,
    norm_two,
    dz_two,
    dz_one,
    grad,
):
    count = got_ref.shape[0]
    rows_two, width = cot_ref.shape
    frames_two = rows_two // count
    frames_one = 2 * frames_two + 1
    rows_even = rows_two + count
    rows_one = frames_one * count
    inv = 1.0 / width

    wave = jnp.concatenate([got_ref[slot] for slot in range(count)], axis=0)
    lane_in = lax.broadcasted_iota(jnp.int32, wave.shape, 1)
    bins = jnp.sum(jnp.where(lane_in == record, wave, 0.0), axis=1, keepdims=True)
    limit = bins.astype(jnp.int32) * frames_two // NB
    limits[...] = jnp.broadcast_to(limit, (count, 128))
    wave = jnp.concatenate([wave, jnp.zeros((count, 128), F32)], axis=1)

    for place, frame in enumerate(
        list(range(0, frames_one, 2)) + list(range(1, frames_one, 2))
    ):
        taps[count * place : count * (place + 1), :] = wave[
            :, STRIDE * frame : STRIDE * frame + 128
        ].astype(BF16)
    src = lax.broadcasted_iota(jnp.int32, (128, 128), 0)
    dst = lax.broadcasted_iota(jnp.int32, (128, 128), 1)
    thrice = ((src < TAPS) & (dst < 3 * ROWS) & (dst % ROWS == src)).astype(BF16)
    lane = lax.broadcasted_iota(jnp.int32, (1, 128), 1)
    ones = ((lane >= 3 * ROWS) & (lane < 3 * ROWS + 3)).astype(F32)
    taps[...] = (jnp.dot(taps[...], thrice, preferred_element_type=F32) + ones).astype(BF16)

    cent_one[...] = jnp.dot(taps[...], weight_ref[...], preferred_element_type=F32)
    gain = table_ref[TAPS + 1 : TAPS + 2, :]
    shift = table_ref[TAPS + 2 : TAPS + 3, :]
    steps_one = rows_one // ROWS
    steps_two = rows_two // ROWS

    def forward(step, _):
        at = pl.ds(pl.multiple_of(step * ROWS, ROWS), ROWS)
        cent = cent_one[at, :]
        var = jnp.sum(cent * cent, axis=1, keepdims=True) * inv
        rstd = lax.rsqrt(var + 1e-05)
        normed = cent * rstd
        act = normed * gain + shift
        cdf, pdf = gelu_parts(act)
        norm_one[at, :] = normed
        rstd_one[at, :] = jnp.broadcast_to(rstd, (ROWS, 128))
        slope_one[at, :] = cdf + act * pdf
        hidden[at, :] = (act * cdf).astype(BF16)
        return 0

    lax.fori_loop(0, steps_one, forward, 0, unroll=together(steps_one))

    windows = (
        slice(0, rows_two),
        slice(rows_even, rows_even + rows_two),
        slice(count, rows_even),
    )
    total = None
    for tap, rows in enumerate(windows):
        term = jnp.dot(
            hidden[rows, :],
            conv_two_ref[tap * width : (tap + 1) * width, :],
            preferred_element_type=F32,
        )
        total = term if total is None else total + term
    norm_two[...] = total

    bias_two = table_ref[TAPS + 3 : TAPS + 4, :]
    gain_b = table_ref[TAPS + 4 : TAPS + 5, :]
    shift_b = table_ref[TAPS + 5 : TAPS + 6, :]
    dz_two[:count, :] = jnp.zeros((count, width), BF16)
    dz_two[count + rows_two :, :] = jnp.zeros((count, width), BF16)

    def eighth(x):
        return x[:8] + x[8:]

    def middle(step, sums):
        start = pl.multiple_of(step * ROWS, ROWS)
        at = pl.ds(start, ROWS)
        first = pl.multiple_of(lax.rem(start, count), ROWS)
        valid = limits[pl.ds(first, ROWS), :1] > lax.div(start, count)
        z = norm_two[at, :] + bias_two
        cent = z - jnp.sum(z, axis=1, keepdims=True) * inv
        var = jnp.sum(cent * cent, axis=1, keepdims=True) * inv
        rstd = lax.rsqrt(var + 1e-05)
        normed = cent * rstd
        act = normed * gain_b + shift_b
        cdf, pdf = gelu_parts(act)
        dact = jnp.where(valid, cot_ref[at, :].astype(F32) * (cdf + act * pdf), 0.0)
        dnorm = dact * gain_b
        mean_a = jnp.sum(dnorm, axis=1, keepdims=True) * inv
        mean_b = jnp.sum(dnorm * normed, axis=1, keepdims=True) * inv
        dz = rstd * (dnorm - mean_a - normed * mean_b)
        dz_two[pl.ds(pl.multiple_of(start + count, ROWS), ROWS), :] = dz.astype(BF16)
        return (
            sums[0] + eighth(dz),
            sums[1] + eighth(dact * normed),
            sums[2] + eighth(dact),
        )

    zero = jnp.zeros((8, width), F32)
    sums_two = lax.fori_loop(
        0, steps_two, middle, (zero, zero, zero), unroll=together(steps_two)
    )

    dz_own = dz_two[count : count + rows_two, :]
    for tap, rows in enumerate(windows):
        grad[tap * width : (tap + 1) * width, :] = lax.dot_general(
            hidden[rows, :], dz_own, (((0,), (0,)), ((), ())), preferred_element_type=F32
        )
    share = grad.shape[0] // shares
    me = place_ref[0]
    order = bit_order(shares)
    half = shares // 2
    for spot in range(shares):
        flip = sum(1 << bit for i, bit in enumerate(reversed(order)) if spot >> i & 1)
        block = grad[pl.ds(pl.multiple_of((me ^ flip) * share, 8), share), :]
        part = send_ref if spot >= half else keep_ref
        at = spot % half * share
        part[at : at + share, :] = block.astype(part.dtype)

    turn = (((1,), (1,)), ((), ()))
    dz_one[rows_even:, :] = lax.dot_general(
        dz_own, conv_two_ref[width : 2 * width, :], turn, preferred_element_type=F32
    )
    dz_one[:rows_even, :] = lax.dot_general(
        dz_two[count:, :], conv_two_ref[:width, :], turn, preferred_element_type=F32
    ) + lax.dot_general(
        dz_two[:rows_even, :], conv_two_ref[2 * width :, :], turn, preferred_element_type=F32
    )

    def backward(step, sums):
        at = pl.ds(pl.multiple_of(step * ROWS, ROWS), ROWS)
        normed = norm_one[at, :]
        dact = dz_one[at, :] * slope_one[at, :]
        dnorm = dact * gain
        mean_a = jnp.sum(dnorm, axis=1, keepdims=True) * inv
        mean_b = jnp.sum(dnorm * normed, axis=1, keepdims=True) * inv
        dz = rstd_one[at, :1] * (dnorm - mean_a - normed * mean_b)
        hidden[at, :] = dz.astype(BF16)
        return (
            sums[0] + eighth(dz),
            sums[1] + eighth(dact * normed),
            sums[2] + eighth(dact),
        )

    sums_one = lax.fori_loop(
        0, steps_one, backward, (zero, zero, zero), unroll=together(steps_one)
    )
    first = lax.dot_general(
        taps[...], hidden[...], (((0,), (0,)), ((), ())), preferred_element_type=F32
    )
    small_ref[:TAPS, :] = first[:TAPS, :]
    for spot, sums in enumerate(sums_one + sums_two):
        small_ref[TAPS + spot : TAPS + spot + 1, :] = jnp.sum(sums, axis=0, keepdims=True)


def local_pass(record, shares, place, got, cot, weight, conv_two, table):
    count = got.shape[0]
    rows_two, width = cot.shape
    rows_one = 2 * rows_two + count
    half = 3 * width // 2
    vmem = pl.BlockSpec(memory_space=pltpu.VMEM)
    return pl.pallas_call(
        functools.partial(local_kernel, record, shares),
        out_shape=(
            jax.ShapeDtypeStruct((half, width), BF16),
            jax.ShapeDtypeStruct((half, width), F32),
            jax.ShapeDtypeStruct((ROWS, width), F32),
        ),
        in_specs=[pl.BlockSpec(memory_space=pltpu.SMEM)] + [vmem] * 5,
        out_specs=(vmem,) * 3,
        scratch_shapes=[
            pltpu.VMEM((rows_one, 128), BF16),
            pltpu.VMEM((count, 128), jnp.int32),
            pltpu.VMEM((rows_one, width), F32),
            pltpu.VMEM((rows_one, width), F32),
            pltpu.VMEM((rows_one, width), F32),
            pltpu.VMEM((rows_one, 128), F32),
            pltpu.VMEM((rows_one, width), BF16),
            pltpu.VMEM((rows_two, width), F32),
            pltpu.VMEM((rows_two + 2 * count, width), BF16),
            pltpu.VMEM((rows_one, width), F32),
            pltpu.VMEM((3 * width, width), F32),
        ],
        cost_estimate=pl.CostEstimate(
            flops=2 * 9 * rows_two * width * width,
            bytes_accessed=8 * rows_one * width,
            transcendentals=3 * rows_one * width,
        ),
        compiler_params=pltpu.CompilerParams(vmem_limit_bytes=36 * 1024 * 1024),
    )(place, got, cot, weight, conv_two, table)


def tree(terms):
    while len(terms) > 1:
        terms = [terms[i] + terms[i + 1] for i in range(0, len(terms), 2)]
    return terms[0]


def exchange(sizes, stage, message):
    far = {axis: 0 for axis in sizes}
    for axis, bit in stage:
        far[axis] ^= 1 << bit
    axes = tuple(axis for axis in sizes if far[axis])
    pairs = [(0, 0)]
    for axis in axes:
        n = sizes[axis]
        pairs = [(a * n + i, b * n + (i ^ far[axis])) for a, b in pairs for i in range(n)]
    return lax.ppermute(message, axes if len(axes) > 1 else axes[0], pairs)


def message(rows, small):
    return jnp.concatenate([rows.astype(BF16), *split_two(small)], axis=0)


def contents(got):
    rows = got.shape[0] - 2 * ROWS
    hi, lo = got[rows : rows + ROWS], got[rows + ROWS :]
    return got[:rows].astype(F32), hi.astype(F32) + lo.astype(F32)


def finish_kernel(own_ref, got_ref, rows_ref, small_ref):
    own, small = contents(own_ref[...])
    got, more = contents(got_ref[...])
    rows_ref[...] = own + got
    small_ref[...] = small + more


def finish(own, got):
    rows, width = own.shape[0] - 2 * ROWS, own.shape[1]
    vmem = pl.BlockSpec(memory_space=pltpu.VMEM)
    return pl.pallas_call(
        finish_kernel,
        out_shape=(
            jax.ShapeDtypeStruct((rows, width), F32),
            jax.ShapeDtypeStruct((ROWS, width), F32),
        ),
        in_specs=[vmem, vmem],
        out_specs=(pl.BlockSpec(), pl.BlockSpec()),
        compiler_params=pltpu.CompilerParams(vmem_limit_bytes=8 * 1024 * 1024),
    )(own, got)


def sum_all(sizes, send, keep, small):
    order = [("dp", bit) for bit in bit_order(sizes["dp"])]
    core, onward, pair, left = order[0], order[1], order[2:4], order[4:]
    small = small + exchange(sizes, [core], small)
    total = keep + exchange(sizes, [core], send).astype(F32)
    rows = total.shape[0] // 8
    near, far = ([total[i * rows : (i + 1) * rows] for i in range(j, j + 4)] for j in (0, 4))
    small = contents(message(far[0], small))[1], small
    fars, smalls, nears = [far[0]], [small[0]], [near[0]]
    chosen = [[bit for i, bit in enumerate(pair) if code >> (1 - i) & 1] for code in range(4)]
    for code in (1, 2, 3):
        got, more = contents(exchange(sizes, chosen[code], message(far[code], small[1])))
        fars.append(got)
        smalls.append(more)
    own = message(tree(fars), tree(smalls))
    for code in (1, 2, 3):
        nears.append(exchange(sizes, chosen[code], near[code].astype(BF16)).astype(F32))
    got, more = contents(exchange(sizes, [onward], own))
    total, small = tree(nears) + got, contents(own)[1] + more
    for bit in left:
        half = total.shape[0] // 2
        own = message(total[half:], small)
        got, more = contents(exchange(sizes, [bit], own))
        total, small = total[:half] + got, contents(own)[1] + more
    bits = sizes["blk"].bit_length() - 1
    for bit in range(bits):
        own = message(total, small)
        got = exchange(sizes, [("blk", bit)], own)
        if bit == bits - 1:
            return finish(own, got)
        (total, small), (got, more) = contents(own), contents(got)
        total, small = total + got, small + more
    return total, small


def per_device(
    sizes,
    waveform,
    length_bin,
    packing,
    cotangent,
    conv_one,
    bias_one,
    gain_one,
    shift_one,
    conv_two,
    bias_two,
    gain_two,
    shift_two,
):
    record = waveform.shape[1]
    count, frames_two, width = cotangent.shape
    shares = sizes["dp"]
    packed = pack(packing, length_bin, waveform)
    got = lax.all_to_all(packed, "dp", split_axis=0, concat_axis=0, tiled=True)
    vectors = (bias_one, gain_one, shift_one, bias_two, gain_two, shift_two)
    table = jnp.concatenate([conv_one.astype(F32), jnp.stack(vectors)], axis=0)
    cot = cotangent.reshape(count * frames_two, width)
    cot, weight = ready(count, cot, table, conv_two)
    place = lax.axis_index("dp").astype(jnp.int32).reshape(1)
    partial = local_pass(record, shares, place, got, cot, weight, conv_two, table)
    return sum_all(sizes, *partial)


def solution(mesh):
    sizes = {axis: mesh.shape[axis] for axis in ("dp", "blk")}
    both = ("dp", "blk")
    return jax.shard_map(
        functools.partial(per_device, sizes),
        mesh=mesh,
        in_specs=(P(both, None), P(both), P(both, None), P(both, None, None)) + (P(),) * 8,
        out_specs=(P("dp", None), P()),
        check_vma=False,
    )
```

```python
import functools
import math

import jax
import jax.numpy as jnp
from jax import lax
from jax.experimental import pallas as pl
from jax.experimental.pallas import tpu as pltpu
from jax.sharding import PartitionSpec as P

NB = 4
TAPS = 10
STRIDE = 5
ROWS = 16
F32 = jnp.float32
BF16 = jnp.bfloat16


def gelu_parts(act):
    cdf = 0.5 + 0.5 * lax.erf(act * 0.7071067811865476)
    return cdf, 0.3989422804014327 * jnp.exp(-0.5 * (act * act))


def split_two(x):
    hi = x.astype(BF16)
    return hi, (x - hi.astype(F32)).astype(BF16)


def pack_kernel(packing, bins, wave_ref, out_ref, wide):
    count, record = wave_ref.shape
    width = wide.shape[1]
    wide[...] = jnp.zeros_like(wide)
    wide[:, :record] = wave_ref[...].astype(F32)
    lane = lax.broadcasted_iota(jnp.int32, (1, width), 1)
    for slot in range(count):
        own = packing[0, slot]
        row = wide[pl.ds(own, 1), :]
        out_ref[slot] = jnp.where(lane == record, bins[own].astype(F32), row)


def pack(packing, length_bin, waveform):
    count, record = waveform.shape
    width = -(-(record + 1) // 128) * 128
    return pl.pallas_call(
        pack_kernel,
        out_shape=jax.ShapeDtypeStruct((count, 1, width), F32),
        in_specs=[
            pl.BlockSpec(memory_space=pltpu.SMEM),
            pl.BlockSpec(memory_space=pltpu.SMEM),
            pl.BlockSpec(memory_space=pltpu.VMEM),
        ],
        out_specs=pl.BlockSpec(memory_space=pltpu.VMEM),
        scratch_shapes=[pltpu.VMEM((count, width), F32)],
    )(packing, length_bin, waveform)


def ready_kernel(count, cot_ref, table_ref, conv_two_ref, moved_ref, weight_ref, weight):
    rows_two, width = cot_ref.shape
    frames_two = rows_two // count
    inv = 1.0 / width
    row = lax.broadcasted_iota(jnp.int32, (rows_two, 1), 0)
    origin = (row % count) * frames_two + row // count
    mover = (lax.broadcasted_iota(jnp.int32, (rows_two, rows_two), 1) == origin).astype(BF16)
    moved_ref[...] = jnp.dot(mover, cot_ref[...], preferred_element_type=F32).astype(BF16)
    weight[...] = jnp.zeros_like(weight)
    kernel = table_ref[:TAPS, :]
    kernel = kernel - jnp.sum(kernel, axis=1, keepdims=True) * inv
    bias = table_ref[TAPS : TAPS + 1, :]
    bias = bias - jnp.sum(bias, axis=1, keepdims=True) * inv
    for part in range(3):
        piece = kernel.astype(BF16).astype(F32)
        weight[part * ROWS : part * ROWS + TAPS, :] = piece
        kernel = kernel - piece
        piece = bias.astype(BF16).astype(F32)
        weight[3 * ROWS + part : 3 * ROWS + part + 1, :] = piece
        bias = bias - piece
    weight_ref[...] = weight[...].astype(BF16)


def ready(count, cot, table, conv_two):
    rows_two, width = cot.shape
    vmem = pl.BlockSpec(memory_space=pltpu.VMEM)
    return pl.pallas_call(
        functools.partial(ready_kernel, count),
        out_shape=(
            jax.ShapeDtypeStruct(cot.shape, BF16),
            jax.ShapeDtypeStruct((128, width), BF16),
        ),
        in_specs=[vmem, vmem, vmem],
        out_specs=(vmem, vmem),
        scratch_shapes=[pltpu.VMEM((128, width), F32)],
        cost_estimate=pl.CostEstimate(
            flops=2 * rows_two * rows_two * width,
            bytes_accessed=4 * cot.size,
            transcendentals=0,
        ),
        compiler_params=pltpu.CompilerParams(vmem_limit_bytes=16 * 1024 * 1024),
    )(cot, table, conv_two)


def together(steps):
    return max(n for n in range(1, 66) if steps % n == 0)


def bit_order(shares):
    bits = shares.bit_length() - 1
    return [0, 3, 1, 2, *range(4, bits)]


def local_kernel(
    record,
    shares,
    place_ref,
    got_ref,
    cot_ref,
    weight_ref,
    conv_two_ref,
    table_ref,
    send_ref,
    keep_ref,
    small_ref,
    taps,
    limits,
    cent_one,
    norm_one,
    slope_one,
    rstd_one,
    hidden,
    norm_two,
    dz_two,
    dz_one,
    grad,
):
    count = got_ref.shape[0]
    rows_two, width = cot_ref.shape
    frames_two = rows_two // count
    frames_one = 2 * frames_two + 1
    rows_even = rows_two + count
    rows_one = frames_one * count
    inv = 1.0 / width

    wave = jnp.concatenate([got_ref[slot] for slot in range(count)], axis=0)
    lane_in = lax.broadcasted_iota(jnp.int32, wave.shape, 1)
    bins = jnp.sum(jnp.where(lane_in == record, wave, 0.0), axis=1, keepdims=True)
    limit = bins.astype(jnp.int32) * frames_two // NB
    limits[...] = jnp.broadcast_to(limit, (count, 128))
    wave = jnp.concatenate([wave, jnp.zeros((count, 128), F32)], axis=1)

    for place, frame in enumerate(
        list(range(0, frames_one, 2)) + list(range(1, frames_one, 2))
    ):
        taps[count * place : count * (place + 1), :] = wave[
            :, STRIDE * frame : STRIDE * frame + 128
        ].astype(BF16)
    src = lax.broadcasted_iota(jnp.int32, (128, 128), 0)
    dst = lax.broadcasted_iota(jnp.int32, (128, 128), 1)
    thrice = ((src < TAPS) & (dst < 3 * ROWS) & (dst % ROWS == src)).astype(BF16)
    lane = lax.broadcasted_iota(jnp.int32, (1, 128), 1)
    ones = ((lane >= 3 * ROWS) & (lane < 3 * ROWS + 3)).astype(F32)
    taps[...] = (jnp.dot(taps[...], thrice, preferred_element_type=F32) + ones).astype(BF16)

    cent_one[...] = jnp.dot(taps[...], weight_ref[...], preferred_element_type=F32)
    gain = table_ref[TAPS + 1 : TAPS + 2, :]
    shift = table_ref[TAPS + 2 : TAPS + 3, :]
    steps_one = rows_one // ROWS
    steps_two = rows_two // ROWS

    def forward(step, _):
        at = pl.ds(pl.multiple_of(step * ROWS, ROWS), ROWS)
        cent = cent_one[at, :]
        var = jnp.sum(cent * cent, axis=1, keepdims=True) * inv
        rstd = lax.rsqrt(var + 1e-05)
        normed = cent * rstd
        act = normed * gain + shift
        cdf, pdf = gelu_parts(act)
        norm_one[at, :] = normed
        rstd_one[at, :] = jnp.broadcast_to(rstd, (ROWS, 128))
        slope_one[at, :] = cdf + act * pdf
        hidden[at, :] = (act * cdf).astype(BF16)
        return 0

    lax.fori_loop(0, steps_one, forward, 0, unroll=together(steps_one))

    windows = (
        slice(0, rows_two),
        slice(rows_even, rows_even + rows_two),
        slice(count, rows_even),
    )
    total = None
    for tap, rows in enumerate(windows):
        term = jnp.dot(
            hidden[rows, :],
            conv_two_ref[tap * width : (tap + 1) * width, :],
            preferred_element_type=F32,
        )
        total = term if total is None else total + term
    norm_two[...] = total

    bias_two = table_ref[TAPS + 3 : TAPS + 4, :]
    gain_b = table_ref[TAPS + 4 : TAPS + 5, :]
    shift_b = table_ref[TAPS + 5 : TAPS + 6, :]
    dz_two[:count, :] = jnp.zeros((count, width), BF16)
    dz_two[count + rows_two :, :] = jnp.zeros((count, width), BF16)

    def eighth(x):
        return x[:8] + x[8:]

    def middle(step, sums):
        start = pl.multiple_of(step * ROWS, ROWS)
        at = pl.ds(start, ROWS)
        first = pl.multiple_of(lax.rem(start, count), ROWS)
        valid = limits[pl.ds(first, ROWS), :1] > lax.div(start, count)
        z = norm_two[at, :] + bias_two
        cent = z - jnp.sum(z, axis=1, keepdims=True) * inv
        var = jnp.sum(cent * cent, axis=1, keepdims=True) * inv
        rstd = lax.rsqrt(var + 1e-05)
        normed = cent * rstd
        act = normed * gain_b + shift_b
        cdf, pdf = gelu_parts(act)
        dact = jnp.where(valid, cot_ref[at, :].astype(F32) * (cdf + act * pdf), 0.0)
        dnorm = dact * gain_b
        mean_a = jnp.sum(dnorm, axis=1, keepdims=True) * inv
        mean_b = jnp.sum(dnorm * normed, axis=1, keepdims=True) * inv
        dz = rstd * (dnorm - mean_a - normed * mean_b)
        dz_two[pl.ds(pl.multiple_of(start + count, ROWS), ROWS), :] = dz.astype(BF16)
        return (
            sums[0] + eighth(dz),
            sums[1] + eighth(dact * normed),
            sums[2] + eighth(dact),
        )

    zero = jnp.zeros((8, width), F32)
    sums_two = lax.fori_loop(
        0, steps_two, middle, (zero, zero, zero), unroll=together(steps_two)
    )

    dz_own = dz_two[count : count + rows_two, :]
    for tap, rows in enumerate(windows):
        grad[tap * width : (tap + 1) * width, :] = lax.dot_general(
            hidden[rows, :], dz_own, (((0,), (0,)), ((), ())), preferred_element_type=F32
        )
    share = grad.shape[0] // shares
    me = place_ref[0]
    order = bit_order(shares)
    half = shares // 2
    for spot in range(shares):
        flip = sum(1 << bit for i, bit in enumerate(reversed(order)) if spot >> i & 1)
        block = grad[pl.ds(pl.multiple_of((me ^ flip) * share, 8), share), :]
        part = send_ref if spot >= half else keep_ref
        at = spot % half * share
        part[at : at + share, :] = block.astype(part.dtype)

    turn = (((1,), (1,)), ((), ()))
    dz_one[rows_even:, :] = lax.dot_general(
        dz_own, conv_two_ref[width : 2 * width, :], turn, preferred_element_type=F32
    )
    dz_one[:rows_even, :] = lax.dot_general(
        dz_two[count:, :], conv_two_ref[:width, :], turn, preferred_element_type=F32
    ) + lax.dot_general(
        dz_two[:rows_even, :], conv_two_ref[2 * width :, :], turn, preferred_element_type=F32
    )

    def backward(step, sums):
        at = pl.ds(pl.multiple_of(step * ROWS, ROWS), ROWS)
        normed = norm_one[at, :]
        dact = dz_one[at, :] * slope_one[at, :]
        dnorm = dact * gain
        mean_a = jnp.sum(dnorm, axis=1, keepdims=True) * inv
        mean_b = jnp.sum(dnorm * normed, axis=1, keepdims=True) * inv
        dz = rstd_one[at, :1] * (dnorm - mean_a - normed * mean_b)
        hidden[at, :] = dz.astype(BF16)
        return (
            sums[0] + eighth(dz),
            sums[1] + eighth(dact * normed),
            sums[2] + eighth(dact),
        )

    sums_one = lax.fori_loop(
        0, steps_one, backward, (zero, zero, zero), unroll=together(steps_one)
    )
    first = lax.dot_general(
        taps[...], hidden[...], (((0,), (0,)), ((), ())), preferred_element_type=F32
    )
    small_ref[:TAPS, :] = first[:TAPS, :]
    for spot, sums in enumerate(sums_one + sums_two):
        small_ref[TAPS + spot : TAPS + spot + 1, :] = jnp.sum(sums, axis=0, keepdims=True)


def local_pass(record, shares, place, got, cot, weight, conv_two, table):
    count = got.shape[0]
    rows_two, width = cot.shape
    rows_one = 2 * rows_two + count
    half = 3 * width // 2
    vmem = pl.BlockSpec(memory_space=pltpu.VMEM)
    return pl.pallas_call(
        functools.partial(local_kernel, record, shares),
        out_shape=(
            jax.ShapeDtypeStruct((half, width), BF16),
            jax.ShapeDtypeStruct((half, width), F32),
            jax.ShapeDtypeStruct((ROWS, width), F32),
        ),
        in_specs=[pl.BlockSpec(memory_space=pltpu.SMEM)] + [vmem] * 5,
        out_specs=(vmem,) * 3,
        scratch_shapes=[
            pltpu.VMEM((rows_one, 128), BF16),
            pltpu.VMEM((count, 128), jnp.int32),
            pltpu.VMEM((rows_one, width), F32),
            pltpu.VMEM((rows_one, width), F32),
            pltpu.VMEM((rows_one, width), F32),
            pltpu.VMEM((rows_one, 128), F32),
            pltpu.VMEM((rows_one, width), BF16),
            pltpu.VMEM((rows_two, width), F32),
            pltpu.VMEM((rows_two + 2 * count, width), BF16),
            pltpu.VMEM((rows_one, width), F32),
            pltpu.VMEM((3 * width, width), F32),
        ],
        cost_estimate=pl.CostEstimate(
            flops=2 * 9 * rows_two * width * width,
            bytes_accessed=8 * rows_one * width,
            transcendentals=3 * rows_one * width,
        ),
        compiler_params=pltpu.CompilerParams(vmem_limit_bytes=36 * 1024 * 1024),
    )(place, got, cot, weight, conv_two, table)


def tree(terms):
    while len(terms) > 1:
        terms = [terms[i] + terms[i + 1] for i in range(0, len(terms), 2)]
    return terms[0]


def exchange(sizes, stage, message):
    far = {axis: 0 for axis in sizes}
    for axis, bit in stage:
        far[axis] ^= 1 << bit
    axes = tuple(axis for axis in sizes if far[axis])
    pairs = [(0, 0)]
    for axis in axes:
        n = sizes[axis]
        pairs = [(a * n + i, b * n + (i ^ far[axis])) for a, b in pairs for i in range(n)]
    return lax.ppermute(message, axes if len(axes) > 1 else axes[0], pairs)


def message(rows, small):
    return jnp.concatenate([rows.astype(BF16), *split_two(small)], axis=0)


def contents(got):
    rows = got.shape[0] - 2 * ROWS
    hi, lo = got[rows : rows + ROWS], got[rows + ROWS :]
    return got[:rows].astype(F32), hi.astype(F32) + lo.astype(F32)


def near_kernel(own_ref, *refs):
    terms = [own_ref[...]] + [ref[...].astype(F32) for ref in refs[:-1]]
    refs[-1][...] = tree(terms)


def near_sum(own, *got):
    vmem = pl.BlockSpec(memory_space=pltpu.VMEM)
    return pl.pallas_call(
        near_kernel,
        out_shape=jax.ShapeDtypeStruct(own.shape, F32),
        in_specs=[vmem] * (1 + len(got)),
        out_specs=vmem,
        cost_estimate=pl.CostEstimate(
            flops=4 * own.size, bytes_accessed=140 * own.size, transcendentals=0
        ),
        compiler_params=pltpu.CompilerParams(vmem_limit_bytes=8 * 1024 * 1024),
    )(own, *got)


def finish_kernel(own_ref, got_ref, rows_ref, small_ref):
    own, small = contents(own_ref[...])
    got, more = contents(got_ref[...])
    rows_ref[...] = own + got
    small_ref[...] = small + more


def finish(own, got):
    rows, width = own.shape[0] - 2 * ROWS, own.shape[1]
    vmem = pl.BlockSpec(memory_space=pltpu.VMEM)
    return pl.pallas_call(
        finish_kernel,
        out_shape=(
            jax.ShapeDtypeStruct((rows, width), F32),
            jax.ShapeDtypeStruct((ROWS, width), F32),
        ),
        in_specs=[vmem, vmem],
        out_specs=(pl.BlockSpec(), pl.BlockSpec()),
        compiler_params=pltpu.CompilerParams(vmem_limit_bytes=8 * 1024 * 1024),
    )(own, got)


def sum_all(sizes, send, keep, small):
    order = [("dp", bit) for bit in bit_order(sizes["dp"])]
    core, onward, pair, left = order[0], order[1], order[2:4], order[4:]
    small = small + exchange(sizes, [core], small)
    total = keep + exchange(sizes, [core], send).astype(F32)
    rows = total.shape[0] // 8
    near, far = ([total[i * rows : (i + 1) * rows] for i in range(j, j + 4)] for j in (0, 4))
    small = contents(message(far[0], small))[1], small
    fars, smalls, nears = [far[0]], [small[0]], []
    chosen = [[bit for i, bit in enumerate(pair) if code >> (1 - i) & 1] for code in range(4)]
    for code in (1, 2, 3):
        got, more = contents(exchange(sizes, chosen[code], message(far[code], small[1])))
        fars.append(got)
        smalls.append(more)
    own = message(tree(fars), tree(smalls))
    for code in (1, 2, 3):
        nears.append(exchange(sizes, chosen[code], near[code].astype(BF16)))
    cut = own.shape[0] // 2 // ROWS * ROWS
    got = [exchange(sizes, [onward], part) for part in (own[:cut], own[cut:])]
    got, more = contents(jnp.concatenate(got, axis=0))
    total, small = near_sum(near[0], *nears) + got, contents(own)[1] + more
    for bit in left:
        half = total.shape[0] // 2
        own = message(total[half:], small)
        got, more = contents(exchange(sizes, [bit], own))
        total, small = total[:half] + got, contents(own)[1] + more
    bits = sizes["blk"].bit_length() - 1
    for bit in range(bits):
        own = message(total, small)
        got = exchange(sizes, [("blk", bit)], own)
        if bit == bits - 1:
            return finish(own, got)
        (total, small), (got, more) = contents(own), contents(got)
        total, small = total + got, small + more
    return total, small


def per_device(
    sizes,
    waveform,
    length_bin,
    packing,
    cotangent,
    conv_one,
    bias_one,
    gain_one,
    shift_one,
    conv_two,
    bias_two,
    gain_two,
    shift_two,
):
    record = waveform.shape[1]
    count, frames_two, width = cotangent.shape
    shares = sizes["dp"]
    packed = pack(packing, length_bin, waveform)
    got = lax.all_to_all(packed, "dp", split_axis=0, concat_axis=0, tiled=True)
    vectors = (bias_one, gain_one, shift_one, bias_two, gain_two, shift_two)
    table = jnp.concatenate([conv_one.astype(F32), jnp.stack(vectors)], axis=0)
    cot = cotangent.reshape(count * frames_two, width)
    cot, weight = ready(count, cot, table, conv_two)
    place = lax.axis_index("dp").astype(jnp.int32).reshape(1)
    partial = local_pass(record, shares, place, got, cot, weight, conv_two, table)
    return sum_all(sizes, *partial)


def solution(mesh):
    sizes = {axis: mesh.shape[axis] for axis in ("dp", "blk")}
    both = ("dp", "blk")
    return jax.shard_map(
        functools.partial(per_device, sizes),
        mesh=mesh,
        in_specs=(P(both, None), P(both), P(both, None), P(both, None, None)) + (P(),) * 8,
        out_specs=(P("dp", None), P()),
        check_vma=False,
    )
```

```python
import functools
import math

import jax
import jax.numpy as jnp
from jax import lax
from jax.experimental import pallas as pl
from jax.experimental.pallas import tpu as pltpu
from jax.sharding import PartitionSpec as P

NB = 4
TAPS = 10
STRIDE = 5
ROWS = 16
F32 = jnp.float32
BF16 = jnp.bfloat16


def gelu_parts(act):
    cdf = 0.5 + 0.5 * lax.erf(act * 0.7071067811865476)
    return cdf, 0.3989422804014327 * jnp.exp(-0.5 * (act * act))


def split_two(x):
    hi = x.astype(BF16)
    return hi, (x - hi.astype(F32)).astype(BF16)


def pack_kernel(packing, bins, wave_ref, out_ref, wide):
    count, record = wave_ref.shape
    width = wide.shape[1]
    wide[...] = jnp.zeros_like(wide)
    wide[:, :record] = wave_ref[...].astype(F32)
    lane = lax.broadcasted_iota(jnp.int32, (1, width), 1)
    for slot in range(count):
        own = packing[0, slot]
        row = wide[pl.ds(own, 1), :]
        out_ref[slot] = jnp.where(lane == record, bins[own].astype(F32), row)


def pack(packing, length_bin, waveform):
    count, record = waveform.shape
    width = -(-(record + 1) // 128) * 128
    return pl.pallas_call(
        pack_kernel,
        out_shape=jax.ShapeDtypeStruct((count, 1, width), F32),
        in_specs=[
            pl.BlockSpec(memory_space=pltpu.SMEM),
            pl.BlockSpec(memory_space=pltpu.SMEM),
            pl.BlockSpec(memory_space=pltpu.VMEM),
        ],
        out_specs=pl.BlockSpec(memory_space=pltpu.VMEM),
        scratch_shapes=[pltpu.VMEM((count, width), F32)],
    )(packing, length_bin, waveform)


def ready_kernel(count, cot_ref, table_ref, conv_two_ref, moved_ref, weight_ref, weight):
    rows_two, width = cot_ref.shape
    frames_two = rows_two // count
    inv = 1.0 / width
    row = lax.broadcasted_iota(jnp.int32, (rows_two, 1), 0)
    origin = (row % count) * frames_two + row // count
    mover = (lax.broadcasted_iota(jnp.int32, (rows_two, rows_two), 1) == origin).astype(BF16)
    moved_ref[...] = jnp.dot(mover, cot_ref[...], preferred_element_type=F32).astype(BF16)
    weight[...] = jnp.zeros_like(weight)
    kernel = table_ref[:TAPS, :]
    kernel = kernel - jnp.sum(kernel, axis=1, keepdims=True) * inv
    bias = table_ref[TAPS : TAPS + 1, :]
    bias = bias - jnp.sum(bias, axis=1, keepdims=True) * inv
    for part in range(3):
        piece = kernel.astype(BF16).astype(F32)
        weight[part * ROWS : part * ROWS + TAPS, :] = piece
        kernel = kernel - piece
        piece = bias.astype(BF16).astype(F32)
        weight[3 * ROWS + part : 3 * ROWS + part + 1, :] = piece
        bias = bias - piece
    weight_ref[...] = weight[...].astype(BF16)


def ready(count, cot, table, conv_two):
    rows_two, width = cot.shape
    vmem = pl.BlockSpec(memory_space=pltpu.VMEM)
    return pl.pallas_call(
        functools.partial(ready_kernel, count),
        out_shape=(
            jax.ShapeDtypeStruct(cot.shape, BF16),
            jax.ShapeDtypeStruct((128, width), BF16),
        ),
        in_specs=[vmem, vmem, vmem],
        out_specs=(vmem, vmem),
        scratch_shapes=[pltpu.VMEM((128, width), F32)],
        cost_estimate=pl.CostEstimate(
            flops=2 * rows_two * rows_two * width,
            bytes_accessed=4 * cot.size,
            transcendentals=0,
        ),
        compiler_params=pltpu.CompilerParams(vmem_limit_bytes=16 * 1024 * 1024),
    )(cot, table, conv_two)


def together(steps):
    return max(n for n in range(1, 66) if steps % n == 0)


def bit_order(shares):
    bits = shares.bit_length() - 1
    return [0, 3, 1, 2, *range(4, bits)]


def local_kernel(
    record,
    shares,
    place_ref,
    got_ref,
    cot_ref,
    weight_ref,
    conv_two_ref,
    table_ref,
    send_far,
    send_near,
    keep_far,
    keep_near,
    small_ref,
    taps,
    limits,
    cent_one,
    norm_one,
    slope_one,
    rstd_one,
    hidden,
    norm_two,
    dz_two,
    dz_one,
    grad,
):
    count = got_ref.shape[0]
    rows_two, width = cot_ref.shape
    frames_two = rows_two // count
    frames_one = 2 * frames_two + 1
    rows_even = rows_two + count
    rows_one = frames_one * count
    inv = 1.0 / width

    wave = jnp.concatenate([got_ref[slot] for slot in range(count)], axis=0)
    lane_in = lax.broadcasted_iota(jnp.int32, wave.shape, 1)
    bins = jnp.sum(jnp.where(lane_in == record, wave, 0.0), axis=1, keepdims=True)
    limit = bins.astype(jnp.int32) * frames_two // NB
    limits[...] = jnp.broadcast_to(limit, (count, 128))
    wave = jnp.concatenate([wave, jnp.zeros((count, 128), F32)], axis=1)

    for place, frame in enumerate(
        list(range(0, frames_one, 2)) + list(range(1, frames_one, 2))
    ):
        taps[count * place : count * (place + 1), :] = wave[
            :, STRIDE * frame : STRIDE * frame + 128
        ].astype(BF16)
    src = lax.broadcasted_iota(jnp.int32, (128, 128), 0)
    dst = lax.broadcasted_iota(jnp.int32, (128, 128), 1)
    thrice = ((src < TAPS) & (dst < 3 * ROWS) & (dst % ROWS == src)).astype(BF16)
    lane = lax.broadcasted_iota(jnp.int32, (1, 128), 1)
    ones = ((lane >= 3 * ROWS) & (lane < 3 * ROWS + 3)).astype(F32)
    taps[...] = (jnp.dot(taps[...], thrice, preferred_element_type=F32) + ones).astype(BF16)

    cent_one[...] = jnp.dot(taps[...], weight_ref[...], preferred_element_type=F32)
    gain = table_ref[TAPS + 1 : TAPS + 2, :]
    shift = table_ref[TAPS + 2 : TAPS + 3, :]
    steps_one = rows_one // ROWS
    steps_two = rows_two // ROWS

    def forward(step, _):
        at = pl.ds(pl.multiple_of(step * ROWS, ROWS), ROWS)
        cent = cent_one[at, :]
        var = jnp.sum(cent * cent, axis=1, keepdims=True) * inv
        rstd = lax.rsqrt(var + 1e-05)
        normed = cent * rstd
        act = normed * gain + shift
        cdf, pdf = gelu_parts(act)
        norm_one[at, :] = normed
        rstd_one[at, :] = jnp.broadcast_to(rstd, (ROWS, 128))
        slope_one[at, :] = cdf + act * pdf
        hidden[at, :] = (act * cdf).astype(BF16)
        return 0

    lax.fori_loop(0, steps_one, forward, 0, unroll=together(steps_one))

    windows = (
        slice(0, rows_two),
        slice(rows_even, rows_even + rows_two),
        slice(count, rows_even),
    )
    total = None
    for tap, rows in enumerate(windows):
        term = jnp.dot(
            hidden[rows, :],
            conv_two_ref[tap * width : (tap + 1) * width, :],
            preferred_element_type=F32,
        )
        total = term if total is None else total + term
    norm_two[...] = total

    bias_two = table_ref[TAPS + 3 : TAPS + 4, :]
    gain_b = table_ref[TAPS + 4 : TAPS + 5, :]
    shift_b = table_ref[TAPS + 5 : TAPS + 6, :]
    dz_two[:count, :] = jnp.zeros((count, width), BF16)
    dz_two[count + rows_two :, :] = jnp.zeros((count, width), BF16)

    def eighth(x):
        return x[:8] + x[8:]

    def middle(step, sums):
        start = pl.multiple_of(step * ROWS, ROWS)
        at = pl.ds(start, ROWS)
        first = pl.multiple_of(lax.rem(start, count), ROWS)
        valid = limits[pl.ds(first, ROWS), :1] > lax.div(start, count)
        z = norm_two[at, :] + bias_two
        cent = z - jnp.sum(z, axis=1, keepdims=True) * inv
        var = jnp.sum(cent * cent, axis=1, keepdims=True) * inv
        rstd = lax.rsqrt(var + 1e-05)
        normed = cent * rstd
        act = normed * gain_b + shift_b
        cdf, pdf = gelu_parts(act)
        dact = jnp.where(valid, cot_ref[at, :].astype(F32) * (cdf + act * pdf), 0.0)
        dnorm = dact * gain_b
        mean_a = jnp.sum(dnorm, axis=1, keepdims=True) * inv
        mean_b = jnp.sum(dnorm * normed, axis=1, keepdims=True) * inv
        dz = rstd * (dnorm - mean_a - normed * mean_b)
        dz_two[pl.ds(pl.multiple_of(start + count, ROWS), ROWS), :] = dz.astype(BF16)
        return (
            sums[0] + eighth(dz),
            sums[1] + eighth(dact * normed),
            sums[2] + eighth(dact),
        )

    zero = jnp.zeros((8, width), F32)
    sums_two = lax.fori_loop(
        0, steps_two, middle, (zero, zero, zero), unroll=together(steps_two)
    )

    dz_own = dz_two[count : count + rows_two, :]
    for tap, rows in enumerate(windows):
        grad[tap * width : (tap + 1) * width, :] = lax.dot_general(
            hidden[rows, :], dz_own, (((0,), (0,)), ((), ())), preferred_element_type=F32
        )
    share = grad.shape[0] // shares
    me = place_ref[0]
    order = bit_order(shares)
    parts = (keep_near, keep_far, send_near, send_far)
    quarter = shares // 4
    for spot in range(shares):
        flip = sum(1 << bit for i, bit in enumerate(reversed(order)) if spot >> i & 1)
        block = grad[pl.ds(pl.multiple_of((me ^ flip) * share, 8), share), :]
        part = parts[spot // quarter]
        at = spot % quarter * share
        part[at : at + share, :] = block.astype(part.dtype)

    turn = (((1,), (1,)), ((), ()))
    dz_one[rows_even:, :] = lax.dot_general(
        dz_own, conv_two_ref[width : 2 * width, :], turn, preferred_element_type=F32
    )
    dz_one[:rows_even, :] = lax.dot_general(
        dz_two[count:, :], conv_two_ref[:width, :], turn, preferred_element_type=F32
    ) + lax.dot_general(
        dz_two[:rows_even, :], conv_two_ref[2 * width :, :], turn, preferred_element_type=F32
    )

    def backward(step, sums):
        at = pl.ds(pl.multiple_of(step * ROWS, ROWS), ROWS)
        normed = norm_one[at, :]
        dact = dz_one[at, :] * slope_one[at, :]
        dnorm = dact * gain
        mean_a = jnp.sum(dnorm, axis=1, keepdims=True) * inv
        mean_b = jnp.sum(dnorm * normed, axis=1, keepdims=True) * inv
        dz = rstd_one[at, :1] * (dnorm - mean_a - normed * mean_b)
        hidden[at, :] = dz.astype(BF16)
        return (
            sums[0] + eighth(dz),
            sums[1] + eighth(dact * normed),
            sums[2] + eighth(dact),
        )

    sums_one = lax.fori_loop(
        0, steps_one, backward, (zero, zero, zero), unroll=together(steps_one)
    )
    first = lax.dot_general(
        taps[...], hidden[...], (((0,), (0,)), ((), ())), preferred_element_type=F32
    )
    small_ref[:TAPS, :] = first[:TAPS, :]
    for spot, sums in enumerate(sums_one + sums_two):
        small_ref[TAPS + spot : TAPS + spot + 1, :] = jnp.sum(sums, axis=0, keepdims=True)


def local_pass(record, shares, place, got, cot, weight, conv_two, table):
    count = got.shape[0]
    rows_two, width = cot.shape
    rows_one = 2 * rows_two + count
    quarter = 3 * width // 4
    vmem = pl.BlockSpec(memory_space=pltpu.VMEM)
    return pl.pallas_call(
        functools.partial(local_kernel, record, shares),
        out_shape=(
            jax.ShapeDtypeStruct((quarter, width), BF16),
            jax.ShapeDtypeStruct((quarter, width), BF16),
            jax.ShapeDtypeStruct((quarter, width), F32),
            jax.ShapeDtypeStruct((quarter, width), F32),
            jax.ShapeDtypeStruct((ROWS, width), F32),
        ),
        in_specs=[pl.BlockSpec(memory_space=pltpu.SMEM)] + [vmem] * 5,
        out_specs=(vmem,) * 5,
        scratch_shapes=[
            pltpu.VMEM((rows_one, 128), BF16),
            pltpu.VMEM((count, 128), jnp.int32),
            pltpu.VMEM((rows_one, width), F32),
            pltpu.VMEM((rows_one, width), F32),
            pltpu.VMEM((rows_one, width), F32),
            pltpu.VMEM((rows_one, 128), F32),
            pltpu.VMEM((rows_one, width), BF16),
            pltpu.VMEM((rows_two, width), F32),
            pltpu.VMEM((rows_two + 2 * count, width), BF16),
            pltpu.VMEM((rows_one, width), F32),
            pltpu.VMEM((3 * width, width), F32),
        ],
        cost_estimate=pl.CostEstimate(
            flops=2 * 9 * rows_two * width * width,
            bytes_accessed=8 * rows_one * width,
            transcendentals=3 * rows_one * width,
        ),
        compiler_params=pltpu.CompilerParams(vmem_limit_bytes=36 * 1024 * 1024),
    )(place, got, cot, weight, conv_two, table)


def tree(terms):
    while len(terms) > 1:
        terms = [terms[i] + terms[i + 1] for i in range(0, len(terms), 2)]
    return terms[0]


def exchange(sizes, stage, message):
    far = {axis: 0 for axis in sizes}
    for axis, bit in stage:
        far[axis] ^= 1 << bit
    axes = tuple(axis for axis in sizes if far[axis])
    pairs = [(0, 0)]
    for axis in axes:
        n = sizes[axis]
        pairs = [(a * n + i, b * n + (i ^ far[axis])) for a, b in pairs for i in range(n)]
    return lax.ppermute(message, axes if len(axes) > 1 else axes[0], pairs)


def message(rows, small):
    return jnp.concatenate([rows.astype(BF16), *split_two(small)], axis=0)


def contents(got):
    rows = got.shape[0] - 2 * ROWS
    hi, lo = got[rows : rows + ROWS], got[rows + ROWS :]
    return got[:rows].astype(F32), hi.astype(F32) + lo.astype(F32)


def near_kernel(own_ref, *refs):
    terms = [own_ref[...]] + [ref[...].astype(F32) for ref in refs[:-1]]
    refs[-1][...] = tree(terms)


def near_sum(own, *got):
    vmem = pl.BlockSpec(memory_space=pltpu.VMEM)
    return pl.pallas_call(
        near_kernel,
        out_shape=jax.ShapeDtypeStruct(own.shape, F32),
        in_specs=[vmem] * (1 + len(got)),
        out_specs=vmem,
        cost_estimate=pl.CostEstimate(
            flops=4 * own.size, bytes_accessed=140 * own.size, transcendentals=0
        ),
        compiler_params=pltpu.CompilerParams(vmem_limit_bytes=8 * 1024 * 1024),
    )(own, *got)


def finish_kernel(own_first, own_second, got_first, got_second, rows_ref, small_ref):
    cut = own_first.shape[0]
    own, small = contents(own_second[...])
    got, more = contents(got_second[...])
    rows_ref[:cut, :] = own_first[...].astype(F32) + got_first[...].astype(F32)
    rows_ref[cut:, :] = own + got
    small_ref[...] = small + more


def finish(*parts):
    rows, width = parts[0].shape[0] + parts[1].shape[0] - 2 * ROWS, parts[0].shape[1]
    vmem = pl.BlockSpec(memory_space=pltpu.VMEM)
    return pl.pallas_call(
        finish_kernel,
        out_shape=(
            jax.ShapeDtypeStruct((rows, width), F32),
            jax.ShapeDtypeStruct((ROWS, width), F32),
        ),
        in_specs=[vmem] * 4,
        out_specs=(pl.BlockSpec(), pl.BlockSpec()),
        compiler_params=pltpu.CompilerParams(vmem_limit_bytes=8 * 1024 * 1024),
    )(*parts)


def sum_all(sizes, send_far, send_near, keep_far, keep_near, small):
    order = [("dp", bit) for bit in bit_order(sizes["dp"])]
    core, onward, pair, left = order[0], order[1], order[2:4], order[4:]
    small = small + exchange(sizes, [core], small)
    far = keep_far + exchange(sizes, [core], send_far).astype(F32)
    near = keep_near + exchange(sizes, [core], send_near).astype(F32)
    rows = far.shape[0] // 4
    near, far = ([part[i * rows : (i + 1) * rows] for i in range(4)] for part in (near, far))
    small = contents(message(far[0], small))[1], small
    fars, smalls, nears = [far[0]], [small[0]], []
    chosen = [[bit for i, bit in enumerate(pair) if code >> (1 - i) & 1] for code in range(4)]
    for code in (1, 2, 3):
        got, more = contents(exchange(sizes, chosen[code], message(far[code], small[1])))
        fars.append(got)
        smalls.append(more)
    own = message(tree(fars), tree(smalls))
    for code in (1, 2, 3):
        nears.append(exchange(sizes, chosen[code], near[code].astype(BF16)))
    cut = own.shape[0] // 2 // ROWS * ROWS
    first, second = (exchange(sizes, [onward], part) for part in (own[:cut], own[cut:]))
    base = near_sum(near[0], *nears)
    first = base[:cut] + first.astype(F32)
    second, more = contents(second)
    second, small = base[cut:] + second, contents(own[cut:])[1] + more
    for bit in left:
        total = jnp.concatenate([first, second], axis=0)
        half = total.shape[0] // 2
        own = message(total[half:], small)
        got, more = contents(exchange(sizes, [bit], own))
        total, small = total[:half] + got, contents(own)[1] + more
        cut = own.shape[0] // 2 // ROWS * ROWS
        first, second = total[:cut], total[cut:]
    bits = sizes["blk"].bit_length() - 1
    for bit in range(bits):
        own = first.astype(BF16), message(second, small)
        got = [exchange(sizes, [("blk", bit)], part) for part in own]
        if bit == bits - 1:
            return finish(*own, *got)
        first = own[0].astype(F32) + got[0].astype(F32)
        (second, small), (more, extra) = contents(own[1]), contents(got[1])
        second, small = second + more, small + extra
    return jnp.concatenate([first, second], axis=0), small


def per_device(
    sizes,
    waveform,
    length_bin,
    packing,
    cotangent,
    conv_one,
    bias_one,
    gain_one,
    shift_one,
    conv_two,
    bias_two,
    gain_two,
    shift_two,
):
    record = waveform.shape[1]
    count, frames_two, width = cotangent.shape
    shares = sizes["dp"]
    packed = pack(packing, length_bin, waveform)
    got = lax.all_to_all(packed, "dp", split_axis=0, concat_axis=0, tiled=True)
    vectors = (bias_one, gain_one, shift_one, bias_two, gain_two, shift_two)
    table = jnp.concatenate([conv_one.astype(F32), jnp.stack(vectors)], axis=0)
    cot = cotangent.reshape(count * frames_two, width)
    cot, weight = ready(count, cot, table, conv_two)
    place = lax.axis_index("dp").astype(jnp.int32).reshape(1)
    partial = local_pass(record, shares, place, got, cot, weight, conv_two, table)
    return sum_all(sizes, *partial)


def solution(mesh):
    sizes = {axis: mesh.shape[axis] for axis in ("dp", "blk")}
    both = ("dp", "blk")
    return jax.shard_map(
        functools.partial(per_device, sizes),
        mesh=mesh,
        in_specs=(P(both, None), P(both), P(both, None), P(both, None, None)) + (P(),) * 8,
        out_specs=(P("dp", None), P()),
        check_vma=False,
    )
```

```python
import functools
import math

import jax
import jax.numpy as jnp
from jax import lax
from jax.experimental import pallas as pl
from jax.experimental.pallas import tpu as pltpu
from jax.sharding import PartitionSpec as P

NB = 4
TAPS = 10
STRIDE = 5
ROWS = 16
F32 = jnp.float32
BF16 = jnp.bfloat16


def gelu_parts(act):
    cdf = 0.5 + 0.5 * lax.erf(act * 0.7071067811865476)
    return cdf, 0.3989422804014327 * jnp.exp(-0.5 * (act * act))


def split_two(x):
    hi = x.astype(BF16)
    return hi, (x - hi.astype(F32)).astype(BF16)


def pack_kernel(packing, bins, wave_ref, out_ref, wide):
    count, record = wave_ref.shape
    width = wide.shape[1]
    wide[...] = jnp.zeros_like(wide)
    wide[:, :record] = wave_ref[...].astype(F32)
    lane = lax.broadcasted_iota(jnp.int32, (1, width), 1)
    for slot in range(count):
        own = packing[0, slot]
        row = wide[pl.ds(own, 1), :]
        out_ref[slot] = jnp.where(lane == record, bins[own].astype(F32), row)


def pack(packing, length_bin, waveform):
    count, record = waveform.shape
    width = -(-(record + 1) // 128) * 128
    return pl.pallas_call(
        pack_kernel,
        out_shape=jax.ShapeDtypeStruct((count, 1, width), F32),
        in_specs=[
            pl.BlockSpec(memory_space=pltpu.SMEM),
            pl.BlockSpec(memory_space=pltpu.SMEM),
            pl.BlockSpec(memory_space=pltpu.VMEM),
        ],
        out_specs=pl.BlockSpec(memory_space=pltpu.VMEM),
        scratch_shapes=[pltpu.VMEM((count, width), F32)],
    )(packing, length_bin, waveform)


def ready_kernel(count, cot_ref, table_ref, conv_two_ref, moved_ref, weight_ref, weight):
    rows_two, width = cot_ref.shape
    frames_two = rows_two // count
    inv = 1.0 / width
    row = lax.broadcasted_iota(jnp.int32, (rows_two, 1), 0)
    origin = (row % count) * frames_two + row // count
    mover = (lax.broadcasted_iota(jnp.int32, (rows_two, rows_two), 1) == origin).astype(BF16)
    moved_ref[...] = jnp.dot(mover, cot_ref[...], preferred_element_type=F32).astype(BF16)
    weight[...] = jnp.zeros_like(weight)
    kernel = table_ref[:TAPS, :]
    kernel = kernel - jnp.sum(kernel, axis=1, keepdims=True) * inv
    bias = table_ref[TAPS : TAPS + 1, :]
    bias = bias - jnp.sum(bias, axis=1, keepdims=True) * inv
    for part in range(3):
        piece = kernel.astype(BF16).astype(F32)
        weight[part * ROWS : part * ROWS + TAPS, :] = piece
        kernel = kernel - piece
        piece = bias.astype(BF16).astype(F32)
        weight[3 * ROWS + part : 3 * ROWS + part + 1, :] = piece
        bias = bias - piece
    weight_ref[...] = weight[...].astype(BF16)


def ready(count, cot, table, conv_two):
    rows_two, width = cot.shape
    vmem = pl.BlockSpec(memory_space=pltpu.VMEM)
    return pl.pallas_call(
        functools.partial(ready_kernel, count),
        out_shape=(
            jax.ShapeDtypeStruct(cot.shape, BF16),
            jax.ShapeDtypeStruct((128, width), BF16),
        ),
        in_specs=[vmem, vmem, vmem],
        out_specs=(vmem, vmem),
        scratch_shapes=[pltpu.VMEM((128, width), F32)],
        cost_estimate=pl.CostEstimate(
            flops=2 * rows_two * rows_two * width,
            bytes_accessed=4 * cot.size,
            transcendentals=0,
        ),
        compiler_params=pltpu.CompilerParams(vmem_limit_bytes=16 * 1024 * 1024),
    )(cot, table, conv_two)


def together(steps):
    return max(n for n in range(1, 66) if steps % n == 0)


def bit_order(shares):
    bits = shares.bit_length() - 1
    return [0, 3, 1, 2, *range(4, bits)]


def local_kernel(
    record,
    shares,
    place_ref,
    got_ref,
    cot_ref,
    weight_ref,
    conv_two_ref,
    table_ref,
    send_far,
    send_near,
    keep_far,
    keep_near,
    small_ref,
    taps,
    limits,
    cent_one,
    norm_one,
    slope_one,
    rstd_one,
    hidden,
    norm_two,
    dz_two,
    dz_one,
    grad,
):
    count = got_ref.shape[0]
    rows_two, width = cot_ref.shape
    frames_two = rows_two // count
    frames_one = 2 * frames_two + 1
    rows_even = rows_two + count
    rows_one = frames_one * count
    inv = 1.0 / width

    wave = jnp.concatenate([got_ref[slot] for slot in range(count)], axis=0)
    lane_in = lax.broadcasted_iota(jnp.int32, wave.shape, 1)
    bins = jnp.sum(jnp.where(lane_in == record, wave, 0.0), axis=1, keepdims=True)
    limit = bins.astype(jnp.int32) * frames_two // NB
    limits[...] = jnp.broadcast_to(limit, (count, 128))
    wave = jnp.concatenate([wave, jnp.zeros((count, 128), F32)], axis=1)

    for place, frame in enumerate(
        list(range(0, frames_one, 2)) + list(range(1, frames_one, 2))
    ):
        taps[count * place : count * (place + 1), :] = wave[
            :, STRIDE * frame : STRIDE * frame + 128
        ].astype(BF16)
    src = lax.broadcasted_iota(jnp.int32, (128, 128), 0)
    dst = lax.broadcasted_iota(jnp.int32, (128, 128), 1)
    thrice = ((src < TAPS) & (dst < 3 * ROWS) & (dst % ROWS == src)).astype(BF16)
    lane = lax.broadcasted_iota(jnp.int32, (1, 128), 1)
    ones = ((lane >= 3 * ROWS) & (lane < 3 * ROWS + 3)).astype(F32)
    taps[...] = (jnp.dot(taps[...], thrice, preferred_element_type=F32) + ones).astype(BF16)

    cent_one[...] = jnp.dot(taps[...], weight_ref[...], preferred_element_type=F32)
    gain = table_ref[TAPS + 1 : TAPS + 2, :]
    shift = table_ref[TAPS + 2 : TAPS + 3, :]
    steps_one = rows_one // ROWS
    steps_two = rows_two // ROWS

    def forward(step, _):
        at = pl.ds(pl.multiple_of(step * ROWS, ROWS), ROWS)
        cent = cent_one[at, :]
        var = jnp.sum(cent * cent, axis=1, keepdims=True) * inv
        rstd = lax.rsqrt(var + 1e-05)
        normed = cent * rstd
        act = normed * gain + shift
        cdf, pdf = gelu_parts(act)
        norm_one[at, :] = normed
        rstd_one[at, :] = jnp.broadcast_to(rstd, (ROWS, 128))
        slope_one[at, :] = cdf + act * pdf
        hidden[at, :] = (act * cdf).astype(BF16)
        return 0

    lax.fori_loop(0, steps_one, forward, 0, unroll=together(steps_one))

    windows = (
        slice(0, rows_two),
        slice(rows_even, rows_even + rows_two),
        slice(count, rows_even),
    )
    total = None
    for tap, rows in enumerate(windows):
        term = jnp.dot(
            hidden[rows, :],
            conv_two_ref[tap * width : (tap + 1) * width, :],
            preferred_element_type=F32,
        )
        total = term if total is None else total + term
    norm_two[...] = total

    bias_two = table_ref[TAPS + 3 : TAPS + 4, :]
    gain_b = table_ref[TAPS + 4 : TAPS + 5, :]
    shift_b = table_ref[TAPS + 5 : TAPS + 6, :]
    dz_two[:count, :] = jnp.zeros((count, width), BF16)
    dz_two[count + rows_two :, :] = jnp.zeros((count, width), BF16)

    def eighth(x):
        return x[:8] + x[8:]

    def middle(step, sums):
        start = pl.multiple_of(step * ROWS, ROWS)
        at = pl.ds(start, ROWS)
        first = pl.multiple_of(lax.rem(start, count), ROWS)
        valid = limits[pl.ds(first, ROWS), :1] > lax.div(start, count)
        z = norm_two[at, :] + bias_two
        cent = z - jnp.sum(z, axis=1, keepdims=True) * inv
        var = jnp.sum(cent * cent, axis=1, keepdims=True) * inv
        rstd = lax.rsqrt(var + 1e-05)
        normed = cent * rstd
        act = normed * gain_b + shift_b
        cdf, pdf = gelu_parts(act)
        dact = jnp.where(valid, cot_ref[at, :].astype(F32) * (cdf + act * pdf), 0.0)
        dnorm = dact * gain_b
        mean_a = jnp.sum(dnorm, axis=1, keepdims=True) * inv
        mean_b = jnp.sum(dnorm * normed, axis=1, keepdims=True) * inv
        dz = rstd * (dnorm - mean_a - normed * mean_b)
        dz_two[pl.ds(pl.multiple_of(start + count, ROWS), ROWS), :] = dz.astype(BF16)
        return (
            sums[0] + eighth(dz),
            sums[1] + eighth(dact * normed),
            sums[2] + eighth(dact),
        )

    zero = jnp.zeros((8, width), F32)
    sums_two = lax.fori_loop(
        0, steps_two, middle, (zero, zero, zero), unroll=together(steps_two)
    )

    dz_own = dz_two[count : count + rows_two, :]
    for tap, rows in enumerate(windows):
        grad[tap * width : (tap + 1) * width, :] = lax.dot_general(
            hidden[rows, :], dz_own, (((0,), (0,)), ((), ())), preferred_element_type=F32
        )
    share = grad.shape[0] // shares
    me = place_ref[0]
    order = bit_order(shares)
    parts = (keep_near, keep_far, send_near, send_far)
    quarter = shares // 4
    for spot in range(shares):
        flip = sum(1 << bit for i, bit in enumerate(reversed(order)) if spot >> i & 1)
        block = grad[pl.ds(pl.multiple_of((me ^ flip) * share, 8), share), :]
        part = parts[spot // quarter]
        at = spot % quarter * share
        part[at : at + share, :] = block.astype(part.dtype)

    turn = (((1,), (1,)), ((), ()))
    dz_one[rows_even:, :] = lax.dot_general(
        dz_own, conv_two_ref[width : 2 * width, :], turn, preferred_element_type=F32
    )
    dz_one[:rows_even, :] = lax.dot_general(
        dz_two[count:, :], conv_two_ref[:width, :], turn, preferred_element_type=F32
    ) + lax.dot_general(
        dz_two[:rows_even, :], conv_two_ref[2 * width :, :], turn, preferred_element_type=F32
    )

    def backward(step, sums):
        at = pl.ds(pl.multiple_of(step * ROWS, ROWS), ROWS)
        normed = norm_one[at, :]
        dact = dz_one[at, :] * slope_one[at, :]
        dnorm = dact * gain
        mean_a = jnp.sum(dnorm, axis=1, keepdims=True) * inv
        mean_b = jnp.sum(dnorm * normed, axis=1, keepdims=True) * inv
        dz = rstd_one[at, :1] * (dnorm - mean_a - normed * mean_b)
        hidden[at, :] = dz.astype(BF16)
        return (
            sums[0] + eighth(dz),
            sums[1] + eighth(dact * normed),
            sums[2] + eighth(dact),
        )

    sums_one = lax.fori_loop(
        0, steps_one, backward, (zero, zero, zero), unroll=together(steps_one)
    )
    first = lax.dot_general(
        taps[...], hidden[...], (((0,), (0,)), ((), ())), preferred_element_type=F32
    )
    small_ref[:TAPS, :] = first[:TAPS, :]
    for spot, sums in enumerate(sums_one + sums_two):
        small_ref[TAPS + spot : TAPS + spot + 1, :] = jnp.sum(sums, axis=0, keepdims=True)


def local_pass(record, shares, place, got, cot, weight, conv_two, table):
    count = got.shape[0]
    rows_two, width = cot.shape
    rows_one = 2 * rows_two + count
    quarter = 3 * width // 4
    vmem = pl.BlockSpec(memory_space=pltpu.VMEM)
    return pl.pallas_call(
        functools.partial(local_kernel, record, shares),
        out_shape=(
            jax.ShapeDtypeStruct((quarter, width), BF16),
            jax.ShapeDtypeStruct((quarter, width), BF16),
            jax.ShapeDtypeStruct((quarter, width), F32),
            jax.ShapeDtypeStruct((quarter, width), F32),
            jax.ShapeDtypeStruct((ROWS, width), F32),
        ),
        in_specs=[pl.BlockSpec(memory_space=pltpu.SMEM)] + [vmem] * 5,
        out_specs=(vmem,) * 5,
        scratch_shapes=[
            pltpu.VMEM((rows_one, 128), BF16),
            pltpu.VMEM((count, 128), jnp.int32),
            pltpu.VMEM((rows_one, width), F32),
            pltpu.VMEM((rows_one, width), F32),
            pltpu.VMEM((rows_one, width), F32),
            pltpu.VMEM((rows_one, 128), F32),
            pltpu.VMEM((rows_one, width), BF16),
            pltpu.VMEM((rows_two, width), F32),
            pltpu.VMEM((rows_two + 2 * count, width), BF16),
            pltpu.VMEM((rows_one, width), F32),
            pltpu.VMEM((3 * width, width), F32),
        ],
        cost_estimate=pl.CostEstimate(
            flops=2 * 9 * rows_two * width * width,
            bytes_accessed=8 * rows_one * width,
            transcendentals=3 * rows_one * width,
        ),
        compiler_params=pltpu.CompilerParams(vmem_limit_bytes=36 * 1024 * 1024),
    )(place, got, cot, weight, conv_two, table)


def tree(terms):
    while len(terms) > 1:
        terms = [terms[i] + terms[i + 1] for i in range(0, len(terms), 2)]
    return terms[0]


def exchange(sizes, stage, message):
    far = {axis: 0 for axis in sizes}
    for axis, bit in stage:
        far[axis] ^= 1 << bit
    axes = tuple(axis for axis in sizes if far[axis])
    pairs = [(0, 0)]
    for axis in axes:
        n = sizes[axis]
        pairs = [(a * n + i, b * n + (i ^ far[axis])) for a, b in pairs for i in range(n)]
    return lax.ppermute(message, axes if len(axes) > 1 else axes[0], pairs)


def message(rows, small):
    return jnp.concatenate([rows.astype(BF16), *split_two(small)], axis=0)


def contents(got):
    rows = got.shape[0] - 2 * ROWS
    hi, lo = got[rows : rows + ROWS], got[rows + ROWS :]
    return got[:rows].astype(F32), hi.astype(F32) + lo.astype(F32)


def finish_kernel(own_first, own_second, got_first, got_second, rows_ref, small_ref):
    cut = own_first.shape[0]
    own, small = contents(own_second[...])
    got, more = contents(got_second[...])
    rows_ref[:cut, :] = own_first[...].astype(F32) + got_first[...].astype(F32)
    rows_ref[cut:, :] = own + got
    small_ref[...] = small + more


def finish(*parts):
    rows, width = parts[0].shape[0] + parts[1].shape[0] - 2 * ROWS, parts[0].shape[1]
    vmem = pl.BlockSpec(memory_space=pltpu.VMEM)
    return pl.pallas_call(
        finish_kernel,
        out_shape=(
            jax.ShapeDtypeStruct((rows, width), F32),
            jax.ShapeDtypeStruct((ROWS, width), F32),
        ),
        in_specs=[vmem] * 4,
        out_specs=(pl.BlockSpec(), pl.BlockSpec()),
        compiler_params=pltpu.CompilerParams(vmem_limit_bytes=8 * 1024 * 1024),
    )(*parts)


def sum_all(sizes, send_far, send_near, keep_far, keep_near, small):
    order = [("dp", bit) for bit in bit_order(sizes["dp"])]
    core, onward, pair, left = order[0], order[1], order[2:4], order[4:]
    small = small + exchange(sizes, [core], small)
    far = keep_far + exchange(sizes, [core], send_far).astype(F32)
    near = keep_near + exchange(sizes, [core], send_near).astype(F32)
    rows = far.shape[0] // 4
    near, far = ([part[i * rows : (i + 1) * rows] for i in range(4)] for part in (near, far))
    chosen = [[bit for i, bit in enumerate(pair) if code >> (1 - i) & 1] for code in range(4)]
    fars, nears = [far[0]], [near[0]]
    smalls = [contents(message(near[0], small))[1]]
    for code in (1, 2, 3):
        fars.append(exchange(sizes, chosen[code], far[code].astype(BF16)).astype(F32))
    for code in (1, 2, 3):
        got, more = contents(exchange(sizes, chosen[code], message(near[code], small)))
        nears.append(got)
        smalls.append(more)
    away, base = tree(fars), tree(nears)
    cut = (away.shape[0] + 2 * ROWS) // 2 // ROWS * ROWS
    own = message(away[cut:], tree(smalls))
    first = exchange(sizes, [onward], away[:cut].astype(BF16))
    second, more = contents(exchange(sizes, [onward], own))
    first = base[:cut] + first.astype(F32)
    second, small = base[cut:] + second, contents(own)[1] + more
    for bit in left:
        total = jnp.concatenate([first, second], axis=0)
        half = total.shape[0] // 2
        own = message(total[half:], small)
        got, more = contents(exchange(sizes, [bit], own))
        total, small = total[:half] + got, contents(own)[1] + more
        cut = own.shape[0] // 2 // ROWS * ROWS
        first, second = total[:cut], total[cut:]
    bits = sizes["blk"].bit_length() - 1
    for bit in range(bits):
        own = first.astype(BF16), message(second, small)
        got = [exchange(sizes, [("blk", bit)], part) for part in own]
        if bit == bits - 1:
            return finish(*own, *got)
        first = own[0].astype(F32) + got[0].astype(F32)
        (second, small), (more, extra) = contents(own[1]), contents(got[1])
        second, small = second + more, small + extra
    return jnp.concatenate([first, second], axis=0), small


def per_device(
    sizes,
    waveform,
    length_bin,
    packing,
    cotangent,
    conv_one,
    bias_one,
    gain_one,
    shift_one,
    conv_two,
    bias_two,
    gain_two,
    shift_two,
):
    record = waveform.shape[1]
    count, frames_two, width = cotangent.shape
    shares = sizes["dp"]
    packed = pack(packing, length_bin, waveform)
    got = lax.all_to_all(packed, "dp", split_axis=0, concat_axis=0, tiled=True)
    vectors = (bias_one, gain_one, shift_one, bias_two, gain_two, shift_two)
    table = jnp.concatenate([conv_one.astype(F32), jnp.stack(vectors)], axis=0)
    cot = cotangent.reshape(count * frames_two, width)
    cot, weight = ready(count, cot, table, conv_two)
    place = lax.axis_index("dp").astype(jnp.int32).reshape(1)
    partial = local_pass(record, shares, place, got, cot, weight, conv_two, table)
    return sum_all(sizes, *partial)


def solution(mesh):
    sizes = {axis: mesh.shape[axis] for axis in ("dp", "blk")}
    both = ("dp", "blk")
    return jax.shard_map(
        functools.partial(per_device, sizes),
        mesh=mesh,
        in_specs=(P(both, None), P(both), P(both, None), P(both, None, None)) + (P(),) * 8,
        out_specs=(P("dp", None), P()),
        check_vma=False,
    )
```

```python
import functools
import math

import jax
import jax.numpy as jnp
from jax import lax
from jax.experimental import pallas as pl
from jax.experimental.pallas import tpu as pltpu
from jax.sharding import PartitionSpec as P

NB = 4
TAPS = 10
STRIDE = 5
ROWS = 16
F32 = jnp.float32
BF16 = jnp.bfloat16


def gelu_parts(act):
    cdf = 0.5 + 0.5 * lax.erf(act * 0.7071067811865476)
    return cdf, 0.3989422804014327 * jnp.exp(-0.5 * (act * act))


def split_two(x):
    hi = x.astype(BF16)
    return hi, (x - hi.astype(F32)).astype(BF16)


def pack_kernel(packing, bins, wave_ref, out_ref, wide):
    count, record = wave_ref.shape
    width = wide.shape[1]
    wide[...] = jnp.zeros_like(wide)
    wide[:, :record] = wave_ref[...].astype(F32)
    lane = lax.broadcasted_iota(jnp.int32, (1, width), 1)
    for slot in range(count):
        own = packing[0, slot]
        row = wide[pl.ds(own, 1), :]
        out_ref[slot] = jnp.where(lane == record, bins[own].astype(F32), row)


def pack(packing, length_bin, waveform):
    count, record = waveform.shape
    width = -(-(record + 1) // 128) * 128
    return pl.pallas_call(
        pack_kernel,
        out_shape=jax.ShapeDtypeStruct((count, 1, width), F32),
        in_specs=[
            pl.BlockSpec(memory_space=pltpu.SMEM),
            pl.BlockSpec(memory_space=pltpu.SMEM),
            pl.BlockSpec(memory_space=pltpu.VMEM),
        ],
        out_specs=pl.BlockSpec(memory_space=pltpu.VMEM),
        scratch_shapes=[pltpu.VMEM((count, width), F32)],
    )(packing, length_bin, waveform)


def ready_kernel(count, cot_ref, table_ref, conv_two_ref, moved_ref, weight_ref, weight):
    rows_two, width = cot_ref.shape
    frames_two = rows_two // count
    inv = 1.0 / width
    row = lax.broadcasted_iota(jnp.int32, (rows_two, 1), 0)
    origin = (row % count) * frames_two + row // count
    mover = (lax.broadcasted_iota(jnp.int32, (rows_two, rows_two), 1) == origin).astype(BF16)
    moved_ref[...] = jnp.dot(mover, cot_ref[...], preferred_element_type=F32).astype(BF16)
    weight[...] = jnp.zeros_like(weight)
    kernel = table_ref[:TAPS, :]
    kernel = kernel - jnp.sum(kernel, axis=1, keepdims=True) * inv
    bias = table_ref[TAPS : TAPS + 1, :]
    bias = bias - jnp.sum(bias, axis=1, keepdims=True) * inv
    for part in range(3):
        piece = kernel.astype(BF16).astype(F32)
        weight[part * ROWS : part * ROWS + TAPS, :] = piece
        kernel = kernel - piece
        piece = bias.astype(BF16).astype(F32)
        weight[3 * ROWS + part : 3 * ROWS + part + 1, :] = piece
        bias = bias - piece
    weight_ref[...] = weight[...].astype(BF16)


def ready(count, cot, table, conv_two):
    rows_two, width = cot.shape
    vmem = pl.BlockSpec(memory_space=pltpu.VMEM)
    return pl.pallas_call(
        functools.partial(ready_kernel, count),
        out_shape=(
            jax.ShapeDtypeStruct(cot.shape, BF16),
            jax.ShapeDtypeStruct((128, width), BF16),
        ),
        in_specs=[vmem, vmem, vmem],
        out_specs=(vmem, vmem),
        scratch_shapes=[pltpu.VMEM((128, width), F32)],
        cost_estimate=pl.CostEstimate(
            flops=2 * rows_two * rows_two * width,
            bytes_accessed=4 * cot.size,
            transcendentals=0,
        ),
        compiler_params=pltpu.CompilerParams(vmem_limit_bytes=16 * 1024 * 1024),
    )(cot, table, conv_two)


def together(steps):
    return max(n for n in range(1, 66) if steps % n == 0)


def bit_order(shares, core):
    return [0, 3, *((2, 1) if core else (1, 2)), *range(4, shares.bit_length() - 1)]


def local_kernel(
    record,
    shares,
    place_ref,
    got_ref,
    cot_ref,
    weight_ref,
    conv_two_ref,
    table_ref,
    send_far,
    send_near,
    keep_far,
    keep_near,
    small_ref,
    taps,
    limits,
    cent_one,
    norm_one,
    slope_one,
    rstd_one,
    hidden,
    norm_two,
    dz_two,
    dz_one,
    grad,
):
    count = got_ref.shape[0]
    rows_two, width = cot_ref.shape
    frames_two = rows_two // count
    frames_one = 2 * frames_two + 1
    rows_even = rows_two + count
    rows_one = frames_one * count
    inv = 1.0 / width

    wave = jnp.concatenate([got_ref[slot] for slot in range(count)], axis=0)
    lane_in = lax.broadcasted_iota(jnp.int32, wave.shape, 1)
    bins = jnp.sum(jnp.where(lane_in == record, wave, 0.0), axis=1, keepdims=True)
    limit = bins.astype(jnp.int32) * frames_two // NB
    limits[...] = jnp.broadcast_to(limit, (count, 128))
    wave = jnp.concatenate([wave, jnp.zeros((count, 128), F32)], axis=1)

    for place, frame in enumerate(
        list(range(0, frames_one, 2)) + list(range(1, frames_one, 2))
    ):
        taps[count * place : count * (place + 1), :] = wave[
            :, STRIDE * frame : STRIDE * frame + 128
        ].astype(BF16)
    src = lax.broadcasted_iota(jnp.int32, (128, 128), 0)
    dst = lax.broadcasted_iota(jnp.int32, (128, 128), 1)
    thrice = ((src < TAPS) & (dst < 3 * ROWS) & (dst % ROWS == src)).astype(BF16)
    lane = lax.broadcasted_iota(jnp.int32, (1, 128), 1)
    ones = ((lane >= 3 * ROWS) & (lane < 3 * ROWS + 3)).astype(F32)
    taps[...] = (jnp.dot(taps[...], thrice, preferred_element_type=F32) + ones).astype(BF16)

    cent_one[...] = jnp.dot(taps[...], weight_ref[...], preferred_element_type=F32)
    gain = table_ref[TAPS + 1 : TAPS + 2, :]
    shift = table_ref[TAPS + 2 : TAPS + 3, :]
    steps_one = rows_one // ROWS
    steps_two = rows_two // ROWS

    def forward(step, _):
        at = pl.ds(pl.multiple_of(step * ROWS, ROWS), ROWS)
        cent = cent_one[at, :]
        var = jnp.sum(cent * cent, axis=1, keepdims=True) * inv
        rstd = lax.rsqrt(var + 1e-05)
        normed = cent * rstd
        act = normed * gain + shift
        cdf, pdf = gelu_parts(act)
        norm_one[at, :] = normed
        rstd_one[at, :] = jnp.broadcast_to(rstd, (ROWS, 128))
        slope_one[at, :] = cdf + act * pdf
        hidden[at, :] = (act * cdf).astype(BF16)
        return 0

    lax.fori_loop(0, steps_one, forward, 0, unroll=together(steps_one))

    windows = (
        slice(0, rows_two),
        slice(rows_even, rows_even + rows_two),
        slice(count, rows_even),
    )
    total = None
    for tap, rows in enumerate(windows):
        term = jnp.dot(
            hidden[rows, :],
            conv_two_ref[tap * width : (tap + 1) * width, :],
            preferred_element_type=F32,
        )
        total = term if total is None else total + term
    norm_two[...] = total

    bias_two = table_ref[TAPS + 3 : TAPS + 4, :]
    gain_b = table_ref[TAPS + 4 : TAPS + 5, :]
    shift_b = table_ref[TAPS + 5 : TAPS + 6, :]
    dz_two[:count, :] = jnp.zeros((count, width), BF16)
    dz_two[count + rows_two :, :] = jnp.zeros((count, width), BF16)

    def eighth(x):
        return x[:8] + x[8:]

    def middle(step, sums):
        start = pl.multiple_of(step * ROWS, ROWS)
        at = pl.ds(start, ROWS)
        first = pl.multiple_of(lax.rem(start, count), ROWS)
        valid = limits[pl.ds(first, ROWS), :1] > lax.div(start, count)
        z = norm_two[at, :] + bias_two
        cent = z - jnp.sum(z, axis=1, keepdims=True) * inv
        var = jnp.sum(cent * cent, axis=1, keepdims=True) * inv
        rstd = lax.rsqrt(var + 1e-05)
        normed = cent * rstd
        act = normed * gain_b + shift_b
        cdf, pdf = gelu_parts(act)
        dact = jnp.where(valid, cot_ref[at, :].astype(F32) * (cdf + act * pdf), 0.0)
        dnorm = dact * gain_b
        mean_a = jnp.sum(dnorm, axis=1, keepdims=True) * inv
        mean_b = jnp.sum(dnorm * normed, axis=1, keepdims=True) * inv
        dz = rstd * (dnorm - mean_a - normed * mean_b)
        dz_two[pl.ds(pl.multiple_of(start + count, ROWS), ROWS), :] = dz.astype(BF16)
        return (
            sums[0] + eighth(dz),
            sums[1] + eighth(dact * normed),
            sums[2] + eighth(dact),
        )

    zero = jnp.zeros((8, width), F32)
    sums_two = lax.fori_loop(
        0, steps_two, middle, (zero, zero, zero), unroll=together(steps_two)
    )

    dz_own = dz_two[count : count + rows_two, :]
    for tap, rows in enumerate(windows):
        grad[tap * width : (tap + 1) * width, :] = lax.dot_general(
            hidden[rows, :], dz_own, (((0,), (0,)), ((), ())), preferred_element_type=F32
        )
    share = grad.shape[0] // shares
    me = place_ref[0]
    parts = (keep_near, keep_far, send_near, send_far)
    quarter = shares // 4
    for spot in range(shares):
        flips = [
            sum(1 << bit for i, bit in enumerate(reversed(bit_order(shares, c))) if spot >> i & 1)
            for c in ((0, 1) if spot < shares // 2 else (1, 0))
        ]
        flip = flips[0] + (me & 1) * (flips[1] - flips[0])
        block = grad[pl.ds(pl.multiple_of((me ^ flip) * share, 8), share), :]
        part = parts[spot // quarter]
        at = spot % quarter * share
        part[at : at + share, :] = block.astype(part.dtype)

    turn = (((1,), (1,)), ((), ()))
    dz_one[rows_even:, :] = lax.dot_general(
        dz_own, conv_two_ref[width : 2 * width, :], turn, preferred_element_type=F32
    )
    dz_one[:rows_even, :] = lax.dot_general(
        dz_two[count:, :], conv_two_ref[:width, :], turn, preferred_element_type=F32
    ) + lax.dot_general(
        dz_two[:rows_even, :], conv_two_ref[2 * width :, :], turn, preferred_element_type=F32
    )

    def backward(step, sums):
        at = pl.ds(pl.multiple_of(step * ROWS, ROWS), ROWS)
        normed = norm_one[at, :]
        dact = dz_one[at, :] * slope_one[at, :]
        dnorm = dact * gain
        mean_a = jnp.sum(dnorm, axis=1, keepdims=True) * inv
        mean_b = jnp.sum(dnorm * normed, axis=1, keepdims=True) * inv
        dz = rstd_one[at, :1] * (dnorm - mean_a - normed * mean_b)
        hidden[at, :] = dz.astype(BF16)
        return (
            sums[0] + eighth(dz),
            sums[1] + eighth(dact * normed),
            sums[2] + eighth(dact),
        )

    sums_one = lax.fori_loop(
        0, steps_one, backward, (zero, zero, zero), unroll=together(steps_one)
    )
    first = lax.dot_general(
        taps[...], hidden[...], (((0,), (0,)), ((), ())), preferred_element_type=F32
    )
    small_ref[:TAPS, :] = first[:TAPS, :]
    for spot, sums in enumerate(sums_one + sums_two):
        small_ref[TAPS + spot : TAPS + spot + 1, :] = jnp.sum(sums, axis=0, keepdims=True)


def local_pass(record, shares, place, got, cot, weight, conv_two, table):
    count = got.shape[0]
    rows_two, width = cot.shape
    rows_one = 2 * rows_two + count
    quarter = 3 * width // 4
    vmem = pl.BlockSpec(memory_space=pltpu.VMEM)
    return pl.pallas_call(
        functools.partial(local_kernel, record, shares),
        out_shape=(
            jax.ShapeDtypeStruct((quarter, width), BF16),
            jax.ShapeDtypeStruct((quarter, width), BF16),
            jax.ShapeDtypeStruct((quarter, width), F32),
            jax.ShapeDtypeStruct((quarter, width), F32),
            jax.ShapeDtypeStruct((ROWS, width), F32),
        ),
        in_specs=[pl.BlockSpec(memory_space=pltpu.SMEM)] + [vmem] * 5,
        out_specs=(vmem,) * 5,
        scratch_shapes=[
            pltpu.VMEM((rows_one, 128), BF16),
            pltpu.VMEM((count, 128), jnp.int32),
            pltpu.VMEM((rows_one, width), F32),
            pltpu.VMEM((rows_one, width), F32),
            pltpu.VMEM((rows_one, width), F32),
            pltpu.VMEM((rows_one, 128), F32),
            pltpu.VMEM((rows_one, width), BF16),
            pltpu.VMEM((rows_two, width), F32),
            pltpu.VMEM((rows_two + 2 * count, width), BF16),
            pltpu.VMEM((rows_one, width), F32),
            pltpu.VMEM((3 * width, width), F32),
        ],
        cost_estimate=pl.CostEstimate(
            flops=2 * 9 * rows_two * width * width,
            bytes_accessed=8 * rows_one * width,
            transcendentals=3 * rows_one * width,
        ),
        compiler_params=pltpu.CompilerParams(vmem_limit_bytes=36 * 1024 * 1024),
    )(place, got, cot, weight, conv_two, table)


def exchange(sizes, stage, message):
    far = {axis: 0 for axis in sizes}
    for axis, bit in stage:
        far[axis] ^= 1 << bit
    axes = tuple(axis for axis in sizes if far[axis])
    pairs = [(0, 0)]
    for axis in axes:
        n = sizes[axis]
        pairs = [(a * n + i, b * n + (i ^ far[axis])) for a, b in pairs for i in range(n)]
    return lax.ppermute(message, axes if len(axes) > 1 else axes[0], pairs)


def exchange_crossed(sizes, turn, message):
    pairs = [(i, i ^ (1 << bit_order(sizes["dp"], i & 1)[2 + turn])) for i in range(sizes["dp"])]
    return lax.ppermute(message, "dp", pairs)


def message(rows, small):
    return jnp.concatenate([rows.astype(BF16), *split_two(small)], axis=0)


def contents(got):
    rows = got.shape[0] - 2 * ROWS
    hi, lo = got[rows : rows + ROWS], got[rows + ROWS :]
    return got[:rows].astype(F32), hi.astype(F32) + lo.astype(F32)


def finish_kernel(own_first, own_second, got_first, got_second, rows_ref, small_ref):
    cut = own_first.shape[0]
    own, small = contents(own_second[...])
    got, more = contents(got_second[...])
    rows_ref[:cut, :] = own_first[...].astype(F32) + got_first[...].astype(F32)
    rows_ref[cut:, :] = own + got
    small_ref[...] = small + more


def finish(*parts):
    rows, width = parts[0].shape[0] + parts[1].shape[0] - 2 * ROWS, parts[0].shape[1]
    vmem = pl.BlockSpec(memory_space=pltpu.VMEM)
    return pl.pallas_call(
        finish_kernel,
        out_shape=(
            jax.ShapeDtypeStruct((rows, width), F32),
            jax.ShapeDtypeStruct((ROWS, width), F32),
        ),
        in_specs=[vmem] * 4,
        out_specs=(pl.BlockSpec(), pl.BlockSpec()),
        compiler_params=pltpu.CompilerParams(vmem_limit_bytes=8 * 1024 * 1024),
    )(*parts)


def sum_all(sizes, send_far, send_near, keep_far, keep_near, small):
    bits = [("dp", bit) for bit in bit_order(sizes["dp"], 0)]
    core, onward, left = bits[0], bits[1], bits[4:]
    far = keep_far + exchange(sizes, [core], send_far).astype(F32)
    small = small + exchange(sizes, [core], small)
    near = keep_near + exchange(sizes, [core], send_near).astype(F32)

    half = far.shape[0] // 2
    far = far[:half] + exchange_crossed(sizes, 0, far[half:].astype(BF16)).astype(F32)
    own = message(near[half:], small)
    got, other = contents(exchange_crossed(sizes, 0, own))
    near, small = near[:half] + got, contents(own)[1]
    half = half // 2
    away = far[:half] + exchange_crossed(sizes, 1, far[half:].astype(BF16)).astype(F32)
    own = jnp.concatenate([message(near[half:], small), *split_two(other)], axis=0)
    own = exchange_crossed(sizes, 1, own)
    got, more = contents(own[:-2 * ROWS])
    base = near[:half] + got
    last = contents(own[-2 * ROWS :])[1]
    even = (lax.axis_index("dp") & 1) == 0
    small = (small + jnp.where(even, other, more)) + (jnp.where(even, more, other) + last)
    cut = (away.shape[0] + 2 * ROWS) // 2 // ROWS * ROWS
    own = message(away[cut:], small)
    first = exchange(sizes, [onward], away[:cut].astype(BF16))
    second, more = contents(exchange(sizes, [onward], own))
    first = base[:cut] + first.astype(F32)
    second, small = base[cut:] + second, contents(own)[1] + more
    for bit in left:
        total = jnp.concatenate([first, second], axis=0)
        half = total.shape[0] // 2
        own = message(total[half:], small)
        got, more = contents(exchange(sizes, [bit], own))
        total, small = total[:half] + got, contents(own)[1] + more
        cut = own.shape[0] // 2 // ROWS * ROWS
        first, second = total[:cut], total[cut:]
    bits = sizes["blk"].bit_length() - 1
    for bit in range(bits):
        own = first.astype(BF16), message(second, small)
        got = [exchange(sizes, [("blk", bit)], part) for part in own]
        if bit == bits - 1:
            return finish(*own, *got)
        first = own[0].astype(F32) + got[0].astype(F32)
        (second, small), (more, extra) = contents(own[1]), contents(got[1])
        second, small = second + more, small + extra
    return jnp.concatenate([first, second], axis=0), small


def per_device(
    sizes,
    waveform,
    length_bin,
    packing,
    cotangent,
    conv_one,
    bias_one,
    gain_one,
    shift_one,
    conv_two,
    bias_two,
    gain_two,
    shift_two,
):
    record = waveform.shape[1]
    count, frames_two, width = cotangent.shape
    shares = sizes["dp"]
    packed = pack(packing, length_bin, waveform)
    got = lax.all_to_all(packed, "dp", split_axis=0, concat_axis=0, tiled=True)
    vectors = (bias_one, gain_one, shift_one, bias_two, gain_two, shift_two)
    table = jnp.concatenate([conv_one.astype(F32), jnp.stack(vectors)], axis=0)
    cot = cotangent.reshape(count * frames_two, width)
    cot, weight = ready(count, cot, table, conv_two)
    place = lax.axis_index("dp").astype(jnp.int32).reshape(1)
    partial = local_pass(record, shares, place, got, cot, weight, conv_two, table)
    return sum_all(sizes, *partial)


def solution(mesh):
    sizes = {axis: mesh.shape[axis] for axis in ("dp", "blk")}
    both = ("dp", "blk")
    return jax.shard_map(
        functools.partial(per_device, sizes),
        mesh=mesh,
        in_specs=(P(both, None), P(both), P(both, None), P(both, None, None)) + (P(),) * 8,
        out_specs=(P("dp", None), P()),
        check_vma=False,
    )
```

```python
import functools
import math

import jax
import jax.numpy as jnp
from jax import lax
from jax.experimental import pallas as pl
from jax.experimental.pallas import tpu as pltpu
from jax.sharding import PartitionSpec as P

NB = 4
TAPS = 10
STRIDE = 5
ROWS = 16
F32 = jnp.float32
BF16 = jnp.bfloat16


def gelu_parts(act):
    cdf = 0.5 + 0.5 * lax.erf(act * 0.7071067811865476)
    return cdf, 0.3989422804014327 * jnp.exp(-0.5 * (act * act))


def pack_kernel(packing, bins, wave_ref, out_ref, wide):
    count, record = wave_ref.shape
    width = wide.shape[1]
    wide[...] = jnp.zeros_like(wide)
    wide[:, :record] = wave_ref[...].astype(F32)
    lane = lax.broadcasted_iota(jnp.int32, (1, width), 1)
    for slot in range(count):
        own = packing[0, slot]
        row = wide[pl.ds(own, 1), :]
        out_ref[slot] = jnp.where(lane == record, bins[own].astype(F32), row)


def pack(packing, length_bin, waveform):
    count, record = waveform.shape
    width = -(-(record + 1) // 128) * 128
    return pl.pallas_call(
        pack_kernel,
        out_shape=jax.ShapeDtypeStruct((count, 1, width), F32),
        in_specs=[
            pl.BlockSpec(memory_space=pltpu.SMEM),
            pl.BlockSpec(memory_space=pltpu.SMEM),
            pl.BlockSpec(memory_space=pltpu.VMEM),
        ],
        out_specs=pl.BlockSpec(memory_space=pltpu.VMEM),
        scratch_shapes=[pltpu.VMEM((count, width), F32)],
    )(packing, length_bin, waveform)


def ready_kernel(count, cot_ref, table_ref, conv_two_ref, moved_ref, weight_ref, weight):
    rows_two, width = cot_ref.shape
    frames_two = rows_two // count
    inv = 1.0 / width
    row = lax.broadcasted_iota(jnp.int32, (rows_two, 1), 0)
    origin = (row % count) * frames_two + row // count
    mover = (lax.broadcasted_iota(jnp.int32, (rows_two, rows_two), 1) == origin).astype(BF16)
    moved_ref[...] = jnp.dot(mover, cot_ref[...], preferred_element_type=F32).astype(BF16)
    weight[...] = jnp.zeros_like(weight)
    kernel = table_ref[:TAPS, :]
    kernel = kernel - jnp.sum(kernel, axis=1, keepdims=True) * inv
    bias = table_ref[TAPS : TAPS + 1, :]
    bias = bias - jnp.sum(bias, axis=1, keepdims=True) * inv
    for part in range(3):
        piece = kernel.astype(BF16).astype(F32)
        weight[part * ROWS : part * ROWS + TAPS, :] = piece
        kernel = kernel - piece
        piece = bias.astype(BF16).astype(F32)
        weight[3 * ROWS + part : 3 * ROWS + part + 1, :] = piece
        bias = bias - piece
    weight_ref[...] = weight[...].astype(BF16)


def ready(count, cot, table, conv_two):
    rows_two, width = cot.shape
    vmem = pl.BlockSpec(memory_space=pltpu.VMEM)
    return pl.pallas_call(
        functools.partial(ready_kernel, count),
        out_shape=(
            jax.ShapeDtypeStruct(cot.shape, BF16),
            jax.ShapeDtypeStruct((128, width), BF16),
        ),
        in_specs=[vmem, vmem, vmem],
        out_specs=(vmem, vmem),
        scratch_shapes=[pltpu.VMEM((128, width), F32)],
        cost_estimate=pl.CostEstimate(
            flops=2 * rows_two * rows_two * width,
            bytes_accessed=4 * cot.size,
            transcendentals=0,
        ),
        compiler_params=pltpu.CompilerParams(vmem_limit_bytes=16 * 1024 * 1024),
    )(cot, table, conv_two)


def together(steps):
    return max(n for n in range(1, 66) if steps % n == 0)


def bit_order(shares):
    bits = shares.bit_length() - 1
    return [0, 3, 1, 2, *range(4, bits)]


def local_kernel(
    record,
    shares,
    place_ref,
    got_ref,
    cot_ref,
    weight_ref,
    conv_two_ref,
    table_ref,
    send_far,
    send_near,
    keep_far,
    keep_near,
    small_ref,
    taps,
    limits,
    cent_one,
    norm_one,
    slope_one,
    rstd_one,
    hidden,
    norm_two,
    dz_two,
    dz_one,
    grad,
):
    count = got_ref.shape[0]
    rows_two, width = cot_ref.shape
    frames_two = rows_two // count
    frames_one = 2 * frames_two + 1
    rows_even = rows_two + count
    rows_one = frames_one * count
    inv = 1.0 / width

    wave = jnp.concatenate([got_ref[slot] for slot in range(count)], axis=0)
    lane_in = lax.broadcasted_iota(jnp.int32, wave.shape, 1)
    bins = jnp.sum(jnp.where(lane_in == record, wave, 0.0), axis=1, keepdims=True)
    limit = bins.astype(jnp.int32) * frames_two // NB
    limits[...] = jnp.broadcast_to(limit, (count, 128))
    wave = jnp.concatenate([wave, jnp.zeros((count, 128), F32)], axis=1)

    for place, frame in enumerate(
        list(range(0, frames_one, 2)) + list(range(1, frames_one, 2))
    ):
        taps[count * place : count * (place + 1), :] = wave[
            :, STRIDE * frame : STRIDE * frame + 128
        ].astype(BF16)
    src = lax.broadcasted_iota(jnp.int32, (128, 128), 0)
    dst = lax.broadcasted_iota(jnp.int32, (128, 128), 1)
    thrice = ((src < TAPS) & (dst < 3 * ROWS) & (dst % ROWS == src)).astype(BF16)
    lane = lax.broadcasted_iota(jnp.int32, (1, 128), 1)
    ones = ((lane >= 3 * ROWS) & (lane < 3 * ROWS + 3)).astype(F32)
    taps[...] = (jnp.dot(taps[...], thrice, preferred_element_type=F32) + ones).astype(BF16)

    cent_one[...] = jnp.dot(taps[...], weight_ref[...], preferred_element_type=F32)
    gain = table_ref[TAPS + 1 : TAPS + 2, :]
    shift = table_ref[TAPS + 2 : TAPS + 3, :]
    steps_one = rows_one // ROWS
    steps_two = rows_two // ROWS

    def forward(step, _):
        at = pl.ds(pl.multiple_of(step * ROWS, ROWS), ROWS)
        cent = cent_one[at, :]
        var = jnp.sum(cent * cent, axis=1, keepdims=True) * inv
        rstd = lax.rsqrt(var + 1e-05)
        normed = cent * rstd
        act = normed * gain + shift
        cdf, pdf = gelu_parts(act)
        norm_one[at, :] = normed
        rstd_one[at, :] = jnp.broadcast_to(rstd, (ROWS, 128))
        slope_one[at, :] = cdf + act * pdf
        hidden[at, :] = (act * cdf).astype(BF16)
        return 0

    lax.fori_loop(0, steps_one, forward, 0, unroll=together(steps_one))

    windows = (
        slice(0, rows_two),
        slice(rows_even, rows_even + rows_two),
        slice(count, rows_even),
    )
    total = None
    for tap, rows in enumerate(windows):
        term = jnp.dot(
            hidden[rows, :],
            conv_two_ref[tap * width : (tap + 1) * width, :],
            preferred_element_type=F32,
        )
        total = term if total is None else total + term
    norm_two[...] = total

    bias_two = table_ref[TAPS + 3 : TAPS + 4, :]
    gain_b = table_ref[TAPS + 4 : TAPS + 5, :]
    shift_b = table_ref[TAPS + 5 : TAPS + 6, :]
    dz_two[:count, :] = jnp.zeros((count, width), BF16)
    dz_two[count + rows_two :, :] = jnp.zeros((count, width), BF16)

    def eighth(x):
        return x[:8] + x[8:]

    def middle(step, sums):
        start = pl.multiple_of(step * ROWS, ROWS)
        at = pl.ds(start, ROWS)
        first = pl.multiple_of(lax.rem(start, count), ROWS)
        valid = limits[pl.ds(first, ROWS), :1] > lax.div(start, count)
        z = norm_two[at, :] + bias_two
        cent = z - jnp.sum(z, axis=1, keepdims=True) * inv
        var = jnp.sum(cent * cent, axis=1, keepdims=True) * inv
        rstd = lax.rsqrt(var + 1e-05)
        normed = cent * rstd
        act = normed * gain_b + shift_b
        cdf, pdf = gelu_parts(act)
        dact = jnp.where(valid, cot_ref[at, :].astype(F32) * (cdf + act * pdf), 0.0)
        dnorm = dact * gain_b
        mean_a = jnp.sum(dnorm, axis=1, keepdims=True) * inv
        mean_b = jnp.sum(dnorm * normed, axis=1, keepdims=True) * inv
        dz = rstd * (dnorm - mean_a - normed * mean_b)
        dz_two[pl.ds(pl.multiple_of(start + count, ROWS), ROWS), :] = dz.astype(BF16)
        return (
            sums[0] + eighth(dz),
            sums[1] + eighth(dact * normed),
            sums[2] + eighth(dact),
        )

    zero = jnp.zeros((8, width), F32)
    sums_two = lax.fori_loop(
        0, steps_two, middle, (zero, zero, zero), unroll=together(steps_two)
    )

    dz_own = dz_two[count : count + rows_two, :]
    for tap, rows in enumerate(windows):
        grad[tap * width : (tap + 1) * width, :] = lax.dot_general(
            hidden[rows, :], dz_own, (((0,), (0,)), ((), ())), preferred_element_type=F32
        )
    share = grad.shape[0] // shares
    me = place_ref[0]
    order = bit_order(shares)
    parts = (keep_near, keep_far, send_near, send_far)
    quarter = shares // 4
    for spot in range(shares):
        flip = sum(1 << bit for i, bit in enumerate(reversed(order)) if spot >> i & 1)
        block = grad[pl.ds(pl.multiple_of((me ^ flip) * share, 8), share), :]
        part = parts[spot // quarter]
        at = spot % quarter * share
        part[at : at + share, :] = block.astype(part.dtype)

    turn = (((1,), (1,)), ((), ()))
    dz_one[rows_even:, :] = lax.dot_general(
        dz_own, conv_two_ref[width : 2 * width, :], turn, preferred_element_type=F32
    )
    dz_one[:rows_even, :] = lax.dot_general(
        dz_two[count:, :], conv_two_ref[:width, :], turn, preferred_element_type=F32
    ) + lax.dot_general(
        dz_two[:rows_even, :], conv_two_ref[2 * width :, :], turn, preferred_element_type=F32
    )

    def backward(step, sums):
        at = pl.ds(pl.multiple_of(step * ROWS, ROWS), ROWS)
        normed = norm_one[at, :]
        dact = dz_one[at, :] * slope_one[at, :]
        dnorm = dact * gain
        mean_a = jnp.sum(dnorm, axis=1, keepdims=True) * inv
        mean_b = jnp.sum(dnorm * normed, axis=1, keepdims=True) * inv
        dz = rstd_one[at, :1] * (dnorm - mean_a - normed * mean_b)
        hidden[at, :] = dz.astype(BF16)
        return (
            sums[0] + eighth(dz),
            sums[1] + eighth(dact * normed),
            sums[2] + eighth(dact),
        )

    sums_one = lax.fori_loop(
        0, steps_one, backward, (zero, zero, zero), unroll=together(steps_one)
    )
    first = lax.dot_general(
        taps[...], hidden[...], (((0,), (0,)), ((), ())), preferred_element_type=F32
    )
    small_ref[:TAPS, :] = first[:TAPS, :]
    for spot, sums in enumerate(sums_one + sums_two):
        small_ref[TAPS + spot : TAPS + spot + 1, :] = jnp.sum(sums, axis=0, keepdims=True)


def local_pass(record, shares, place, got, cot, weight, conv_two, table):
    count = got.shape[0]
    rows_two, width = cot.shape
    rows_one = 2 * rows_two + count
    quarter = 3 * width // 4
    vmem = pl.BlockSpec(memory_space=pltpu.VMEM)
    return pl.pallas_call(
        functools.partial(local_kernel, record, shares),
        out_shape=(
            jax.ShapeDtypeStruct((quarter, width), BF16),
            jax.ShapeDtypeStruct((quarter, width), BF16),
            jax.ShapeDtypeStruct((quarter, width), F32),
            jax.ShapeDtypeStruct((quarter, width), F32),
            jax.ShapeDtypeStruct((ROWS, width), F32),
        ),
        in_specs=[pl.BlockSpec(memory_space=pltpu.SMEM)] + [vmem] * 5,
        out_specs=(vmem,) * 5,
        scratch_shapes=[
            pltpu.VMEM((rows_one, 128), BF16),
            pltpu.VMEM((count, 128), jnp.int32),
            pltpu.VMEM((rows_one, width), F32),
            pltpu.VMEM((rows_one, width), F32),
            pltpu.VMEM((rows_one, width), F32),
            pltpu.VMEM((rows_one, 128), F32),
            pltpu.VMEM((rows_one, width), BF16),
            pltpu.VMEM((rows_two, width), F32),
            pltpu.VMEM((rows_two + 2 * count, width), BF16),
            pltpu.VMEM((rows_one, width), F32),
            pltpu.VMEM((3 * width, width), F32),
        ],
        cost_estimate=pl.CostEstimate(
            flops=2 * 9 * rows_two * width * width,
            bytes_accessed=8 * rows_one * width,
            transcendentals=3 * rows_one * width,
        ),
        compiler_params=pltpu.CompilerParams(vmem_limit_bytes=36 * 1024 * 1024),
    )(place, got, cot, weight, conv_two, table)


def tree(terms):
    while len(terms) > 1:
        terms = [terms[i] + terms[i + 1] for i in range(0, len(terms), 2)]
    return terms[0]


def exchange(sizes, stage, message):
    far = {axis: 0 for axis in sizes}
    for axis, bit in stage:
        far[axis] ^= 1 << bit
    axes = tuple(axis for axis in sizes if far[axis])
    pairs = [(0, 0)]
    for axis in axes:
        n = sizes[axis]
        pairs = [(a * n + i, b * n + (i ^ far[axis])) for a, b in pairs for i in range(n)]
    return lax.ppermute(message, axes if len(axes) > 1 else axes[0], pairs)


def rounded(x):
    return lax.reduce_precision(x, exponent_bits=8, mantissa_bits=7)


def message(rows, small):
    return jnp.concatenate([rows.astype(BF16), small.astype(BF16)], axis=0)


def contents(got):
    rows = got.shape[0] - ROWS
    return got[:rows].astype(F32), got[rows:].astype(F32)


def near_kernel(own_ref, *refs):
    terms = [own_ref[...]] + [ref[...].astype(F32) for ref in refs[:-1]]
    refs[-1][...] = tree(terms)


def near_sum(own, *got):
    vmem = pl.BlockSpec(memory_space=pltpu.VMEM)
    return pl.pallas_call(
        near_kernel,
        out_shape=jax.ShapeDtypeStruct(own.shape, F32),
        in_specs=[vmem] * (1 + len(got)),
        out_specs=vmem,
        cost_estimate=pl.CostEstimate(
            flops=4 * own.size, bytes_accessed=140 * own.size, transcendentals=0
        ),
        compiler_params=pltpu.CompilerParams(vmem_limit_bytes=8 * 1024 * 1024),
    )(own, *got)


def finish_kernel(own_first, own_second, got_first, got_second, rows_ref, small_ref):
    cut = own_first.shape[0]
    own, small = contents(own_second[...])
    got, more = contents(got_second[...])
    rows_ref[:cut, :] = own_first[...].astype(F32) + got_first[...].astype(F32)
    rows_ref[cut:, :] = own + got
    small_ref[...] = small + more


def finish(*parts):
    rows, width = parts[0].shape[0] + parts[1].shape[0] - ROWS, parts[0].shape[1]
    vmem = pl.BlockSpec(memory_space=pltpu.VMEM)
    return pl.pallas_call(
        finish_kernel,
        out_shape=(
            jax.ShapeDtypeStruct((rows, width), F32),
            jax.ShapeDtypeStruct((ROWS, width), F32),
        ),
        in_specs=[vmem] * 4,
        out_specs=(pl.BlockSpec(), pl.BlockSpec()),
        compiler_params=pltpu.CompilerParams(vmem_limit_bytes=8 * 1024 * 1024),
    )(*parts)


def sum_all(sizes, send_far, send_near, keep_far, keep_near, small):
    order = [("dp", bit) for bit in bit_order(sizes["dp"])]
    core, onward, pair, left = order[0], order[1], order[2:4], order[4:]
    small = rounded(small + exchange(sizes, [core], small))
    far = keep_far + exchange(sizes, [core], send_far).astype(F32)
    near = keep_near + exchange(sizes, [core], send_near).astype(F32)
    rows = far.shape[0] // 4
    near, far = ([part[i * rows : (i + 1) * rows] for i in range(4)] for part in (near, far))
    fars, smalls, nears = [far[0]], [small], []
    chosen = [[bit for i, bit in enumerate(pair) if code >> (1 - i) & 1] for code in range(4)]
    for code in (1, 2, 3):
        got, more = contents(exchange(sizes, chosen[code], message(far[code], small)))
        fars.append(got)
        smalls.append(more)
    small = rounded(tree(smalls))
    own = message(tree(fars), small)
    for code in (1, 2, 3):
        nears.append(exchange(sizes, chosen[code], near[code].astype(BF16)))
    cut = own.shape[0] // 2 // ROWS * ROWS
    first, second = (exchange(sizes, [onward], part) for part in (own[:cut], own[cut:]))
    base = near_sum(near[0], *nears)
    first = base[:cut] + first.astype(F32)
    second, more = contents(second)
    second, small = base[cut:] + second, small + more
    for bit in left:
        total = jnp.concatenate([first, second], axis=0)
        half = total.shape[0] // 2
        small = rounded(small)
        own = message(total[half:], small)
        got, more = contents(exchange(sizes, [bit], own))
        total, small = total[:half] + got, small + more
        cut = own.shape[0] // 2 // ROWS * ROWS
        first, second = total[:cut], total[cut:]
    bits = sizes["blk"].bit_length() - 1
    for bit in range(bits):
        first, second, small = rounded(first), rounded(second), rounded(small)
        own = first.astype(BF16), message(second, small)
        got = [exchange(sizes, [("blk", bit)], part) for part in own]
        if bit == bits - 1:
            return finish(*own, *got)
        more, extra = contents(got[1])
        first, second, small = first + got[0].astype(F32), second + more, small + extra
    return jnp.concatenate([first, second], axis=0), small


def per_device(
    sizes,
    waveform,
    length_bin,
    packing,
    cotangent,
    conv_one,
    bias_one,
    gain_one,
    shift_one,
    conv_two,
    bias_two,
    gain_two,
    shift_two,
):
    record = waveform.shape[1]
    count, frames_two, width = cotangent.shape
    shares = sizes["dp"]
    packed = pack(packing, length_bin, waveform)
    got = lax.all_to_all(packed, "dp", split_axis=0, concat_axis=0, tiled=True)
    vectors = (bias_one, gain_one, shift_one, bias_two, gain_two, shift_two)
    table = jnp.concatenate([conv_one.astype(F32), jnp.stack(vectors)], axis=0)
    cot = cotangent.reshape(count * frames_two, width)
    cot, weight = ready(count, cot, table, conv_two)
    place = lax.axis_index("dp").astype(jnp.int32).reshape(1)
    partial = local_pass(record, shares, place, got, cot, weight, conv_two, table)
    return sum_all(sizes, *partial)


def solution(mesh):
    sizes = {axis: mesh.shape[axis] for axis in ("dp", "blk")}
    both = ("dp", "blk")
    return jax.shard_map(
        functools.partial(per_device, sizes),
        mesh=mesh,
        in_specs=(P(both, None), P(both), P(both, None), P(both, None, None)) + (P(),) * 8,
        out_specs=(P("dp", None), P()),
        check_vma=False,
    )
```

```python
import functools
import math

import jax
import jax.numpy as jnp
from jax import lax
from jax.experimental import pallas as pl
from jax.experimental.pallas import tpu as pltpu
from jax.sharding import PartitionSpec as P

NB = 4
TAPS = 10
STRIDE = 5
ROWS = 16
F32 = jnp.float32
BF16 = jnp.bfloat16


def gelu_parts(act):
    cdf = 0.5 + 0.5 * lax.erf(act * 0.7071067811865476)
    return cdf, 0.3989422804014327 * jnp.exp(-0.5 * (act * act))


def pack_kernel(packing, bins, wave_ref, out_ref, wide):
    count, record = wave_ref.shape
    width = wide.shape[1]
    wide[...] = jnp.zeros_like(wide)
    wide[:, :record] = wave_ref[...].astype(F32)
    lane = lax.broadcasted_iota(jnp.int32, (1, width), 1)
    for slot in range(count):
        own = packing[0, slot]
        row = wide[pl.ds(own, 1), :]
        out_ref[slot] = jnp.where(lane == record, bins[own].astype(F32), row)


def pack(packing, length_bin, waveform):
    count, record = waveform.shape
    width = -(-(record + 1) // 128) * 128
    return pl.pallas_call(
        pack_kernel,
        out_shape=jax.ShapeDtypeStruct((count, 1, width), F32),
        in_specs=[
            pl.BlockSpec(memory_space=pltpu.SMEM),
            pl.BlockSpec(memory_space=pltpu.SMEM),
            pl.BlockSpec(memory_space=pltpu.VMEM),
        ],
        out_specs=pl.BlockSpec(memory_space=pltpu.VMEM),
        scratch_shapes=[pltpu.VMEM((count, width), F32)],
    )(packing, length_bin, waveform)


def ready_kernel(count, cot_ref, table_ref, conv_two_ref, moved_ref, weight_ref, weight):
    rows_two, width = cot_ref.shape
    frames_two = rows_two // count
    inv = 1.0 / width
    row = lax.broadcasted_iota(jnp.int32, (rows_two, 1), 0)
    origin = (row % count) * frames_two + row // count
    mover = (lax.broadcasted_iota(jnp.int32, (rows_two, rows_two), 1) == origin).astype(BF16)
    moved_ref[...] = jnp.dot(mover, cot_ref[...], preferred_element_type=F32).astype(BF16)
    weight[...] = jnp.zeros_like(weight)
    kernel = table_ref[:TAPS, :]
    kernel = kernel - jnp.sum(kernel, axis=1, keepdims=True) * inv
    bias = table_ref[TAPS : TAPS + 1, :]
    bias = bias - jnp.sum(bias, axis=1, keepdims=True) * inv
    for part in range(3):
        piece = kernel.astype(BF16).astype(F32)
        weight[part * ROWS : part * ROWS + TAPS, :] = piece
        kernel = kernel - piece
        piece = bias.astype(BF16).astype(F32)
        weight[3 * ROWS + part : 3 * ROWS + part + 1, :] = piece
        bias = bias - piece
    weight_ref[...] = weight[...].astype(BF16)


def ready(count, cot, table, conv_two):
    rows_two, width = cot.shape
    vmem = pl.BlockSpec(memory_space=pltpu.VMEM)
    return pl.pallas_call(
        functools.partial(ready_kernel, count),
        out_shape=(
            jax.ShapeDtypeStruct(cot.shape, BF16),
            jax.ShapeDtypeStruct((128, width), BF16),
        ),
        in_specs=[vmem, vmem, vmem],
        out_specs=(vmem, vmem),
        scratch_shapes=[pltpu.VMEM((128, width), F32)],
        cost_estimate=pl.CostEstimate(
            flops=2 * rows_two * rows_two * width,
            bytes_accessed=4 * cot.size,
            transcendentals=0,
        ),
        compiler_params=pltpu.CompilerParams(vmem_limit_bytes=16 * 1024 * 1024),
    )(cot, table, conv_two)


def together(steps):
    return max(n for n in range(1, 66) if steps % n == 0)


def bit_order(shares):
    bits = shares.bit_length() - 1
    return [0, 3, 1, 2, *range(4, bits)]


def local_kernel(
    record,
    shares,
    place_ref,
    got_ref,
    cot_ref,
    weight_ref,
    conv_two_ref,
    table_ref,
    send_ref,
    keep_ref,
    small_ref,
    taps,
    limits,
    cent_one,
    norm_one,
    slope_one,
    rstd_one,
    hidden,
    norm_two,
    dz_two,
    dz_one,
    grad,
):
    count = got_ref.shape[0]
    rows_two, width = cot_ref.shape
    frames_two = rows_two // count
    frames_one = 2 * frames_two + 1
    rows_even = rows_two + count
    rows_one = frames_one * count
    inv = 1.0 / width

    wave = jnp.concatenate([got_ref[slot] for slot in range(count)], axis=0)
    lane_in = lax.broadcasted_iota(jnp.int32, wave.shape, 1)
    bins = jnp.sum(jnp.where(lane_in == record, wave, 0.0), axis=1, keepdims=True)
    limit = bins.astype(jnp.int32) * frames_two // NB
    limits[...] = jnp.broadcast_to(limit, (count, 128))
    wave = jnp.concatenate([wave, jnp.zeros((count, 128), F32)], axis=1)

    for place, frame in enumerate(
        list(range(0, frames_one, 2)) + list(range(1, frames_one, 2))
    ):
        taps[count * place : count * (place + 1), :] = wave[
            :, STRIDE * frame : STRIDE * frame + 128
        ].astype(BF16)
    src = lax.broadcasted_iota(jnp.int32, (128, 128), 0)
    dst = lax.broadcasted_iota(jnp.int32, (128, 128), 1)
    thrice = ((src < TAPS) & (dst < 3 * ROWS) & (dst % ROWS == src)).astype(BF16)
    lane = lax.broadcasted_iota(jnp.int32, (1, 128), 1)
    ones = ((lane >= 3 * ROWS) & (lane < 3 * ROWS + 3)).astype(F32)
    taps[...] = (jnp.dot(taps[...], thrice, preferred_element_type=F32) + ones).astype(BF16)

    cent_one[...] = jnp.dot(taps[...], weight_ref[...], preferred_element_type=F32)
    gain = table_ref[TAPS + 1 : TAPS + 2, :]
    shift = table_ref[TAPS + 2 : TAPS + 3, :]
    steps_one = rows_one // ROWS
    steps_two = rows_two // ROWS

    def forward(step, _):
        at = pl.ds(pl.multiple_of(step * ROWS, ROWS), ROWS)
        cent = cent_one[at, :]
        var = jnp.sum(cent * cent, axis=1, keepdims=True) * inv
        rstd = lax.rsqrt(var + 1e-05)
        normed = cent * rstd
        act = normed * gain + shift
        cdf, pdf = gelu_parts(act)
        norm_one[at, :] = normed
        rstd_one[at, :] = jnp.broadcast_to(rstd, (ROWS, 128))
        slope_one[at, :] = cdf + act * pdf
        hidden[at, :] = (act * cdf).astype(BF16)
        return 0

    lax.fori_loop(0, steps_one, forward, 0, unroll=together(steps_one))

    windows = (
        slice(0, rows_two),
        slice(rows_even, rows_even + rows_two),
        slice(count, rows_even),
    )
    total = None
    for tap, rows in enumerate(windows):
        term = jnp.dot(
            hidden[rows, :],
            conv_two_ref[tap * width : (tap + 1) * width, :],
            preferred_element_type=F32,
        )
        total = term if total is None else total + term
    norm_two[...] = total

    bias_two = table_ref[TAPS + 3 : TAPS + 4, :]
    gain_b = table_ref[TAPS + 4 : TAPS + 5, :]
    shift_b = table_ref[TAPS + 5 : TAPS + 6, :]
    dz_two[:count, :] = jnp.zeros((count, width), BF16)
    dz_two[count + rows_two :, :] = jnp.zeros((count, width), BF16)

    def eighth(x):
        return x[:8] + x[8:]

    def middle(step, sums):
        start = pl.multiple_of(step * ROWS, ROWS)
        at = pl.ds(start, ROWS)
        first = pl.multiple_of(lax.rem(start, count), ROWS)
        valid = limits[pl.ds(first, ROWS), :1] > lax.div(start, count)
        z = norm_two[at, :] + bias_two
        cent = z - jnp.sum(z, axis=1, keepdims=True) * inv
        var = jnp.sum(cent * cent, axis=1, keepdims=True) * inv
        rstd = lax.rsqrt(var + 1e-05)
        normed = cent * rstd
        act = normed * gain_b + shift_b
        cdf, pdf = gelu_parts(act)
        dact = jnp.where(valid, cot_ref[at, :].astype(F32) * (cdf + act * pdf), 0.0)
        dnorm = dact * gain_b
        mean_a = jnp.sum(dnorm, axis=1, keepdims=True) * inv
        mean_b = jnp.sum(dnorm * normed, axis=1, keepdims=True) * inv
        dz = rstd * (dnorm - mean_a - normed * mean_b)
        dz_two[pl.ds(pl.multiple_of(start + count, ROWS), ROWS), :] = dz.astype(BF16)
        return (
            sums[0] + eighth(dz),
            sums[1] + eighth(dact * normed),
            sums[2] + eighth(dact),
        )

    zero = jnp.zeros((8, width), F32)
    sums_two = lax.fori_loop(
        0, steps_two, middle, (zero, zero, zero), unroll=together(steps_two)
    )

    dz_own = dz_two[count : count + rows_two, :]
    for tap, rows in enumerate(windows):
        grad[tap * width : (tap + 1) * width, :] = lax.dot_general(
            hidden[rows, :], dz_own, (((0,), (0,)), ((), ())), preferred_element_type=F32
        )
    share = grad.shape[0] // shares
    me = place_ref[0]
    order = bit_order(shares)
    half = shares // 2
    for spot in range(shares):
        flip = sum(1 << bit for i, bit in enumerate(reversed(order)) if spot >> i & 1)
        block = grad[pl.ds(pl.multiple_of((me ^ flip) * share, 8), share), :]
        part = send_ref if spot >= half else keep_ref
        at = spot % half * share
        part[at : at + share, :] = block.astype(part.dtype)

    turn = (((1,), (1,)), ((), ()))
    dz_one[rows_even:, :] = lax.dot_general(
        dz_own, conv_two_ref[width : 2 * width, :], turn, preferred_element_type=F32
    )
    dz_one[:rows_even, :] = lax.dot_general(
        dz_two[count:, :], conv_two_ref[:width, :], turn, preferred_element_type=F32
    ) + lax.dot_general(
        dz_two[:rows_even, :], conv_two_ref[2 * width :, :], turn, preferred_element_type=F32
    )

    def backward(step, sums):
        at = pl.ds(pl.multiple_of(step * ROWS, ROWS), ROWS)
        normed = norm_one[at, :]
        dact = dz_one[at, :] * slope_one[at, :]
        dnorm = dact * gain
        mean_a = jnp.sum(dnorm, axis=1, keepdims=True) * inv
        mean_b = jnp.sum(dnorm * normed, axis=1, keepdims=True) * inv
        dz = rstd_one[at, :1] * (dnorm - mean_a - normed * mean_b)
        hidden[at, :] = dz.astype(BF16)
        return (
            sums[0] + eighth(dz),
            sums[1] + eighth(dact * normed),
            sums[2] + eighth(dact),
        )

    sums_one = lax.fori_loop(
        0, steps_one, backward, (zero, zero, zero), unroll=together(steps_one)
    )
    first = lax.dot_general(
        taps[...], hidden[...], (((0,), (0,)), ((), ())), preferred_element_type=F32
    )
    small_ref[:TAPS, :] = first[:TAPS, :]
    for spot, sums in enumerate(sums_one + sums_two):
        small_ref[TAPS + spot : TAPS + spot + 1, :] = jnp.sum(sums, axis=0, keepdims=True)


def local_pass(record, shares, place, got, cot, weight, conv_two, table):
    count = got.shape[0]
    rows_two, width = cot.shape
    rows_one = 2 * rows_two + count
    half = 3 * width // 2
    vmem = pl.BlockSpec(memory_space=pltpu.VMEM)
    return pl.pallas_call(
        functools.partial(local_kernel, record, shares),
        out_shape=(
            jax.ShapeDtypeStruct((half, width), BF16),
            jax.ShapeDtypeStruct((half, width), F32),
            jax.ShapeDtypeStruct((ROWS, width), F32),
        ),
        in_specs=[pl.BlockSpec(memory_space=pltpu.SMEM)] + [vmem] * 5,
        out_specs=(vmem,) * 3,
        scratch_shapes=[
            pltpu.VMEM((rows_one, 128), BF16),
            pltpu.VMEM((count, 128), jnp.int32),
            pltpu.VMEM((rows_one, width), F32),
            pltpu.VMEM((rows_one, width), F32),
            pltpu.VMEM((rows_one, width), F32),
            pltpu.VMEM((rows_one, 128), F32),
            pltpu.VMEM((rows_one, width), BF16),
            pltpu.VMEM((rows_two, width), F32),
            pltpu.VMEM((rows_two + 2 * count, width), BF16),
            pltpu.VMEM((rows_one, width), F32),
            pltpu.VMEM((3 * width, width), F32),
        ],
        cost_estimate=pl.CostEstimate(
            flops=2 * 9 * rows_two * width * width,
            bytes_accessed=8 * rows_one * width,
            transcendentals=3 * rows_one * width,
        ),
        compiler_params=pltpu.CompilerParams(vmem_limit_bytes=36 * 1024 * 1024),
    )(place, got, cot, weight, conv_two, table)


def tree(terms):
    while len(terms) > 1:
        terms = [terms[i] + terms[i + 1] for i in range(0, len(terms), 2)]
    return terms[0]


def exchange(sizes, stage, message):
    far = {axis: 0 for axis in sizes}
    for axis, bit in stage:
        far[axis] ^= 1 << bit
    axes = tuple(axis for axis in sizes if far[axis])
    pairs = [(0, 0)]
    for axis in axes:
        n = sizes[axis]
        pairs = [(a * n + i, b * n + (i ^ far[axis])) for a, b in pairs for i in range(n)]
    return lax.ppermute(message, axes if len(axes) > 1 else axes[0], pairs)


def rounded(x):
    return lax.reduce_precision(x, exponent_bits=8, mantissa_bits=7)


def message(rows, small):
    return jnp.concatenate([rows.astype(BF16), small.astype(BF16)], axis=0)


def contents(got):
    rows = got.shape[0] - ROWS
    return got[:rows].astype(F32), got[rows:].astype(F32)


def near_kernel(own_ref, *refs):
    terms = [own_ref[...]] + [ref[...].astype(F32) for ref in refs[:-1]]
    refs[-1][...] = tree(terms)


def near_sum(own, *got):
    vmem = pl.BlockSpec(memory_space=pltpu.VMEM)
    return pl.pallas_call(
        near_kernel,
        out_shape=jax.ShapeDtypeStruct(own.shape, F32),
        in_specs=[vmem] * (1 + len(got)),
        out_specs=vmem,
        cost_estimate=pl.CostEstimate(
            flops=4 * own.size, bytes_accessed=140 * own.size, transcendentals=0
        ),
        compiler_params=pltpu.CompilerParams(vmem_limit_bytes=8 * 1024 * 1024),
    )(own, *got)


def finish_kernel(own_first, own_second, got_first, got_second, rows_ref, small_ref):
    cut = own_first.shape[0]
    own, small = contents(own_second[...])
    got, more = contents(got_second[...])
    rows_ref[:cut, :] = own_first[...].astype(F32) + got_first[...].astype(F32)
    rows_ref[cut:, :] = own + got
    small_ref[...] = small + more


def finish(*parts):
    rows, width = parts[0].shape[0] + parts[1].shape[0] - ROWS, parts[0].shape[1]
    vmem = pl.BlockSpec(memory_space=pltpu.VMEM)
    return pl.pallas_call(
        finish_kernel,
        out_shape=(
            jax.ShapeDtypeStruct((rows, width), F32),
            jax.ShapeDtypeStruct((ROWS, width), F32),
        ),
        in_specs=[vmem] * 4,
        out_specs=(pl.BlockSpec(), pl.BlockSpec()),
        compiler_params=pltpu.CompilerParams(vmem_limit_bytes=8 * 1024 * 1024),
    )(*parts)


def sum_all(sizes, send, keep, small):
    order = [("dp", bit) for bit in bit_order(sizes["dp"])]
    core, onward, pair, left = order[0], order[1], order[2:4], order[4:]
    small = rounded(small + exchange(sizes, [core], small))
    total = keep + exchange(sizes, [core], send).astype(F32)
    rows = total.shape[0] // 8
    near, far = ([total[i * rows : (i + 1) * rows] for i in range(j, j + 4)] for j in (0, 4))
    fars, smalls, nears = [far[0]], [small], []
    chosen = [[bit for i, bit in enumerate(pair) if code >> (1 - i) & 1] for code in range(4)]
    for code in (1, 2, 3):
        got, more = contents(exchange(sizes, chosen[code], message(far[code], small)))
        fars.append(got)
        smalls.append(more)
    small = rounded(tree(smalls))
    own = message(tree(fars), small)
    for code in (1, 2, 3):
        nears.append(exchange(sizes, chosen[code], near[code].astype(BF16)))
    cut = own.shape[0] // 2 // ROWS * ROWS
    first, second = (exchange(sizes, [onward], part) for part in (own[:cut], own[cut:]))
    base = near_sum(near[0], *nears)
    first = base[:cut] + first.astype(F32)
    second, more = contents(second)
    second, small = base[cut:] + second, small + more
    for bit in left:
        total = jnp.concatenate([first, second], axis=0)
        half = total.shape[0] // 2
        small = rounded(small)
        own = message(total[half:], small)
        got, more = contents(exchange(sizes, [bit], own))
        total, small = total[:half] + got, small + more
        cut = own.shape[0] // 2 // ROWS * ROWS
        first, second = total[:cut], total[cut:]
    bits = sizes["blk"].bit_length() - 1
    for bit in range(bits):
        first, second, small = rounded(first), rounded(second), rounded(small)
        own = first.astype(BF16), message(second, small)
        got = [exchange(sizes, [("blk", bit)], part) for part in own]
        if bit == bits - 1:
            return finish(*own, *got)
        more, extra = contents(got[1])
        first, second, small = first + got[0].astype(F32), second + more, small + extra
    return jnp.concatenate([first, second], axis=0), small


def per_device(
    sizes,
    waveform,
    length_bin,
    packing,
    cotangent,
    conv_one,
    bias_one,
    gain_one,
    shift_one,
    conv_two,
    bias_two,
    gain_two,
    shift_two,
):
    record = waveform.shape[1]
    count, frames_two, width = cotangent.shape
    shares = sizes["dp"]
    packed = pack(packing, length_bin, waveform)
    got = lax.all_to_all(packed, "dp", split_axis=0, concat_axis=0, tiled=True)
    vectors = (bias_one, gain_one, shift_one, bias_two, gain_two, shift_two)
    table = jnp.concatenate([conv_one.astype(F32), jnp.stack(vectors)], axis=0)
    cot = cotangent.reshape(count * frames_two, width)
    cot, weight = ready(count, cot, table, conv_two)
    place = lax.axis_index("dp").astype(jnp.int32).reshape(1)
    partial = local_pass(record, shares, place, got, cot, weight, conv_two, table)
    return sum_all(sizes, *partial)


def solution(mesh):
    sizes = {axis: mesh.shape[axis] for axis in ("dp", "blk")}
    both = ("dp", "blk")
    return jax.shard_map(
        functools.partial(per_device, sizes),
        mesh=mesh,
        in_specs=(P(both, None), P(both), P(both, None), P(both, None, None)) + (P(),) * 8,
        out_specs=(P("dp", None), P()),
        check_vma=False,
    )
```

```python
import functools
import math

import jax
import jax.numpy as jnp
from jax import lax
from jax.experimental import pallas as pl
from jax.experimental.pallas import tpu as pltpu
from jax.sharding import PartitionSpec as P

NB = 4
TAPS = 10
STRIDE = 5
ROWS = 16
F32 = jnp.float32
BF16 = jnp.bfloat16


def gelu_parts(act):
    cdf = 0.5 + 0.5 * lax.erf(act * 0.7071067811865476)
    return cdf, 0.3989422804014327 * jnp.exp(-0.5 * (act * act))


def pack_kernel(packing, bins, wave_ref, out_ref, wide):
    count, record = wave_ref.shape
    width = wide.shape[1]
    wide[...] = jnp.zeros_like(wide)
    wide[:, :record] = wave_ref[...].astype(F32)
    lane = lax.broadcasted_iota(jnp.int32, (1, width), 1)
    for slot in range(count):
        own = packing[0, slot]
        row = wide[pl.ds(own, 1), :]
        out_ref[slot] = jnp.where(lane == record, bins[own].astype(F32), row)


def pack(packing, length_bin, waveform):
    count, record = waveform.shape
    width = -(-(record + 1) // 128) * 128
    return pl.pallas_call(
        pack_kernel,
        out_shape=jax.ShapeDtypeStruct((count, 1, width), F32),
        in_specs=[
            pl.BlockSpec(memory_space=pltpu.SMEM),
            pl.BlockSpec(memory_space=pltpu.SMEM),
            pl.BlockSpec(memory_space=pltpu.VMEM),
        ],
        out_specs=pl.BlockSpec(memory_space=pltpu.VMEM),
        scratch_shapes=[pltpu.VMEM((count, width), F32)],
    )(packing, length_bin, waveform)


def ready_kernel(count, cot_ref, table_ref, conv_two_ref, moved_ref, weight_ref, weight):
    rows_two, width = cot_ref.shape
    frames_two = rows_two // count
    inv = 1.0 / width
    row = lax.broadcasted_iota(jnp.int32, (rows_two, 1), 0)
    origin = (row % count) * frames_two + row // count
    mover = (lax.broadcasted_iota(jnp.int32, (rows_two, rows_two), 1) == origin).astype(BF16)
    moved_ref[...] = jnp.dot(mover, cot_ref[...], preferred_element_type=F32).astype(BF16)
    weight[...] = jnp.zeros_like(weight)
    kernel = table_ref[:TAPS, :]
    kernel = kernel - jnp.sum(kernel, axis=1, keepdims=True) * inv
    bias = table_ref[TAPS : TAPS + 1, :]
    bias = bias - jnp.sum(bias, axis=1, keepdims=True) * inv
    for part in range(3):
        piece = kernel.astype(BF16).astype(F32)
        weight[part * ROWS : part * ROWS + TAPS, :] = piece
        kernel = kernel - piece
        piece = bias.astype(BF16).astype(F32)
        weight[3 * ROWS + part : 3 * ROWS + part + 1, :] = piece
        bias = bias - piece
    weight_ref[...] = weight[...].astype(BF16)


def ready(count, cot, table, conv_two):
    rows_two, width = cot.shape
    vmem = pl.BlockSpec(memory_space=pltpu.VMEM)
    return pl.pallas_call(
        functools.partial(ready_kernel, count),
        out_shape=(
            jax.ShapeDtypeStruct(cot.shape, BF16),
            jax.ShapeDtypeStruct((128, width), BF16),
        ),
        in_specs=[vmem, vmem, vmem],
        out_specs=(vmem, vmem),
        scratch_shapes=[pltpu.VMEM((128, width), F32)],
        cost_estimate=pl.CostEstimate(
            flops=2 * rows_two * rows_two * width,
            bytes_accessed=4 * cot.size,
            transcendentals=0,
        ),
        compiler_params=pltpu.CompilerParams(vmem_limit_bytes=16 * 1024 * 1024),
    )(cot, table, conv_two)


def together(steps):
    return max(n for n in range(1, 66) if steps % n == 0)


def bit_order(shares):
    bits = shares.bit_length() - 1
    return [0, 3, 1, 2, *range(4, bits)]


def local_kernel(
    record,
    shares,
    place_ref,
    got_ref,
    cot_ref,
    weight_ref,
    conv_two_ref,
    table_ref,
    send_ref,
    keep_ref,
    small_ref,
    taps,
    limits,
    cent_one,
    norm_one,
    slope_one,
    rstd_one,
    hidden,
    norm_two,
    dz_two,
    dz_one,
    grad,
):
    count = got_ref.shape[0]
    rows_two, width = cot_ref.shape
    frames_two = rows_two // count
    frames_one = 2 * frames_two + 1
    rows_even = rows_two + count
    rows_one = frames_one * count
    inv = 1.0 / width

    wave = jnp.concatenate([got_ref[slot] for slot in range(count)], axis=0)
    lane_in = lax.broadcasted_iota(jnp.int32, wave.shape, 1)
    bins = jnp.sum(jnp.where(lane_in == record, wave, 0.0), axis=1, keepdims=True)
    limit = bins.astype(jnp.int32) * frames_two // NB
    limits[...] = jnp.broadcast_to(limit, (count, 128))
    wave = jnp.concatenate([wave, jnp.zeros((count, 128), F32)], axis=1)

    for place, frame in enumerate(
        list(range(0, frames_one, 2)) + list(range(1, frames_one, 2))
    ):
        taps[count * place : count * (place + 1), :] = wave[
            :, STRIDE * frame : STRIDE * frame + 128
        ].astype(BF16)
    src = lax.broadcasted_iota(jnp.int32, (128, 128), 0)
    dst = lax.broadcasted_iota(jnp.int32, (128, 128), 1)
    thrice = ((src < TAPS) & (dst < 3 * ROWS) & (dst % ROWS == src)).astype(BF16)
    lane = lax.broadcasted_iota(jnp.int32, (1, 128), 1)
    ones = ((lane >= 3 * ROWS) & (lane < 3 * ROWS + 3)).astype(F32)
    taps[...] = (jnp.dot(taps[...], thrice, preferred_element_type=F32) + ones).astype(BF16)

    cent_one[...] = jnp.dot(taps[...], weight_ref[...], preferred_element_type=F32)
    gain = table_ref[TAPS + 1 : TAPS + 2, :]
    shift = table_ref[TAPS + 2 : TAPS + 3, :]
    steps_one = rows_one // ROWS
    steps_two = rows_two // ROWS

    def forward(step, _):
        at = pl.ds(pl.multiple_of(step * ROWS, ROWS), ROWS)
        cent = cent_one[at, :]
        var = jnp.sum(cent * cent, axis=1, keepdims=True) * inv
        rstd = lax.rsqrt(var + 1e-05)
        normed = cent * rstd
        act = normed * gain + shift
        cdf, pdf = gelu_parts(act)
        norm_one[at, :] = normed
        rstd_one[at, :] = jnp.broadcast_to(rstd, (ROWS, 128))
        slope_one[at, :] = cdf + act * pdf
        hidden[at, :] = (act * cdf).astype(BF16)
        return 0

    lax.fori_loop(0, steps_one, forward, 0, unroll=together(steps_one))

    windows = (
        slice(0, rows_two),
        slice(rows_even, rows_even + rows_two),
        slice(count, rows_even),
    )
    total = None
    for tap, rows in enumerate(windows):
        term = jnp.dot(
            hidden[rows, :],
            conv_two_ref[tap * width : (tap + 1) * width, :],
            preferred_element_type=F32,
        )
        total = term if total is None else total + term
    norm_two[...] = total

    bias_two = table_ref[TAPS + 3 : TAPS + 4, :]
    gain_b = table_ref[TAPS + 4 : TAPS + 5, :]
    shift_b = table_ref[TAPS + 5 : TAPS + 6, :]
    dz_two[:count, :] = jnp.zeros((count, width), BF16)
    dz_two[count + rows_two :, :] = jnp.zeros((count, width), BF16)

    def eighth(x):
        return x[:8] + x[8:]

    def middle(step, sums):
        start = pl.multiple_of(step * ROWS, ROWS)
        at = pl.ds(start, ROWS)
        first = pl.multiple_of(lax.rem(start, count), ROWS)
        valid = limits[pl.ds(first, ROWS), :1] > lax.div(start, count)
        z = norm_two[at, :] + bias_two
        cent = z - jnp.sum(z, axis=1, keepdims=True) * inv
        var = jnp.sum(cent * cent, axis=1, keepdims=True) * inv
        rstd = lax.rsqrt(var + 1e-05)
        normed = cent * rstd
        act = normed * gain_b + shift_b
        cdf, pdf = gelu_parts(act)
        dact = jnp.where(valid, cot_ref[at, :].astype(F32) * (cdf + act * pdf), 0.0)
        dnorm = dact * gain_b
        mean_a = jnp.sum(dnorm, axis=1, keepdims=True) * inv
        mean_b = jnp.sum(dnorm * normed, axis=1, keepdims=True) * inv
        dz = rstd * (dnorm - mean_a - normed * mean_b)
        dz_two[pl.ds(pl.multiple_of(start + count, ROWS), ROWS), :] = dz.astype(BF16)
        return (
            sums[0] + eighth(dz),
            sums[1] + eighth(dact * normed),
            sums[2] + eighth(dact),
        )

    zero = jnp.zeros((8, width), F32)
    sums_two = lax.fori_loop(
        0, steps_two, middle, (zero, zero, zero), unroll=together(steps_two)
    )

    dz_own = dz_two[count : count + rows_two, :]
    for tap, rows in enumerate(windows):
        grad[tap * width : (tap + 1) * width, :] = lax.dot_general(
            hidden[rows, :], dz_own, (((0,), (0,)), ((), ())), preferred_element_type=F32
        )
    share = grad.shape[0] // shares
    me = place_ref[0]
    order = bit_order(shares)
    half = shares // 2
    for spot in range(shares):
        flip = sum(1 << bit for i, bit in enumerate(reversed(order)) if spot >> i & 1)
        block = grad[pl.ds(pl.multiple_of((me ^ flip) * share, 8), share), :]
        part = send_ref if spot >= half else keep_ref
        at = spot % half * share
        part[at : at + share, :] = block.astype(part.dtype)

    turn = (((1,), (1,)), ((), ()))
    dz_one[rows_even:, :] = lax.dot_general(
        dz_own, conv_two_ref[width : 2 * width, :], turn, preferred_element_type=F32
    )
    dz_one[:rows_even, :] = lax.dot_general(
        dz_two[count:, :], conv_two_ref[:width, :], turn, preferred_element_type=F32
    ) + lax.dot_general(
        dz_two[:rows_even, :], conv_two_ref[2 * width :, :], turn, preferred_element_type=F32
    )

    def backward(step, sums):
        at = pl.ds(pl.multiple_of(step * ROWS, ROWS), ROWS)
        normed = norm_one[at, :]
        dact = dz_one[at, :] * slope_one[at, :]
        dnorm = dact * gain
        mean_a = jnp.sum(dnorm, axis=1, keepdims=True) * inv
        mean_b = jnp.sum(dnorm * normed, axis=1, keepdims=True) * inv
        dz = rstd_one[at, :1] * (dnorm - mean_a - normed * mean_b)
        hidden[at, :] = dz.astype(BF16)
        return (
            sums[0] + eighth(dz),
            sums[1] + eighth(dact * normed),
            sums[2] + eighth(dact),
        )

    sums_one = lax.fori_loop(
        0, steps_one, backward, (zero, zero, zero), unroll=together(steps_one)
    )
    first = lax.dot_general(
        taps[...], hidden[...], (((0,), (0,)), ((), ())), preferred_element_type=F32
    )
    small_ref[:TAPS, :] = first[:TAPS, :]
    for spot, sums in enumerate(sums_one + sums_two):
        small_ref[TAPS + spot : TAPS + spot + 1, :] = jnp.sum(sums, axis=0, keepdims=True)


def local_pass(record, shares, place, got, cot, weight, conv_two, table):
    count = got.shape[0]
    rows_two, width = cot.shape
    rows_one = 2 * rows_two + count
    half = 3 * width // 2
    vmem = pl.BlockSpec(memory_space=pltpu.VMEM)
    return pl.pallas_call(
        functools.partial(local_kernel, record, shares),
        out_shape=(
            jax.ShapeDtypeStruct((half, width), BF16),
            jax.ShapeDtypeStruct((half, width), F32),
            jax.ShapeDtypeStruct((ROWS, width), F32),
        ),
        in_specs=[pl.BlockSpec(memory_space=pltpu.SMEM)] + [vmem] * 5,
        out_specs=(vmem,) * 3,
        scratch_shapes=[
            pltpu.VMEM((rows_one, 128), BF16),
            pltpu.VMEM((count, 128), jnp.int32),
            pltpu.VMEM((rows_one, width), F32),
            pltpu.VMEM((rows_one, width), F32),
            pltpu.VMEM((rows_one, width), F32),
            pltpu.VMEM((rows_one, 128), F32),
            pltpu.VMEM((rows_one, width), BF16),
            pltpu.VMEM((rows_two, width), F32),
            pltpu.VMEM((rows_two + 2 * count, width), BF16),
            pltpu.VMEM((rows_one, width), F32),
            pltpu.VMEM((3 * width, width), F32),
        ],
        cost_estimate=pl.CostEstimate(
            flops=2 * 9 * rows_two * width * width,
            bytes_accessed=8 * rows_one * width,
            transcendentals=3 * rows_one * width,
        ),
        compiler_params=pltpu.CompilerParams(vmem_limit_bytes=36 * 1024 * 1024),
    )(place, got, cot, weight, conv_two, table)


def tree(terms):
    while len(terms) > 1:
        terms = [terms[i] + terms[i + 1] for i in range(0, len(terms), 2)]
    return terms[0]


def exchange(sizes, stage, message):
    far = {axis: 0 for axis in sizes}
    for axis, bit in stage:
        far[axis] ^= 1 << bit
    axes = tuple(axis for axis in sizes if far[axis])
    pairs = [(0, 0)]
    for axis in axes:
        n = sizes[axis]
        pairs = [(a * n + i, b * n + (i ^ far[axis])) for a, b in pairs for i in range(n)]
    return lax.ppermute(message, axes if len(axes) > 1 else axes[0], pairs)


def rounded(x):
    return lax.reduce_precision(x, exponent_bits=8, mantissa_bits=7)


def message(rows, small):
    return jnp.concatenate([rows.astype(BF16), small.astype(BF16)], axis=0)


def contents(got):
    rows = got.shape[0] - ROWS
    return got[:rows].astype(F32), got[rows:].astype(F32)


def near_kernel(own_ref, *refs):
    terms = [own_ref[...]] + [ref[...].astype(F32) for ref in refs[:-2]]
    total = tree(terms)
    cut = refs[-2].shape[0]
    refs[-2][...] = total[:cut]
    refs[-1][...] = total[cut:]


def near_sum(cut, own, *got):
    vmem = pl.BlockSpec(memory_space=pltpu.VMEM)
    return pl.pallas_call(
        near_kernel,
        out_shape=(
            jax.ShapeDtypeStruct((cut, own.shape[1]), F32),
            jax.ShapeDtypeStruct((own.shape[0] - cut, own.shape[1]), F32),
        ),
        in_specs=[vmem] * (1 + len(got)),
        out_specs=(vmem, vmem),
        cost_estimate=pl.CostEstimate(
            flops=4 * own.size, bytes_accessed=140 * own.size, transcendentals=0
        ),
        compiler_params=pltpu.CompilerParams(vmem_limit_bytes=8 * 1024 * 1024),
    )(own, *got)


def finish_kernel(own_first, own_second, got_first, got_second, rows_ref, small_ref):
    cut = own_first.shape[0]
    own, small = contents(own_second[...])
    got, more = contents(got_second[...])
    rows_ref[:cut, :] = own_first[...].astype(F32) + got_first[...].astype(F32)
    rows_ref[cut:, :] = own + got
    small_ref[...] = small + more


def finish(*parts):
    rows, width = parts[0].shape[0] + parts[1].shape[0] - ROWS, parts[0].shape[1]
    vmem = pl.BlockSpec(memory_space=pltpu.VMEM)
    return pl.pallas_call(
        finish_kernel,
        out_shape=(
            jax.ShapeDtypeStruct((rows, width), F32),
            jax.ShapeDtypeStruct((ROWS, width), F32),
        ),
        in_specs=[vmem] * 4,
        out_specs=(pl.BlockSpec(), pl.BlockSpec()),
        compiler_params=pltpu.CompilerParams(vmem_limit_bytes=8 * 1024 * 1024),
    )(*parts)


def sum_all(sizes, send, keep, small):
    order = [("dp", bit) for bit in bit_order(sizes["dp"])]
    core, onward, pair, left = order[0], order[1], order[2:4], order[4:]
    small = rounded(small + exchange(sizes, [core], small))
    total = keep + exchange(sizes, [core], send).astype(F32)
    rows = total.shape[0] // 8
    near, far = ([total[i * rows : (i + 1) * rows] for i in range(j, j + 4)] for j in (0, 4))
    fars, smalls, nears = [far[0]], [small], []
    chosen = [[bit for i, bit in enumerate(pair) if code >> (1 - i) & 1] for code in range(4)]
    for code in (1, 2, 3):
        got, more = contents(exchange(sizes, chosen[code], message(far[code], small)))
        fars.append(got)
        smalls.append(more)
    small = rounded(tree(smalls))
    own = message(tree(fars), small)
    for code in (1, 2, 3):
        nears.append(exchange(sizes, chosen[code], near[code].astype(BF16)))
    cut = own.shape[0] // 2 // ROWS * ROWS
    first, second = (exchange(sizes, [onward], part) for part in (own[:cut], own[cut:]))
    base = near_sum(cut, near[0], *nears)
    first = base[0] + first.astype(F32)
    second, more = contents(second)
    second, small = base[1] + second, small + more
    for bit in left:
        total = jnp.concatenate([first, second], axis=0)
        half = total.shape[0] // 2
        small = rounded(small)
        own = message(total[half:], small)
        got, more = contents(exchange(sizes, [bit], own))
        total, small = total[:half] + got, small + more
        cut = own.shape[0] // 2 // ROWS * ROWS
        first, second = total[:cut], total[cut:]
    bits = sizes["blk"].bit_length() - 1
    for bit in range(bits):
        first, second, small = rounded(first), rounded(second), rounded(small)
        own = first.astype(BF16), message(second, small)
        got = [exchange(sizes, [("blk", bit)], part) for part in own]
        if bit == bits - 1:
            return finish(*own, *got)
        more, extra = contents(got[1])
        first, second, small = first + got[0].astype(F32), second + more, small + extra
    return jnp.concatenate([first, second], axis=0), small


def per_device(
    sizes,
    waveform,
    length_bin,
    packing,
    cotangent,
    conv_one,
    bias_one,
    gain_one,
    shift_one,
    conv_two,
    bias_two,
    gain_two,
    shift_two,
):
    record = waveform.shape[1]
    count, frames_two, width = cotangent.shape
    shares = sizes["dp"]
    packed = pack(packing, length_bin, waveform)
    got = lax.all_to_all(packed, "dp", split_axis=0, concat_axis=0, tiled=True)
    vectors = (bias_one, gain_one, shift_one, bias_two, gain_two, shift_two)
    table = jnp.concatenate([conv_one.astype(F32), jnp.stack(vectors)], axis=0)
    cot = cotangent.reshape(count * frames_two, width)
    cot, weight = ready(count, cot, table, conv_two)
    place = lax.axis_index("dp").astype(jnp.int32).reshape(1)
    partial = local_pass(record, shares, place, got, cot, weight, conv_two, table)
    return sum_all(sizes, *partial)


def solution(mesh):
    sizes = {axis: mesh.shape[axis] for axis in ("dp", "blk")}
    both = ("dp", "blk")
    return jax.shard_map(
        functools.partial(per_device, sizes),
        mesh=mesh,
        in_specs=(P(both, None), P(both), P(both, None), P(both, None, None)) + (P(),) * 8,
        out_specs=(P("dp", None), P()),
        check_vma=False,
    )
```

```python
import functools
import math

import jax
import jax.numpy as jnp
from jax import lax
from jax.experimental import pallas as pl
from jax.experimental.pallas import tpu as pltpu
from jax.sharding import PartitionSpec as P

NB = 4
TAPS = 10
STRIDE = 5
ROWS = 16
F32 = jnp.float32
BF16 = jnp.bfloat16


def gelu_parts(act):
    cdf = 0.5 + 0.5 * lax.erf(act * 0.7071067811865476)
    return cdf, 0.3989422804014327 * jnp.exp(-0.5 * (act * act))


def pack_kernel(packing, bins, wave_ref, out_ref, wide):
    count, record = wave_ref.shape
    width = wide.shape[1]
    wide[...] = jnp.zeros_like(wide)
    wide[:, :record] = wave_ref[...].astype(F32)
    lane = lax.broadcasted_iota(jnp.int32, (1, width), 1)
    for slot in range(count):
        own = packing[0, slot]
        row = wide[pl.ds(own, 1), :]
        out_ref[slot] = jnp.where(lane == record, bins[own].astype(F32), row)


def pack(packing, length_bin, waveform):
    count, record = waveform.shape
    width = -(-(record + 1) // 128) * 128
    return pl.pallas_call(
        pack_kernel,
        out_shape=jax.ShapeDtypeStruct((count, 1, width), F32),
        in_specs=[
            pl.BlockSpec(memory_space=pltpu.SMEM),
            pl.BlockSpec(memory_space=pltpu.SMEM),
            pl.BlockSpec(memory_space=pltpu.VMEM),
        ],
        out_specs=pl.BlockSpec(memory_space=pltpu.VMEM),
        scratch_shapes=[pltpu.VMEM((count, width), F32)],
    )(packing, length_bin, waveform)


def ready_kernel(count, cot_ref, table_ref, conv_two_ref, moved_ref, weight_ref, weight):
    rows_two, width = cot_ref.shape
    frames_two = rows_two // count
    inv = 1.0 / width
    row = lax.broadcasted_iota(jnp.int32, (rows_two, 1), 0)
    origin = (row % count) * frames_two + row // count
    mover = (lax.broadcasted_iota(jnp.int32, (rows_two, rows_two), 1) == origin).astype(BF16)
    moved_ref[...] = jnp.dot(mover, cot_ref[...], preferred_element_type=F32).astype(BF16)
    weight[...] = jnp.zeros_like(weight)
    kernel = table_ref[:TAPS, :]
    kernel = kernel - jnp.sum(kernel, axis=1, keepdims=True) * inv
    bias = table_ref[TAPS : TAPS + 1, :]
    bias = bias - jnp.sum(bias, axis=1, keepdims=True) * inv
    for part in range(3):
        piece = kernel.astype(BF16).astype(F32)
        weight[part * ROWS : part * ROWS + TAPS, :] = piece
        kernel = kernel - piece
        piece = bias.astype(BF16).astype(F32)
        weight[3 * ROWS + part : 3 * ROWS + part + 1, :] = piece
        bias = bias - piece
    weight_ref[...] = weight[...].astype(BF16)


def ready(count, cot, table, conv_two):
    rows_two, width = cot.shape
    vmem = pl.BlockSpec(memory_space=pltpu.VMEM)
    return pl.pallas_call(
        functools.partial(ready_kernel, count),
        out_shape=(
            jax.ShapeDtypeStruct(cot.shape, BF16),
            jax.ShapeDtypeStruct((128, width), BF16),
        ),
        in_specs=[vmem, vmem, vmem],
        out_specs=(vmem, vmem),
        scratch_shapes=[pltpu.VMEM((128, width), F32)],
        cost_estimate=pl.CostEstimate(
            flops=2 * rows_two * rows_two * width,
            bytes_accessed=4 * cot.size,
            transcendentals=0,
        ),
        compiler_params=pltpu.CompilerParams(vmem_limit_bytes=16 * 1024 * 1024),
    )(cot, table, conv_two)


def together(steps):
    return max(n for n in range(1, 66) if steps % n == 0)


def bit_order(shares):
    bits = shares.bit_length() - 1
    return [0, 3, 1, 2, *range(4, bits)]


def local_kernel(
    record,
    shares,
    place_ref,
    got_ref,
    cot_ref,
    weight_ref,
    conv_two_ref,
    table_ref,
    send_far,
    send_near,
    keep_far,
    keep_near,
    small_ref,
    taps,
    limits,
    cent_one,
    norm_one,
    slope_one,
    rstd_one,
    hidden,
    norm_two,
    dz_two,
    dz_one,
    grad,
):
    count = got_ref.shape[0]
    rows_two, width = cot_ref.shape
    frames_two = rows_two // count
    frames_one = 2 * frames_two + 1
    rows_even = rows_two + count
    rows_one = frames_one * count
    inv = 1.0 / width

    wave = jnp.concatenate([got_ref[slot] for slot in range(count)], axis=0)
    lane_in = lax.broadcasted_iota(jnp.int32, wave.shape, 1)
    bins = jnp.sum(jnp.where(lane_in == record, wave, 0.0), axis=1, keepdims=True)
    limit = bins.astype(jnp.int32) * frames_two // NB
    limits[...] = jnp.broadcast_to(limit, (count, 128))
    wave = jnp.concatenate([wave, jnp.zeros((count, 128), F32)], axis=1)

    for place, frame in enumerate(
        list(range(0, frames_one, 2)) + list(range(1, frames_one, 2))
    ):
        taps[count * place : count * (place + 1), :] = wave[
            :, STRIDE * frame : STRIDE * frame + 128
        ].astype(BF16)
    src = lax.broadcasted_iota(jnp.int32, (128, 128), 0)
    dst = lax.broadcasted_iota(jnp.int32, (128, 128), 1)
    thrice = ((src < TAPS) & (dst < 3 * ROWS) & (dst % ROWS == src)).astype(BF16)
    lane = lax.broadcasted_iota(jnp.int32, (1, 128), 1)
    ones = ((lane >= 3 * ROWS) & (lane < 3 * ROWS + 3)).astype(F32)
    taps[...] = (jnp.dot(taps[...], thrice, preferred_element_type=F32) + ones).astype(BF16)

    cent_one[...] = jnp.dot(taps[...], weight_ref[...], preferred_element_type=F32)
    gain = table_ref[TAPS + 1 : TAPS + 2, :]
    shift = table_ref[TAPS + 2 : TAPS + 3, :]
    steps_one = rows_one // ROWS
    steps_two = rows_two // ROWS

    def forward(step, _):
        at = pl.ds(pl.multiple_of(step * ROWS, ROWS), ROWS)
        cent = cent_one[at, :]
        var = jnp.sum(cent * cent, axis=1, keepdims=True) * inv
        rstd = lax.rsqrt(var + 1e-05)
        normed = cent * rstd
        act = normed * gain + shift
        cdf, pdf = gelu_parts(act)
        norm_one[at, :] = normed
        rstd_one[at, :] = jnp.broadcast_to(rstd, (ROWS, 128))
        slope_one[at, :] = cdf + act * pdf
        hidden[at, :] = (act * cdf).astype(BF16)
        return 0

    lax.fori_loop(0, steps_one, forward, 0, unroll=together(steps_one))

    windows = (
        slice(0, rows_two),
        slice(rows_even, rows_even + rows_two),
        slice(count, rows_even),
    )
    total = None
    for tap, rows in enumerate(windows):
        term = jnp.dot(
            hidden[rows, :],
            conv_two_ref[tap * width : (tap + 1) * width, :],
            preferred_element_type=F32,
        )
        total = term if total is None else total + term
    norm_two[...] = total

    bias_two = table_ref[TAPS + 3 : TAPS + 4, :]
    gain_b = table_ref[TAPS + 4 : TAPS + 5, :]
    shift_b = table_ref[TAPS + 5 : TAPS + 6, :]
    dz_two[:count, :] = jnp.zeros((count, width), BF16)
    dz_two[count + rows_two :, :] = jnp.zeros((count, width), BF16)

    def eighth(x):
        return x[:8] + x[8:]

    def middle(step, sums):
        start = pl.multiple_of(step * ROWS, ROWS)
        at = pl.ds(start, ROWS)
        first = pl.multiple_of(lax.rem(start, count), ROWS)
        valid = limits[pl.ds(first, ROWS), :1] > lax.div(start, count)
        z = norm_two[at, :] + bias_two
        cent = z - jnp.sum(z, axis=1, keepdims=True) * inv
        var = jnp.sum(cent * cent, axis=1, keepdims=True) * inv
        rstd = lax.rsqrt(var + 1e-05)
        normed = cent * rstd
        act = normed * gain_b + shift_b
        cdf, pdf = gelu_parts(act)
        dact = jnp.where(valid, cot_ref[at, :].astype(F32) * (cdf + act * pdf), 0.0)
        dnorm = dact * gain_b
        mean_a = jnp.sum(dnorm, axis=1, keepdims=True) * inv
        mean_b = jnp.sum(dnorm * normed, axis=1, keepdims=True) * inv
        dz = rstd * (dnorm - mean_a - normed * mean_b)
        dz_two[pl.ds(pl.multiple_of(start + count, ROWS), ROWS), :] = dz.astype(BF16)
        return (
            sums[0] + eighth(dz),
            sums[1] + eighth(dact * normed),
            sums[2] + eighth(dact),
        )

    zero = jnp.zeros((8, width), F32)
    sums_two = lax.fori_loop(
        0, steps_two, middle, (zero, zero, zero), unroll=together(steps_two)
    )

    dz_own = dz_two[count : count + rows_two, :]
    for tap, rows in enumerate(windows):
        grad[tap * width : (tap + 1) * width, :] = lax.dot_general(
            hidden[rows, :], dz_own, (((0,), (0,)), ((), ())), preferred_element_type=F32
        )
    share = grad.shape[0] // shares
    me = place_ref[0]
    order = bit_order(shares)
    parts = (keep_near, keep_far, send_near, send_far)
    quarter = shares // 4
    for spot in range(shares):
        flip = sum(1 << bit for i, bit in enumerate(reversed(order)) if spot >> i & 1)
        block = grad[pl.ds(pl.multiple_of((me ^ flip) * share, 8), share), :]
        part = parts[spot // quarter]
        at = spot % quarter * share
        part[at : at + share, :] = block.astype(part.dtype)

    turn = (((1,), (1,)), ((), ()))
    dz_one[rows_even:, :] = lax.dot_general(
        dz_own, conv_two_ref[width : 2 * width, :], turn, preferred_element_type=F32
    )
    dz_one[:rows_even, :] = lax.dot_general(
        dz_two[count:, :], conv_two_ref[:width, :], turn, preferred_element_type=F32
    ) + lax.dot_general(
        dz_two[:rows_even, :], conv_two_ref[2 * width :, :], turn, preferred_element_type=F32
    )

    def backward(step, sums):
        at = pl.ds(pl.multiple_of(step * ROWS, ROWS), ROWS)
        normed = norm_one[at, :]
        dact = dz_one[at, :] * slope_one[at, :]
        dnorm = dact * gain
        mean_a = jnp.sum(dnorm, axis=1, keepdims=True) * inv
        mean_b = jnp.sum(dnorm * normed, axis=1, keepdims=True) * inv
        dz = rstd_one[at, :1] * (dnorm - mean_a - normed * mean_b)
        hidden[at, :] = dz.astype(BF16)
        return (
            sums[0] + eighth(dz),
            sums[1] + eighth(dact * normed),
            sums[2] + eighth(dact),
        )

    sums_one = lax.fori_loop(
        0, steps_one, backward, (zero, zero, zero), unroll=together(steps_one)
    )
    first = lax.dot_general(
        taps[...], hidden[...], (((0,), (0,)), ((), ())), preferred_element_type=F32
    )
    small_ref[:TAPS, :] = first[:TAPS, :]
    for spot, sums in enumerate(sums_one + sums_two):
        small_ref[TAPS + spot : TAPS + spot + 1, :] = jnp.sum(sums, axis=0, keepdims=True)


def local_pass(record, shares, place, got, cot, weight, conv_two, table):
    count = got.shape[0]
    rows_two, width = cot.shape
    rows_one = 2 * rows_two + count
    quarter = 3 * width // 4
    vmem = pl.BlockSpec(memory_space=pltpu.VMEM)
    return pl.pallas_call(
        functools.partial(local_kernel, record, shares),
        out_shape=(
            jax.ShapeDtypeStruct((quarter, width), BF16),
            jax.ShapeDtypeStruct((quarter, width), BF16),
            jax.ShapeDtypeStruct((quarter, width), F32),
            jax.ShapeDtypeStruct((quarter, width), F32),
            jax.ShapeDtypeStruct((ROWS, width), F32),
        ),
        in_specs=[pl.BlockSpec(memory_space=pltpu.SMEM)] + [vmem] * 5,
        out_specs=(vmem,) * 5,
        scratch_shapes=[
            pltpu.VMEM((rows_one, 128), BF16),
            pltpu.VMEM((count, 128), jnp.int32),
            pltpu.VMEM((rows_one, width), F32),
            pltpu.VMEM((rows_one, width), F32),
            pltpu.VMEM((rows_one, width), F32),
            pltpu.VMEM((rows_one, 128), F32),
            pltpu.VMEM((rows_one, width), BF16),
            pltpu.VMEM((rows_two, width), F32),
            pltpu.VMEM((rows_two + 2 * count, width), BF16),
            pltpu.VMEM((rows_one, width), F32),
            pltpu.VMEM((3 * width, width), F32),
        ],
        cost_estimate=pl.CostEstimate(
            flops=2 * 9 * rows_two * width * width,
            bytes_accessed=8 * rows_one * width,
            transcendentals=3 * rows_one * width,
        ),
        compiler_params=pltpu.CompilerParams(vmem_limit_bytes=36 * 1024 * 1024),
    )(place, got, cot, weight, conv_two, table)


def tree(terms):
    while len(terms) > 1:
        terms = [terms[i] + terms[i + 1] for i in range(0, len(terms), 2)]
    return terms[0]


def exchange(sizes, stage, message):
    far = {axis: 0 for axis in sizes}
    for axis, bit in stage:
        far[axis] ^= 1 << bit
    axes = tuple(axis for axis in sizes if far[axis])
    pairs = [(0, 0)]
    for axis in axes:
        n = sizes[axis]
        pairs = [(a * n + i, b * n + (i ^ far[axis])) for a, b in pairs for i in range(n)]
    return lax.ppermute(message, axes if len(axes) > 1 else axes[0], pairs)


def rounded(x):
    return lax.reduce_precision(x, exponent_bits=8, mantissa_bits=7)


def message(rows, small):
    return jnp.concatenate([rows.astype(BF16), small.astype(BF16)], axis=0)


def contents(got):
    rows = got.shape[0] - ROWS
    return got[:rows].astype(F32), got[rows:].astype(F32)


def near_kernel(own_ref, *refs):
    terms = [own_ref[...]] + [ref[...].astype(F32) for ref in refs[:-2]]
    total = tree(terms)
    cut = refs[-2].shape[0]
    refs[-2][...] = total[:cut]
    refs[-1][...] = total[cut:]


def near_sum(cut, own, *got):
    vmem = pl.BlockSpec(memory_space=pltpu.VMEM)
    return pl.pallas_call(
        near_kernel,
        out_shape=(
            jax.ShapeDtypeStruct((cut, own.shape[1]), F32),
            jax.ShapeDtypeStruct((own.shape[0] - cut, own.shape[1]), F32),
        ),
        in_specs=[vmem] * (1 + len(got)),
        out_specs=(vmem, vmem),
        cost_estimate=pl.CostEstimate(
            flops=4 * own.size, bytes_accessed=140 * own.size, transcendentals=0
        ),
        compiler_params=pltpu.CompilerParams(vmem_limit_bytes=8 * 1024 * 1024),
    )(own, *got)


def finish_kernel(own_first, own_second, got_first, got_second, rows_ref, small_ref):
    cut = own_first.shape[0]
    own, small = contents(own_second[...])
    got, more = contents(got_second[...])
    rows_ref[:cut, :] = own_first[...].astype(F32) + got_first[...].astype(F32)
    rows_ref[cut:, :] = own + got
    small_ref[...] = small + more


def finish(*parts):
    rows, width = parts[0].shape[0] + parts[1].shape[0] - ROWS, parts[0].shape[1]
    vmem = pl.BlockSpec(memory_space=pltpu.VMEM)
    return pl.pallas_call(
        finish_kernel,
        out_shape=(
            jax.ShapeDtypeStruct((rows, width), F32),
            jax.ShapeDtypeStruct((ROWS, width), F32),
        ),
        in_specs=[vmem] * 4,
        out_specs=(pl.BlockSpec(), pl.BlockSpec()),
        compiler_params=pltpu.CompilerParams(vmem_limit_bytes=8 * 1024 * 1024),
    )(*parts)


def sum_all(sizes, send_far, send_near, keep_far, keep_near, small):
    order = [("dp", bit) for bit in bit_order(sizes["dp"])]
    core, onward, pair, left = order[0], order[1], order[2:4], order[4:]
    small = rounded(small + exchange(sizes, [core], small))
    far = keep_far + exchange(sizes, [core], send_far).astype(F32)
    near = keep_near + exchange(sizes, [core], send_near).astype(F32)
    rows = far.shape[0] // 4
    near, far = ([part[i * rows : (i + 1) * rows] for i in range(4)] for part in (near, far))
    fars, smalls, nears = [far[0]], [small], []
    chosen = [[bit for i, bit in enumerate(pair) if code >> (1 - i) & 1] for code in range(4)]
    for code in (1, 2, 3):
        got, more = contents(exchange(sizes, chosen[code], message(far[code], small)))
        fars.append(got)
        smalls.append(more)
    small = rounded(tree(smalls))
    own = message(tree(fars), small)
    for code in (1, 2, 3):
        nears.append(exchange(sizes, chosen[code], near[code].astype(BF16)))
    cut = own.shape[0] // 2 // ROWS * ROWS
    first, second = (exchange(sizes, [onward], part) for part in (own[:cut], own[cut:]))
    base = near_sum(cut, near[0], *nears)
    first = base[0] + first.astype(F32)
    second, more = contents(second)
    second, small = base[1] + second, small + more
    for bit in left:
        total = jnp.concatenate([first, second], axis=0)
        half = total.shape[0] // 2
        small = rounded(small)
        own = message(total[half:], small)
        got, more = contents(exchange(sizes, [bit], own))
        total, small = total[:half] + got, small + more
        cut = own.shape[0] // 2 // ROWS * ROWS
        first, second = total[:cut], total[cut:]
    bits = sizes["blk"].bit_length() - 1
    for bit in range(bits):
        first, second, small = rounded(first), rounded(second), rounded(small)
        own = first.astype(BF16), message(second, small)
        got = [exchange(sizes, [("blk", bit)], part) for part in own]
        if bit == bits - 1:
            return finish(*own, *got)
        more, extra = contents(got[1])
        first, second, small = first + got[0].astype(F32), second + more, small + extra
    return jnp.concatenate([first, second], axis=0), small


def per_device(
    sizes,
    waveform,
    length_bin,
    packing,
    cotangent,
    conv_one,
    bias_one,
    gain_one,
    shift_one,
    conv_two,
    bias_two,
    gain_two,
    shift_two,
):
    record = waveform.shape[1]
    count, frames_two, width = cotangent.shape
    shares = sizes["dp"]
    packed = pack(packing, length_bin, waveform)
    got = lax.all_to_all(packed, "dp", split_axis=0, concat_axis=0, tiled=True)
    vectors = (bias_one, gain_one, shift_one, bias_two, gain_two, shift_two)
    table = jnp.concatenate([conv_one.astype(F32), jnp.stack(vectors)], axis=0)
    cot = cotangent.reshape(count * frames_two, width)
    cot, weight = ready(count, cot, table, conv_two)
    place = lax.axis_index("dp").astype(jnp.int32).reshape(1)
    partial = local_pass(record, shares, place, got, cot, weight, conv_two, table)
    return sum_all(sizes, *partial)


def solution(mesh):
    sizes = {axis: mesh.shape[axis] for axis in ("dp", "blk")}
    both = ("dp", "blk")
    return jax.shard_map(
        functools.partial(per_device, sizes),
        mesh=mesh,
        in_specs=(P(both, None), P(both), P(both, None), P(both, None, None)) + (P(),) * 8,
        out_specs=(P("dp", None), P()),
        check_vma=False,
    )
```
